32 devices in a mesh: dp: 8 (over z, y), tensor: 4 (over x, core).
Axes of the slice: x: 2, y: 2, z: 4, core: 2. Of those that a mesh axis runs over, the one named last changes fastest.
Arguments:
- hidden_in: bfloat16 [8192, 1536], P(('dp', 'tensor')), may hold values from -6 to 6
- segments: int32 [8192], P('dp'), may hold values from 0 to 4, as said below
- attn_gain: bfloat16 [1536], P('dp'), may hold values from 0.25 to 1.75
- w_query: bfloat16 [1536, 1536], P('dp', 'tensor'), may hold values from -0.21875 to 0.21875
- w_key: bfloat16 [1536, 768], P('dp', 'tensor'), may hold values from -0.21875 to 0.21875
- w_value: bfloat16 [1536, 768], P('dp', 'tensor'), may hold values from -0.15625 to 0.15625
- w_out: bfloat16 [1536, 1536], P('tensor', 'dp'), may hold values from -0.4375 to 0.4375
- mlp_gain: bfloat16 [1536], P('dp'), may hold values from 0.25 to 1.75
- w_gate: bfloat16 [1536, 4096], P('dp', 'tensor'), may hold values from -0.15625 to 0.15625
- w_up: bfloat16 [1536, 4096], P('dp', 'tensor'), may hold values from -0.15625 to 0.15625
- w_down: bfloat16 [4096, 1536], P('tensor', 'dp'), may hold values from -0.09375 to 0.09375
- cotangent: bfloat16 [8192, 1536], P(('dp', 'tensor')), may hold values from -6 to 6
Outputs:
- mixed: bfloat16 [8192, 1536], P(('dp', 'tensor'))
- hidden_grad: bfloat16 [8192, 1536], P(('dp', 'tensor'))
- attn_gain_grad: float32 [1536], P('dp')
- w_query_grad: float32 [1536, 1536], P('dp', 'tensor')
- w_key_grad: float32 [1536, 768], P('dp', 'tensor')
- w_value_grad: float32 [1536, 768], P('dp', 'tensor')
- w_out_grad: float32 [1536, 1536], P('tensor', 'dp')
- mlp_gain_grad: float32 [1536], P('dp')
- w_gate_grad: float32 [1536, 4096], P('dp', 'tensor')
- w_up_grad: float32 [1536, 4096], P('dp', 'tensor')
- w_down_grad: float32 [4096, 1536], P('tensor', 'dp')
The draws below stay inside these ranges and needn't reach their ends.
Inputs may be any that keep to these rules, and one draw needn't show every extreme that they name: `segments`: along each sequence of 1024 tokens the segment numbers start at 0, never fall, and rise by one where a new document begins; every sequence holds exactly five documents.
All inputs are finite; a program needn't handle non-finite values.
Results may differ from the reference program's by a relative error of at most 0.02.
Values may be sent and summed in bfloat16 or wider, within the bound.
No kernel may reach another device: no remote copies, remote signals or barrier semaphores. Data moves between devices by JAX's collectives and lax.ppermute only.
A program may use at most 128 MiB of HBM per device.

```python
import math
import jax
import jax.numpy as jnp
from jax import lax

D = 1536
H = 16
KV = 8
HD = 96
FF = 4096
SEQ = 1024
GROUPS = 8
TOKENS = 8192


def draw_segments(key, part):
    key = jax.random.fold_in(key, 7)
    key_open, key_close, key_early, key_late = jax.random.split(key, 4)
    opening = jax.random.randint(key_open, (GROUPS, 1), SEQ // 8, SEQ // 4)
    closing = jax.random.randint(key_close, (GROUPS, 1), 3 * SEQ // 4 + 1, 7 * SEQ // 8 + 1)
    early = jax.random.randint(key_early, (GROUPS, 1), 1, opening)
    late = jax.random.randint(key_late, (GROUPS, 1), closing + 1, SEQ)
    places = jnp.arange(SEQ, dtype=jnp.int32)[None, :]
    begins = (places == early).astype(jnp.int32) + (places == opening).astype(jnp.int32)
    begins = begins + (places == closing).astype(jnp.int32) + (places == late).astype(jnp.int32)
    return jnp.cumsum(begins, axis=1).astype(jnp.int32).reshape(GROUPS * SEQ)


def spiked(values, stream_key, source, target, blocks, factor):
    owner, partner = [(jnp.arange(values.shape[axis_at]) // (values.shape[axis_at] // blocks)).reshape([-1 if axis == axis_at else 1 for axis in range(values.ndim)]) for axis_at in (source, target)]
    chosen = jax.random.permutation(stream_key, blocks)[partner]
    strong = (owner == chosen) | (owner == (partner + blocks // 2) % blocks)
    return jnp.where(strong, factor * values, values)


def shard_levels(stream_key, dims, pieces, least, high):
    loudness = 1.0
    for axis_at, shards_of in pieces:
        steps = jax.random.uniform(jax.random.fold_in(jax.random.fold_in(stream_key, 6), axis_at), (shards_of,), jnp.float32, least / len(pieces), high / len(pieces))
        loudness = loudness * jnp.repeat(jnp.exp(steps), dims[axis_at] // shards_of).reshape((-1,) + (1,) * (len(dims) - 1 - axis_at))
    return loudness


def scatter_about(rng, dims, spread, reach, cuts=(), held_as=jnp.bfloat16):
    entries = spread * jax.random.normal(rng, dims, jnp.float32)
    if cuts:
        entries = entries * shard_levels(rng, dims, cuts, -0.22, 0.18)
    return jnp.clip(entries, -reach, reach).astype(held_as)


def gaussian_with(rng, dims, scale, reach, pieces, heavy, held_as=jnp.bfloat16):
    array = scale * jax.random.normal(rng, dims, jnp.float32)
    if pieces:
        array = array * shard_levels(rng, dims, pieces, -0.22, 0.18)
    return jnp.clip(spiked(array, jax.random.fold_in(rng, 3), *heavy), -reach, reach).astype(held_as)


def setup_inputs(seed: int = 0) -> dict:
    key_of = jax.random.split(jax.random.key(seed), 13)
    return {
        "hidden_in": scatter_about(key_of[0], (TOKENS, D), 1.0, 6.0, ((0, 32),)),
        "segments": draw_segments(jax.random.fold_in(key_of[12], 71), 0),
        "attn_gain": jnp.clip(1.0 + 0.15 * jax.random.normal(key_of[2], (D,), jnp.float32), 0.25, 1.75).astype(jnp.bfloat16),
        "w_query": scatter_about(key_of[3], (D, H * HD), (D // 2) ** -0.5, 0.21875, ((0, 8), (1, 4))),
        "w_key": scatter_about(key_of[4], (D, KV * HD), (D // 2) ** -0.5, 0.21875, ((0, 8), (1, 4))),
        "w_value": scatter_about(key_of[5], (D, KV * HD), D ** -0.5, 0.15625, ((0, 8), (1, 4))),
        "w_out": scatter_about(key_of[6], (H * HD, D), (H * HD // 8) ** -0.5, 0.4375, ((0, 4), (1, 8))),
        "mlp_gain": jnp.clip(1.0 + 0.15 * jax.random.normal(key_of[7], (D,), jnp.float32), 0.25, 1.75).astype(jnp.bfloat16),
        "w_gate": scatter_about(key_of[8], (D, FF), D ** -0.5, 0.15625, ((0, 8), (1, 4))),
        "w_up": scatter_about(key_of[9], (D, FF), D ** -0.5, 0.15625, ((0, 8), (1, 4))),
        "w_down": scatter_about(key_of[10], (FF, D), FF ** -0.5, 0.09375, ((0, 4), (1, 8))),
        "cotangent": gaussian_with(key_of[11], (TOKENS, D), 1.0, 6.0, ((0, 32),), (0, 1, 32, 2.75)),
    }


EPS = 1e-05
NEG = -1e+30
THETA = 100000.0
HIGH = lax.Precision.HIGHEST

@jax.custom_vjp
def low(v):
    return lax.optimization_barrier(v.astype(jnp.bfloat16)).astype(jnp.float32)

@jax.custom_vjp
def low_back(v):
    return v

def low_keep(v):
    return (low(v), None)

def low_pass(kept, grad):
    return (grad,)

def back_keep(v):
    return (v, None)

def back_low(kept, grad):
    return (low(grad),)
low.defvjp(low_keep, low_pass)
low_back.defvjp(back_keep, back_low)

def product(left_side, right_side):
    return jnp.dot(left_side, right_side, preferred_element_type=jnp.float32, precision=HIGH)

def rms_norm(values, gain):
    return values * lax.rsqrt(lax.optimization_barrier(jnp.mean(values * values, axis=-1, keepdims=True)) + EPS) * gain

def rope_tables(segment):
    places = jnp.arange(segment.shape[0], dtype=jnp.int32)
    previous = jnp.concatenate([segment[:1] - 1, segment[:-1]]).astype(jnp.int32)
    opening = jnp.where(segment != previous, places, 0).astype(jnp.int32)
    position = (places - lax.cummax(opening, axis=0)).astype(jnp.float32)
    half_dim = HD // 2
    inverse = jnp.exp(-(2.0 * jnp.arange(half_dim, dtype=jnp.float32) / HD) * math.log(THETA))
    angle = position[:, None] * inverse[None, :]
    return (jnp.cos(angle), jnp.sin(angle))

def rotate(values, cosine_table, sine_table):
    half_dim = values.shape[-1] // 2
    first_half = values[..., :half_dim]
    second_half = values[..., half_dim:]
    cosine = cosine_table[:, None, :]
    sine = sine_table[:, None, :]
    return jnp.concatenate([first_half * cosine - second_half * sine, second_half * cosine + first_half * sine], axis=-1)

def layer(hidden, segment, attn_gain, w_query, w_key, w_value, w_out, mlp_gain, w_gate, w_up, w_down):
    length = hidden.shape[0]
    cosine_table, sine_table = rope_tables(segment)
    normed = low(rms_norm(hidden, attn_gain))
    queries = low_back(product(normed, w_query)).reshape(length, H, HD)
    queries = low(rotate(queries, cosine_table, sine_table)).reshape(length, KV, H // KV, HD)
    keys_rot = low_back(product(normed, w_key)).reshape(length, KV, HD)
    keys_rot = low(rotate(keys_rot, cosine_table, sine_table))
    values = low(low_back(product(normed, w_value))).reshape(length, KV, HD)
    scores = jnp.einsum('qgrd,kgd->grqk', queries, keys_rot, precision=HIGH) * HD ** (-0.5)
    places = jnp.arange(length, dtype=jnp.int32)
    allowed = (segment[:, None] == segment[None, :]) & (places[None, :] <= places[:, None])
    scores = low_back(jnp.where(allowed, scores, NEG))
    log_total = jax.nn.logsumexp(scores, axis=-1, keepdims=True)
    probs = low(jnp.exp(scores - log_total))
    heads_out = jnp.einsum('grqk,kgd->qgrd', probs, values, precision=HIGH).reshape(length, H * HD)
    heads_out = low(low_back(heads_out))
    resid = hidden + low_back(product(heads_out, w_out))
    normed_two = low(rms_norm(resid, mlp_gain))
    gate_pre = low_back(product(normed_two, w_gate))
    upward = low_back(product(normed_two, w_up))
    activated = low(jax.nn.silu(gate_pre) * upward)
    return resid + low_back(product(activated, w_down))

def reference(hidden_in, segments, attn_gain, w_query, w_key, w_value, w_out, mlp_gain, w_gate, w_up, w_down, cotangent):
    params = tuple((weight.astype(jnp.float32) for weight in (attn_gain, w_query, w_key, w_value, w_out, mlp_gain, w_gate, w_up, w_down)))
    hidden = hidden_in.astype(jnp.float32).reshape(GROUPS, SEQ, D)
    pulled_all = cotangent.astype(jnp.float32).reshape(GROUPS, SEQ, D)
    segment_all = segments.reshape(GROUPS, SEQ)

    def one_group(totals, group_item):
        group_rows, segment, pulled = group_item

        def closed(rows_in, *weights):
            return layer(rows_in, segment, *weights)
        output, pullback = jax.vjp(closed, group_rows, *params)
        gradients = pullback(pulled)
        totals = tuple((total + grad_part for total, grad_part in zip(totals, gradients[1:])))
        return (totals, (output, gradients[0]))
    start_sums = tuple((jnp.zeros_like(weight) for weight in params))
    totals, (outputs, input_grads) = lax.scan(one_group, start_sums, (hidden, segment_all, pulled_all))
    return (outputs.reshape(TOKENS, D).astype(jnp.bfloat16), input_grads.reshape(TOKENS, D).astype(jnp.bfloat16), totals[0], totals[1], totals[2], totals[3], totals[4], totals[5], totals[6], totals[7], totals[8])
```

```python
import math

import jax
import jax.numpy as jnp
from jax import lax
from jax.sharding import PartitionSpec as P

HD = 96
EPS = 1e-05
NEG = -1e30
THETA = 100000.0
BF = jnp.bfloat16
F32 = jnp.float32

CORE_PAIRS = [(0, 1), (1, 0), (2, 3), (3, 2)]
X_PAIRS = [(0, 2), (2, 0), (1, 3), (3, 1)]


def matmul(left_side, right_side):
    return jnp.dot(left_side, right_side, preferred_element_type=F32)


def left_t(left_side, right_side):
    return lax.dot_general(
        left_side, right_side, (((0,), (0,)), ((), ())), preferred_element_type=F32
    )


def right_t(left_side, right_side):
    return lax.dot_general(
        left_side, right_side, (((1,), (1,)), ((), ())), preferred_element_type=F32
    )


class Ring:
    def __init__(self, count):
        self.count = count
        self.half = count // 2
        order = [2 * k if k < self.half else 2 * (count - 1 - k) + 1 for k in range(count)]
        self.right = [(order[k], order[(k + 1) % count]) for k in range(count)]
        self.left = [(b, a) for a, b in self.right]
        me = lax.axis_index("dp")
        self.place = jnp.where(me % 2 == 0, me // 2, count - 1 - me // 2)

    def index(self, offset):
        place = (self.place + offset + self.count) % self.count
        return jnp.where(place < self.half, 2 * place, 2 * (self.count - 1 - place) + 1)

    def go_right(self, value):
        return lax.ppermute(value, "dp", self.right)

    def go_left(self, value):
        return lax.ppermute(value, "dp", self.left)


def cut_of(columns):
    return max(128, (columns // 2 + 127) // 128 * 128)


def gather_pieces(ring, shard):
    cut = cut_of(shard.shape[1])
    pieces = [(0, 0, shard)]
    from_left = from_right = shard
    for step in range(1, ring.half):
        from_left = ring.go_right(from_left)
        from_right = ring.go_left(from_right)
        pieces += [(-step, 0, from_left), (step, 0, from_right)]
    pieces.append((-ring.half, 0, ring.go_right(from_left[:, :cut])))
    pieces.append((ring.half, cut, ring.go_left(from_right[:, cut:])))
    return pieces


def assemble(ring, pieces):
    rows, columns = pieces[0][2].shape
    whole = jnp.zeros((ring.count * rows, columns), pieces[0][2].dtype)
    for offset, column, piece in pieces:
        whole = lax.dynamic_update_slice(whole, piece, (ring.index(offset) * rows, column))
    return whole


def scatter_sum(ring, whole):
    rows, columns = whole.shape[0] // ring.count, whole.shape[1]
    cut = cut_of(columns)

    def chunk(offset):
        return lax.dynamic_slice(whole, (ring.index(offset) * rows, 0), (rows, columns))

    far = chunk(ring.half)
    from_left = ring.go_right(far[:, :cut])
    from_right = ring.go_left(far[:, cut:])
    for step in range(ring.half - 1, 0, -1):
        to_right, to_left = chunk(step).astype(F32), chunk(-step).astype(F32)
        if step == ring.half - 1:
            to_right = jnp.concatenate(
                [to_right[:, :cut] + from_left.astype(F32), to_right[:, cut:]], axis=1
            )
            to_left = jnp.concatenate(
                [to_left[:, :cut], to_left[:, cut:] + from_right.astype(F32)], axis=1
            )
        else:
            to_right = to_right + from_left.astype(F32)
            to_left = to_left + from_right.astype(F32)
        from_left = ring.go_right(to_right.astype(BF))
        from_right = ring.go_left(to_left.astype(BF))
    return chunk(0).astype(F32) + from_left.astype(F32) + from_right.astype(F32)


def swap_core(value):
    return lax.ppermute(value, "tensor", CORE_PAIRS)


def swap_x(value):
    return lax.ppermute(value, "tensor", X_PAIRS)


def pick(pair, which):
    return lax.dynamic_index_in_dim(pair, which, 0, keepdims=False)


def in_order(own, other, which):
    return jnp.where(which == 0, jnp.stack([own, other]), jnp.stack([other, own]))


def gather_tokens(rows, core, chip):
    mine = in_order(rows, swap_core(rows), core)
    across = swap_x(rows)
    theirs = in_order(across, swap_core(across), core)
    return in_order(mine, theirs, chip)


def core_sum(partial, core):
    received = swap_core(pick(partial, 1 - core).astype(BF))
    return pick(partial, core).astype(F32) + received.astype(F32)


def sum_both(partial, core):
    chip_sum = core_sum(partial, core).astype(BF)
    return chip_sum.astype(F32) + swap_x(chip_sum).astype(F32)


def sum_own(partial, core, chip):
    away = core_sum(pick(partial, 1 - chip), core).astype(BF)
    received = swap_x(away)
    return core_sum(pick(partial, chip), core) + received.astype(F32)


def rope_tables(segment):
    places = jnp.arange(segment.shape[0], dtype=jnp.int32)
    previous = jnp.concatenate([segment[:1] - 1, segment[:-1]])
    opening = jnp.where(segment != previous, places, 0)
    position = (places - lax.cummax(opening, axis=0)).astype(F32)
    half_dim = HD // 2
    inverse = jnp.exp(-(2.0 * jnp.arange(half_dim, dtype=F32) / HD) * math.log(THETA))
    angle = position[:, None] * inverse[None, :]
    return (jnp.cos(angle), jnp.sin(angle))


def rotate(values, cosine_table, sine_table):
    half_dim = values.shape[-1] // 2
    first_half = values[..., :half_dim]
    second_half = values[..., half_dim:]
    cosine = cosine_table[:, None, :]
    sine = sine_table[:, None, :]
    return jnp.concatenate(
        [first_half * cosine - second_half * sine, second_half * cosine + first_half * sine],
        axis=-1,
    )


def unrotate(values, cosine_table, sine_table):
    return rotate(values, cosine_table, -sine_table)


def inverse_rms(values):
    return lax.rsqrt(jnp.mean(values * values, axis=-1, keepdims=True) + EPS)


def norm_back(scaled, values, inverse):
    return inverse * scaled - values * inverse * inverse * inverse * jnp.mean(
        scaled * values, axis=-1, keepdims=True
    )


def scores_of(query_rows, keys_rot, segment, offset):
    row_count = query_rows.shape[0]
    places = jnp.arange(segment.shape[0], dtype=jnp.int32)
    scores = jnp.einsum(
        "qgrd,kgd->grqk", query_rows, keys_rot, preferred_element_type=F32
    ) * HD ** (-0.5)
    row_segment = lax.dynamic_slice_in_dim(segment, offset, row_count)
    row_place = offset + jnp.arange(row_count, dtype=jnp.int32)
    allowed = (row_segment[:, None] == segment[None, :]) & (places[None, :] <= row_place[:, None])
    return jnp.where(allowed, scores, NEG)


def attend(queries, keys_rot, values, segment, block_rows):
    length = queries.shape[0]

    def one_block(block_index):
        offset = block_index * block_rows
        query_rows = lax.dynamic_slice_in_dim(queries, offset, block_rows)
        scores = scores_of(query_rows, keys_rot, segment, offset)
        log_total = jax.nn.logsumexp(scores, axis=-1)
        probs = jnp.exp(scores - log_total[..., None]).astype(BF)
        block_out = jnp.einsum("grqk,kgd->qgrd", probs, values, preferred_element_type=F32)
        return (block_out.astype(BF), log_total)

    outputs, log_totals = lax.map(one_block, jnp.arange(length // block_rows, dtype=jnp.int32))
    return (outputs.reshape(length, -1), log_totals)


def attend_back(queries, keys_rot, values, grad_heads, log_totals, segment, block_rows):
    length = queries.shape[0]
    scale = HD ** (-0.5)

    def one_block(totals, block_item):
        grad_keys, grad_values = totals
        block_index, log_total = block_item
        offset = block_index * block_rows
        query_rows = lax.dynamic_slice_in_dim(queries, offset, block_rows)
        grad_rows = lax.dynamic_slice_in_dim(grad_heads, offset, block_rows)
        scores = scores_of(query_rows, keys_rot, segment, offset)
        probs = jnp.exp(scores - log_total[..., None])
        grad_probs = jnp.einsum("qgrd,kgd->grqk", grad_rows, values, preferred_element_type=F32)
        inner_sum = jnp.sum(probs * grad_probs, axis=-1, keepdims=True)
        grad_scores = (probs * (grad_probs - inner_sum)).astype(BF)
        grad_query = (
            jnp.einsum("grqk,kgd->qgrd", grad_scores, keys_rot, preferred_element_type=F32) * scale
        )
        grad_keys = (
            grad_keys
            + jnp.einsum("grqk,qgrd->kgd", grad_scores, query_rows, preferred_element_type=F32)
            * scale
        )
        grad_values = grad_values + jnp.einsum(
            "grqk,qgrd->kgd", probs.astype(BF), grad_rows, preferred_element_type=F32
        )
        return ((grad_keys, grad_values), grad_query)

    empty_grad = jnp.zeros(keys_rot.shape, F32)
    indices = jnp.arange(length // block_rows, dtype=jnp.int32)
    (grad_keys, grad_values), grad_query = lax.scan(
        one_block, (empty_grad, empty_grad), (indices, log_totals)
    )
    return (grad_query.reshape(queries.shape), grad_keys, grad_values)


def per_device(
    dp_count,
    hidden_in,
    segments,
    attn_gain,
    w_query,
    w_key,
    w_value,
    w_out,
    mlp_gain,
    w_gate,
    w_up,
    w_down,
    cotangent,
):
    ring = Ring(dp_count)
    place = lax.axis_index("tensor")
    chip, core = place // 2, place % 2
    rows, width = hidden_in.shape
    length = segments.shape[0]
    query_columns, key_columns = w_query.shape[1], w_key.shape[1]
    query_heads, key_heads = query_columns // HD, key_columns // HD
    units = w_gate.shape[1]
    gain_one = attn_gain.astype(F32)[:, None]
    gain_two = mlp_gain.astype(F32)[:, None]

    w_qkv = jnp.concatenate([w_query, w_key, w_value], axis=1)
    w_gate_up = jnp.concatenate([w_gate, w_up], axis=1)
    shard_qkv = (w_qkv.astype(F32) * gain_one).astype(BF)
    shard_gate_up = (w_gate_up.astype(F32) * gain_two).astype(BF)
    shard_attn = jnp.concatenate([shard_qkv, w_out.T], axis=1)
    full_attn = assemble(ring, gather_pieces(ring, shard_attn))
    full_gate_up = assemble(ring, gather_pieces(ring, shard_gate_up))
    full_down = assemble(ring, gather_pieces(ring, w_down.T))
    qkv_columns = w_qkv.shape[1]
    full_qkv, full_out = full_attn[:, :qkv_columns], full_attn[:, qkv_columns:]

    hidden = gather_tokens(hidden_in, core, chip)
    grad_rows = gather_tokens(cotangent, core, chip)
    hidden_f = hidden.astype(F32)
    normed = (hidden_f * inverse_rms(hidden_f)).astype(BF).reshape(length, width)
    block_rows = min(512, length)
    cosine_table, sine_table = rope_tables(segments)
    projected = matmul(normed, full_qkv)
    queries = projected[:, :query_columns].reshape(length, query_heads, HD)
    queries = rotate(queries, cosine_table, sine_table).astype(BF)
    queries = queries.reshape(length, key_heads, query_heads // key_heads, HD)
    keys_rot = projected[:, query_columns : query_columns + key_columns]
    keys_rot = rotate(keys_rot.reshape(length, key_heads, HD), cosine_table, sine_table).astype(BF)
    values = projected[:, query_columns + key_columns :].astype(BF)
    values = values.reshape(length, key_heads, HD)
    heads_out, log_totals = attend(queries, keys_rot, values, segments, block_rows)

    branch = right_t(heads_out, full_out).reshape(2, 2, rows, width)
    resid, inverse_two, normed_two = [], [], []
    for block in range(2):
        total = sum_both(branch[block], core)
        resid.append(pick(hidden[block], core).astype(F32) + total)
        inverse_two.append(inverse_rms(resid[block]))
        part = (resid[block] * inverse_two[block]).astype(BF)
        normed_two.append(in_order(part, swap_core(part), core))
    normed_two = jnp.stack(normed_two).reshape(length, width)
    resid = jnp.stack(resid)
    inverse_two = jnp.stack(inverse_two)

    gate_up = matmul(normed_two, full_gate_up)
    gate_pre, upward = gate_up[:, :units], gate_up[:, units:]
    sigmoid_gate = jax.nn.sigmoid(gate_pre)
    silu_gate = gate_pre * sigmoid_gate
    activated = (silu_gate * upward).astype(BF)
    down = right_t(activated, full_down).reshape(2, 2, rows, width)
    output = pick(resid, chip) + sum_own(down, core, chip)

    grad_rows_flat = grad_rows.reshape(length, width)
    grad_down_w = scatter_sum(ring, left_t(grad_rows_flat, activated).astype(BF))
    grad_act = matmul(grad_rows_flat, full_down)
    grad_gate = (grad_act * upward * sigmoid_gate * (1.0 + gate_pre * (1.0 - sigmoid_gate))).astype(
        BF
    )
    grad_up = (grad_act * silu_gate).astype(BF)
    grad_gate_up = jnp.concatenate([grad_gate, grad_up], axis=1)
    grad_gate_up_w = scatter_sum(ring, left_t(normed_two, grad_gate_up).astype(BF))
    scaled_two = right_t(grad_gate_up, full_gate_up).reshape(2, 2, rows, width)
    grad_resid, grad_branch = [], []
    for block in range(2):
        total = sum_both(scaled_two[block], core)
        upstream = pick(grad_rows[block], core).astype(F32)
        grad_resid.append(upstream + norm_back(total, resid[block], inverse_two[block]))
        part = grad_resid[block].astype(BF)
        grad_branch.append(in_order(part, swap_core(part), core))
    grad_branch = jnp.stack(grad_branch).reshape(length, width)
    grad_resid = pick(jnp.stack(grad_resid), chip)

    grad_out_w = left_t(grad_branch, heads_out).astype(BF)
    grad_heads = matmul(grad_branch, full_out).astype(BF).reshape(queries.shape)
    grad_query, grad_keys, grad_values = attend_back(
        queries, keys_rot, values, grad_heads, log_totals, segments, block_rows
    )
    grad_query = unrotate(grad_query.reshape(length, query_heads, HD), cosine_table, sine_table)
    grad_keys = unrotate(grad_keys, cosine_table, sine_table)
    grad_qkv = jnp.concatenate(
        [
            grad_query.astype(BF).reshape(length, query_columns),
            grad_keys.astype(BF).reshape(length, key_columns),
            grad_values.astype(BF).reshape(length, key_columns),
        ],
        axis=1,
    )
    grad_attn_w = scatter_sum(
        ring, jnp.concatenate([left_t(normed, grad_qkv).astype(BF), grad_out_w], axis=1)
    )
    scaled_one = sum_own(right_t(grad_qkv, full_qkv).reshape(2, 2, rows, width), core, chip)
    own = hidden_in.astype(F32)
    hidden_grad = (grad_resid + norm_back(scaled_one, own, inverse_rms(own))).astype(BF)

    grad_qkv_w = grad_attn_w[:, :qkv_columns]
    gain_parts = jnp.stack(
        [
            jnp.sum(grad_qkv_w * w_qkv.astype(F32), axis=1),
            jnp.sum(grad_gate_up_w * w_gate_up.astype(F32), axis=1),
        ]
    )
    gain_sums = lax.psum(gain_parts, "tensor")
    grad_qkv_w = grad_qkv_w * gain_one
    grad_gate_up_w = grad_gate_up_w * gain_two
    return (
        output.astype(BF),
        hidden_grad,
        gain_sums[0],
        grad_qkv_w[:, :query_columns],
        grad_qkv_w[:, query_columns : query_columns + key_columns],
        grad_qkv_w[:, query_columns + key_columns :],
        grad_attn_w[:, qkv_columns:].T,
        gain_sums[1],
        grad_gate_up_w[:, :units],
        grad_gate_up_w[:, units:],
        grad_down_w.T,
    )


def solution(mesh):
    in_specs = (
        P(("dp", "tensor"), None),
        P("dp"),
        P("dp"),
        P("dp", "tensor"),
        P("dp", "tensor"),
        P("dp", "tensor"),
        P("tensor", "dp"),
        P("dp"),
        P("dp", "tensor"),
        P("dp", "tensor"),
        P("tensor", "dp"),
        P(("dp", "tensor"), None),
    )
    out_specs = (
        P(("dp", "tensor"), None),
        P(("dp", "tensor"), None),
        P("dp"),
        P("dp", "tensor"),
        P("dp", "tensor"),
        P("dp", "tensor"),
        P("tensor", "dp"),
        P("dp"),
        P("dp", "tensor"),
        P("dp", "tensor"),
        P("tensor", "dp"),
    )
    dp_count = mesh.shape["dp"]

    def body(*arrays):
        return per_device(dp_count, *arrays)

    return jax.shard_map(body, mesh=mesh, in_specs=in_specs, out_specs=out_specs, check_vma=False)
```

```python
import functools
import math

import jax
import jax.numpy as jnp
from jax import lax
from jax.experimental import pallas as pl
from jax.experimental.pallas import tpu as pltpu
from jax.sharding import PartitionSpec as P

HD = 96
HALF = HD // 2
EPS = 1e-05
NEG = -1e30
THETA = 100000.0
SCALE = HD ** (-0.5)
LOG2E = math.log2(math.e)
BF = jnp.bfloat16
F32 = jnp.float32
MIB = 1024 * 1024

CORE_PAIRS = [(0, 1), (1, 0), (2, 3), (3, 2)]
X_PAIRS = [(0, 2), (2, 0), (1, 3), (3, 1)]


def dot(left_side, right_side):
    return jnp.dot(left_side, right_side, preferred_element_type=F32)


def dot_nt(left_side, right_side):
    return lax.dot_general(
        left_side, right_side, (((1,), (1,)), ((), ())), preferred_element_type=F32
    )


def turned(value):
    return value.astype(F32).T


def after(value, *others):
    return lax.optimization_barrier((value, *others))[0]


def params(mib):
    return pltpu.CompilerParams(vmem_limit_bytes=mib * MIB)


def cost(flops, size, exps=0):
    return pl.CostEstimate(flops=flops, bytes_accessed=size, transcendentals=exps)


ANY = pl.BlockSpec(memory_space=pl.ANY)
SMEM = pl.BlockSpec(memory_space=pltpu.SMEM)
VMEM = pl.BlockSpec(memory_space=pltpu.VMEM)


def assemble_kernel(spans, place_ref, *refs):
    pieces, whole, sems = refs[: len(spans)], refs[len(spans)], refs[len(spans) + 1]
    copies = []
    for k, (column, width) in enumerate(spans):
        rows = pieces[k].shape[0]
        at = pl.multiple_of(place_ref[k], 16)
        copies.append(
            pltpu.make_async_copy(
                pieces[k], whole.at[pl.ds(at, rows), pl.ds(column, width)], sems.at[k]
            )
        )
    for copy in copies:
        copy.start()
    for copy in copies:
        copy.wait()


def assemble(ring, pieces):
    rows, columns = pieces[0][2].shape
    spans = tuple((column, piece.shape[1]) for _, column, piece in pieces)
    places = jnp.stack([ring.index(offset) * rows for offset, _, _ in pieces])
    size = ring.count * rows * columns * 2
    return pl.pallas_call(
        functools.partial(assemble_kernel, spans),
        in_specs=[SMEM] + [ANY] * len(spans),
        out_specs=ANY,
        out_shape=jax.ShapeDtypeStruct((ring.count * rows, columns), BF),
        scratch_shapes=[pltpu.SemaphoreType.DMA((len(spans),))],
        compiler_params=params(16),
        cost_estimate=cost(0, 2 * size),
        name="assemble",
    )(places.astype(jnp.int32), *[piece for _, _, piece in pieces])


def rope_rows(values, cosine, sine):
    first, second = values[:HALF], values[HALF:]
    return first * cosine - second * sine, second * cosine + first * sine


def project_kernel(query_heads, key_heads, x_ref, w_ref, c_ref, s_ref, o_ref):
    turned_heads = dot(x_ref[...], w_ref[...]).T
    cosine, sine = c_ref[...], s_ref[...]
    for h in range(query_heads + key_heads):
        first, second = rope_rows(turned_heads[h * HD : (h + 1) * HD], cosine, sine)
        if h < query_heads:
            first, second = first * (SCALE * LOG2E), second * (SCALE * LOG2E)
        o_ref[h * HD : h * HD + HALF, :] = first.astype(BF)
        o_ref[h * HD + HALF : (h + 1) * HD, :] = second.astype(BF)
    done = (query_heads + key_heads) * HD
    o_ref[done:, :] = turned_heads[done:].astype(BF)


def project(x, w, cosine, sine, query_heads, key_heads, block):
    n, d = x.shape
    columns = (query_heads + 2 * key_heads) * HD
    return pl.pallas_call(
        functools.partial(project_kernel, query_heads, key_heads),
        grid=(n // block,),
        in_specs=[
            pl.BlockSpec((block, d), lambda i: (i, 0)),
            pl.BlockSpec((d, columns), lambda i: (0, 0)),
            pl.BlockSpec((HALF, block), lambda i: (0, i)),
            pl.BlockSpec((HALF, block), lambda i: (0, i)),
        ],
        out_specs=pl.BlockSpec((columns, block), lambda i: (0, i)),
        out_shape=jax.ShapeDtypeStruct((columns, n), BF),
        compiler_params=params(40),
        cost_estimate=cost(2 * n * d * columns, 2 * (n * d + d * columns + n * columns)),
        name="project",
    )(x, w, cosine, sine)


def side(ref, low, high):
    return jnp.concatenate(
        [ref[h * HD : (h + 1) * HD, low:high] for h in range(ref.shape[0] // HD)], axis=1
    )


def attend_kernel(block, q_ref, k_ref, v_ref, start_ref, o_ref, l_ref):
    n, group = q_ref.shape[1], q_ref.shape[0] // HD
    keys = turned(k_ref[...]).astype(BF)
    row = lax.broadcasted_iota(jnp.int32, (block, group * block), 0)
    column = lax.broadcasted_iota(jnp.int32, (block, group * block), 1) % block
    for i in range(n // block):
        low, high = i * block, (i + 1) * block
        start = jnp.concatenate([start_ref[:, low:high]] * group, axis=1)
        scores = dot(keys[:high], side(q_ref, low, high))
        at = lax.broadcasted_iota(jnp.int32, (high, group * block), 0)
        scores = jnp.where(at >= start, scores, NEG)
        near = jnp.where(row <= column, scores[low:], NEG)
        top = jnp.max(near, axis=0, keepdims=True)
        if i:
            top = jnp.maximum(top, jnp.max(scores[:low], axis=0, keepdims=True))
        near = jnp.exp2(near - top)
        total = jnp.sum(near, axis=0, keepdims=True)
        out = dot(v_ref[:, low:high], near.astype(BF))
        if i:
            far = jnp.exp2(scores[:low] - top)
            total = total + jnp.sum(far, axis=0, keepdims=True)
            out = out + dot(v_ref[:, :low], far.astype(BF))
        out = out * (1.0 / total)
        log_total = top + jnp.log2(total)
        for h in range(group):
            part = slice(h * block, (h + 1) * block)
            o_ref[h * HD : (h + 1) * HD, low:high] = out[:, part].astype(BF)
            l_ref[0, h : h + 1, low:high] = log_total[:, part]


def attend(qkv, start, query_heads, key_heads, block):
    n, group = qkv.shape[1], query_heads // key_heads
    return pl.pallas_call(
        functools.partial(attend_kernel, block),
        grid=(key_heads,),
        in_specs=[
            pl.BlockSpec((group * HD, n), lambda i: (i, 0)),
            pl.BlockSpec((HD, n), lambda i: (query_heads + i, 0)),
            pl.BlockSpec((HD, n), lambda i: (query_heads + key_heads + i, 0)),
            pl.BlockSpec((1, n), lambda i: (0, 0)),
        ],
        out_specs=[
            pl.BlockSpec((group * HD, n), lambda i: (i, 0)),
            pl.BlockSpec((1, group, n), lambda i: (i, 0, 0)),
        ],
        out_shape=[
            jax.ShapeDtypeStruct((query_heads * HD, n), BF),
            jax.ShapeDtypeStruct((key_heads, group, n), F32),
        ],
        compiler_params=params(40),
        cost_estimate=cost(
            4 * n * n * HD * query_heads, 4 * n * HD * (query_heads + key_heads),
            n * n * query_heads // 2,
        ),
        name="attend",
    )(qkv, qkv, qkv, start)


def attend_back_kernel(
    block, q_ref, k_ref, v_ref, g_ref, h_ref, l_ref, start_ref, c_ref, s_ref,
    dq_ref, dk_ref, dv_ref, dk_sum, dv_sum,
):
    n, group = q_ref.shape[1], q_ref.shape[0] // HD
    keys = turned(k_ref[...]).astype(BF)
    values = turned(v_ref[...]).astype(BF)
    dk_sum[...] = jnp.zeros_like(dk_sum)
    dv_sum[...] = jnp.zeros_like(dv_sum)
    for i in range(n // block):
        low, high = i * block, (i + 1) * block
        queries, grads = side(q_ref, low, high), side(g_ref, low, high)
        outs = side(h_ref, low, high)
        query_rows, grad_rows = turned(queries).astype(BF), turned(grads).astype(BF)
        inner = jnp.sum(grads.astype(F32) * outs.astype(F32), axis=0, keepdims=True)
        log_total = jnp.concatenate([l_ref[0, h : h + 1, low:high] for h in range(group)], axis=1)
        start = jnp.concatenate([start_ref[:, low:high]] * group, axis=1)
        dq = jnp.zeros((HD, group * block), F32)
        for first, last in ([(0, low)] if i else []) + [(low, high)]:
            scores = dot(keys[first:last], queries)
            at = lax.broadcasted_iota(jnp.int32, scores.shape, 0) + first
            allowed = at >= start
            if first == low:
                column = lax.broadcasted_iota(jnp.int32, scores.shape, 1) % block + low
                allowed = allowed & (at <= column)
            probs = jnp.exp2(jnp.where(allowed, scores - log_total, NEG))
            dp = dot(values[first:last], grads)
            ds = (probs * (dp - inner)).astype(BF)
            dv_sum[first:last, :] += dot(probs.astype(BF), grad_rows)
            dk_sum[first:last, :] += dot(ds, query_rows)
            dq = dq + dot(k_ref[:, first:last], ds)
        dq = dq * SCALE
        cosine, sine = c_ref[:, low:high], s_ref[:, low:high]
        for h in range(group):
            top, bottom = rope_rows(dq[:, h * block : (h + 1) * block], cosine, -sine)
            dq_ref[h * HD : h * HD + HALF, low:high] = top.astype(BF)
            dq_ref[h * HD + HALF : (h + 1) * HD, low:high] = bottom.astype(BF)
    top, bottom = rope_rows(dk_sum[...].T * (1.0 / LOG2E), c_ref[...], -s_ref[...])
    dk_ref[:HALF, :] = top.astype(BF)
    dk_ref[HALF:, :] = bottom.astype(BF)
    dv_ref[...] = dv_sum[...].T.astype(BF)


def attend_back(qkv, grads, heads_out, log_total, start, cosine, sine, query_heads, key_heads, block):
    n, group = qkv.shape[1], query_heads // key_heads
    whole = lambda i: (0, 0)
    wide = pl.BlockSpec((group * HD, n), lambda i: (i, 0))
    narrow = pl.BlockSpec((HD, n), lambda i: (i, 0))
    return pl.pallas_call(
        functools.partial(attend_back_kernel, block),
        grid=(key_heads,),
        in_specs=[
            wide,
            pl.BlockSpec((HD, n), lambda i: (query_heads + i, 0)),
            pl.BlockSpec((HD, n), lambda i: (query_heads + key_heads + i, 0)),
            wide,
            wide,
            pl.BlockSpec((1, group, n), lambda i: (i, 0, 0)),
            pl.BlockSpec((1, n), whole),
            pl.BlockSpec((HALF, n), whole),
            pl.BlockSpec((HALF, n), whole),
        ],
        out_specs=[wide, narrow, narrow],
        out_shape=[
            jax.ShapeDtypeStruct((query_heads * HD, n), BF),
            jax.ShapeDtypeStruct((key_heads * HD, n), BF),
            jax.ShapeDtypeStruct((key_heads * HD, n), BF),
        ],
        scratch_shapes=[pltpu.VMEM((n, HD), F32), pltpu.VMEM((n, HD), F32)],
        compiler_params=params(40),
        cost_estimate=cost(
            10 * n * n * HD * query_heads, 8 * n * HD * (query_heads + key_heads),
            n * n * query_heads // 2,
        ),
        name="attend_back",
    )(qkv, qkv, qkv, grads, heads_out, log_total, start, cosine, sine)


def columns_of(ref, place, block):
    return ref[:, pl.ds(pl.multiple_of(place * block, block), block)]


def branch_kernel(place_ref, h_ref, w_ref, *out_refs):
    for k, out in enumerate(out_refs):
        heads = turned(columns_of(h_ref, place_ref[k], out.shape[0])).astype(BF)
        out[...] = dot_nt(heads, w_ref[...]).astype(BF)


def branch(places, heads_out, w_full, width, rows):
    depth = heads_out.shape[0]
    first = w_full.shape[1] // depth - 1
    d = w_full.shape[0]
    return pl.pallas_call(
        branch_kernel,
        grid=(1,),
        in_specs=[
            SMEM,
            pl.BlockSpec(heads_out.shape, lambda i: (0, 0)),
            pl.BlockSpec((d, depth), lambda i: (0, first)),
        ],
        out_specs=[pl.BlockSpec((rows, d), lambda i: (0, 0))] * len(places),
        out_shape=[jax.ShapeDtypeStruct((rows, d), BF)] * len(places),
        compiler_params=params(40),
        cost_estimate=cost(2 * rows * len(places) * d * depth, 2 * d * (depth + 2 * rows)),
        name="branch",
    )(jnp.stack(places), heads_out, w_full)


def gate_up_kernel(x0_ref, x1_ref, w_ref, act_ref, a_ref, b_ref, x_all):
    rows, half = x0_ref.shape[0], w_ref.shape[1] // 2

    @pl.when(pl.program_id(0) == 0)
    def _():
        x_all[:rows] = x0_ref[...]
        x_all[rows:] = x1_ref[...]

    product = dot(x_all[...], w_ref[...])
    gate, up = product[:, :half], product[:, half:]
    sigmoid = 1.0 / (1.0 + jnp.exp(-gate))
    silu = gate * sigmoid
    act_ref[...] = (silu * up).astype(BF)
    a_ref[...] = (up * sigmoid * (1.0 + gate * (1.0 - sigmoid))).astype(BF)
    b_ref[...] = silu.astype(BF)


def gate_up(x0, x1, w, block):
    rows, d = x0.shape
    units = w.shape[1] // 2
    out = pl.BlockSpec((2 * rows, block), lambda j: (0, j))
    whole = pl.BlockSpec((rows, d), lambda j: (0, 0))
    return pl.pallas_call(
        gate_up_kernel,
        grid=(units // block,),
        in_specs=[whole, whole, pl.BlockSpec((d, 2 * block), lambda j: (0, j))],
        out_specs=[out] * 3,
        out_shape=[jax.ShapeDtypeStruct((2 * rows, units), BF)] * 3,
        scratch_shapes=[pltpu.VMEM((2 * rows, d), BF)],
        compiler_params=params(40),
        cost_estimate=cost(8 * rows * d * units, 4 * (d * units + rows * d), 2 * rows * units),
        name="gate_up",
    )(x0, x1, w)


def mlp_back_kernel(g0_ref, g1_ref, a_ref, b_ref, wd_ref, w_ref, d_ref, u0_ref, u1_ref, g_all, total):
    rows, half = g0_ref.shape[0], a_ref.shape[1]
    step = pl.program_id(0)

    @pl.when(step == 0)
    def _():
        g_all[:rows] = g0_ref[...]
        g_all[rows:] = g1_ref[...]

    grad_act = dot(g_all[...], wd_ref[...])
    d_ref[:, :half] = (grad_act * a_ref[...].astype(F32)).astype(BF)
    d_ref[:, half:] = (grad_act * b_ref[...].astype(F32)).astype(BF)
    part = dot_nt(d_ref[...], w_ref[...])

    @pl.when(step == 0)
    def _():
        total[...] = part

    @pl.when(step > 0)
    def _():
        total[...] += part

    @pl.when(step == pl.num_programs(0) - 1)
    def _():
        u0_ref[...] = total[:rows].astype(BF)
        u1_ref[...] = total[rows:].astype(BF)


def mlp_back(g0, g1, a, b, w_down, w, block):
    rows, d = g0.shape
    units = a.shape[1]
    whole = pl.BlockSpec((rows, d), lambda j: (0, 0))
    narrow = pl.BlockSpec((2 * rows, block), lambda j: (0, j))
    return pl.pallas_call(
        mlp_back_kernel,
        grid=(units // block,),
        in_specs=[
            whole, whole, narrow, narrow,
            pl.BlockSpec((d, block), lambda j: (0, j)),
            pl.BlockSpec((d, 2 * block), lambda j: (0, j)),
        ],
        out_specs=[pl.BlockSpec((2 * rows, 2 * block), lambda j: (0, j)), whole, whole],
        out_shape=[
            jax.ShapeDtypeStruct((2 * rows, 2 * units), BF),
            jax.ShapeDtypeStruct((rows, d), BF),
            jax.ShapeDtypeStruct((rows, d), BF),
        ],
        scratch_shapes=[pltpu.VMEM((2 * rows, d), BF), pltpu.VMEM((2 * rows, d), F32)],
        compiler_params=params(48),
        cost_estimate=cost(12 * rows * d * units, 6 * d * units + 12 * rows * (units + d)),
        name="mlp_back",
    )(g0, g1, a, b, w_down, w)


def weight_grad_kernel(x0_ref, x1_ref, x2_ref, x3_ref, d0_ref, d1_ref, o_ref, x_turned):
    rows = x0_ref.shape[0]

    @pl.when(pl.program_id(0) == 0)
    def _():
        for k, ref in enumerate((x0_ref, x1_ref, x2_ref, x3_ref)):
            x_turned[:, k * rows : (k + 1) * rows] = turned(ref[...]).astype(BF)

    both = 2 * rows
    o_ref[...] = (
        dot(x_turned[:, :both], d0_ref[...]) + dot(x_turned[:, both:], d1_ref[...])
    ).astype(BF)


def weight_grad(pieces, d0, d1, block):
    rows, d = pieces[0].shape
    columns = d0.shape[1]
    whole = pl.BlockSpec((rows, d), lambda j: (0, 0))
    narrow = pl.BlockSpec((2 * rows, block), lambda j: (0, j))
    return pl.pallas_call(
        weight_grad_kernel,
        grid=(columns // block,),
        in_specs=[whole] * 4 + [narrow] * 2,
        out_specs=pl.BlockSpec((d, block), lambda j: (0, j)),
        out_shape=jax.ShapeDtypeStruct((d, columns), BF),
        scratch_shapes=[pltpu.VMEM((d, 4 * rows), BF)],
        compiler_params=params(40),
        cost_estimate=cost(8 * rows * d * columns, 8 * rows * (d + columns) + 2 * d * columns),
        name="weight_grad",
    )(*pieces, d0, d1)


def down_kernel(act_ref, w_ref, o0_ref, o1_ref):
    rows = o0_ref.shape[0]
    out = dot_nt(act_ref[...], w_ref[...])
    o0_ref[...] = out[:rows].astype(BF)
    o1_ref[...] = out[rows:].astype(BF)


def down(act, w_down, block):
    both, units = act.shape
    d = w_down.shape[0]
    out = pl.BlockSpec((both // 2, block), lambda j: (0, j))
    return pl.pallas_call(
        down_kernel,
        grid=(d // block,),
        in_specs=[
            pl.BlockSpec((both, units), lambda j: (0, 0)),
            pl.BlockSpec((block, units), lambda j: (j, 0)),
        ],
        out_specs=[out, out],
        out_shape=[jax.ShapeDtypeStruct((both // 2, d), BF)] * 2,
        compiler_params=params(40),
        cost_estimate=cost(2 * both * d * units, 2 * (both * units + d * units + both * d)),
        name="down",
    )(act, w_down)


def grad_heads_kernel(place_ref, g0_ref, g1_ref, g2_ref, g3_ref, w_ref, o_ref):
    for k, ref in enumerate((g0_ref, g1_ref, g2_ref, g3_ref)):
        rows = ref.shape[0]
        at = pl.multiple_of(place_ref[k] * rows, rows)
        o_ref[:, pl.ds(at, rows)] = dot(ref[...], w_ref[...]).T.astype(BF)


def grad_heads(places, pieces, w_full, depth):
    rows, d = pieces[0].shape
    first = w_full.shape[1] // depth - 1
    whole = pl.BlockSpec((rows, d), lambda i: (0, 0))
    return pl.pallas_call(
        grad_heads_kernel,
        grid=(1,),
        in_specs=[SMEM] + [whole] * 4 + [pl.BlockSpec((d, depth), lambda i: (0, first))],
        out_specs=pl.BlockSpec((depth, 4 * rows), lambda i: (0, 0)),
        out_shape=jax.ShapeDtypeStruct((depth, 4 * rows), BF),
        compiler_params=params(40),
        cost_estimate=cost(8 * rows * d * depth, 2 * d * (depth + 4 * rows)),
        name="grad_heads",
    )(jnp.stack(places), *pieces, w_full)


def grad_x_kernel(place_ref, q_ref, k_ref, v_ref, w_ref, *out_refs):
    for k, out in enumerate(out_refs):
        rows = out.shape[0]
        parts = [columns_of(ref, place_ref[k], rows).astype(F32) for ref in (q_ref, k_ref, v_ref)]
        grads = jnp.concatenate(parts, axis=0).T.astype(BF)
        out[...] = dot_nt(grads, w_ref[...]).astype(BF)


def grad_x(places, dq, dk, dv, w_full, rows):
    d = w_full.shape[0]
    columns = dq.shape[0] + dk.shape[0] + dv.shape[0]
    whole = lambda i: (0, 0)
    return pl.pallas_call(
        grad_x_kernel,
        grid=(1,),
        in_specs=[
            SMEM,
            pl.BlockSpec(dq.shape, whole),
            pl.BlockSpec(dk.shape, whole),
            pl.BlockSpec(dv.shape, whole),
            pl.BlockSpec((d, columns), whole),
        ],
        out_specs=[pl.BlockSpec((rows, d), whole)] * len(places),
        out_shape=[jax.ShapeDtypeStruct((rows, d), BF)] * len(places),
        compiler_params=params(40),
        cost_estimate=cost(2 * rows * len(places) * d * columns, 2 * columns * (d + 4 * rows)),
        name="grad_x",
    )(jnp.stack(places), dq, dk, dv, w_full)


def attn_grad_kernel(
    place_ref, x_ref, q_ref, k_ref, v_ref, h_ref, g0_ref, g1_ref, g2_ref, g3_ref, o_ref
):
    at = 0
    for ref in (q_ref, k_ref, v_ref):
        size = ref.shape[0]
        o_ref[:, at : at + size] = dot(ref[...], x_ref[...]).T.astype(BF)
        at += size
    total = None
    for k, ref in enumerate((g0_ref, g1_ref, g2_ref, g3_ref)):
        part = dot(columns_of(h_ref, place_ref[k], ref.shape[0]), ref[...])
        total = part if total is None else total + part
    o_ref[:, at:] = total.T.astype(BF)


def attn_grad(places, x, dq, dk, dv, heads_out, pieces):
    n, d = x.shape
    rows = pieces[0].shape[0]
    columns = dq.shape[0] + dk.shape[0] + dv.shape[0] + heads_out.shape[0]
    whole = lambda i: (0, 0)
    arrays = (x, dq, dk, dv, heads_out, *pieces)
    return pl.pallas_call(
        attn_grad_kernel,
        grid=(1,),
        in_specs=[SMEM] + [pl.BlockSpec(a.shape, whole) for a in arrays],
        out_specs=pl.BlockSpec((d, columns), whole),
        out_shape=jax.ShapeDtypeStruct((d, columns), BF),
        compiler_params=params(48),
        cost_estimate=cost(2 * n * d * columns, 2 * (2 * n * d + n * columns + d * columns)),
        name="attn_grad",
    )(jnp.stack(places), *arrays)


class Ring:
    def __init__(self, count):
        self.count = count
        self.half = count // 2
        order = [2 * k if k < self.half else 2 * (count - 1 - k) + 1 for k in range(count)]
        self.right = [(order[k], order[(k + 1) % count]) for k in range(count)]
        self.left = [(b, a) for a, b in self.right]
        me = lax.axis_index("dp")
        self.place = jnp.where(me % 2 == 0, me // 2, count - 1 - me // 2)

    def index(self, offset):
        place = (self.place + offset + self.count) % self.count
        return jnp.where(place < self.half, 2 * place, 2 * (self.count - 1 - place) + 1)

    def go_right(self, value):
        return lax.ppermute(value, "dp", self.right)

    def go_left(self, value):
        return lax.ppermute(value, "dp", self.left)


def cut_of(columns):
    return max(128, (columns // 2 + 127) // 128 * 128)


def gather_pieces(ring, shard):
    cut = cut_of(shard.shape[1])
    pieces = [(0, 0, shard)]
    from_left = from_right = shard
    for step in range(1, ring.half):
        from_left = ring.go_right(from_left)
        from_right = ring.go_left(from_right)
        pieces += [(-step, 0, from_left), (step, 0, from_right)]
    pieces.append((-ring.half, 0, ring.go_right(from_left[:, :cut])))
    pieces.append((ring.half, cut, ring.go_left(from_right[:, cut:])))
    return pieces


def scatter_sum(ring, whole):
    rows, columns = whole.shape[0] // ring.count, whole.shape[1]
    cut = cut_of(columns)

    def chunk(offset):
        return lax.dynamic_slice(whole, (ring.index(offset) * rows, 0), (rows, columns))

    far = chunk(ring.half)
    from_left = ring.go_right(far[:, :cut])
    from_right = ring.go_left(far[:, cut:])
    for step in range(ring.half - 1, 0, -1):
        to_right, to_left = chunk(step).astype(F32), chunk(-step).astype(F32)
        if step == ring.half - 1:
            to_right = jnp.concatenate(
                [to_right[:, :cut] + from_left.astype(F32), to_right[:, cut:]], axis=1
            )
            to_left = jnp.concatenate(
                [to_left[:, :cut], to_left[:, cut:] + from_right.astype(F32)], axis=1
            )
        else:
            to_right = to_right + from_left.astype(F32)
            to_left = to_left + from_right.astype(F32)
        from_left = ring.go_right(to_right.astype(BF))
        from_right = ring.go_left(to_left.astype(BF))
    return chunk(0).astype(F32) + from_left.astype(F32) + from_right.astype(F32)


def swap_core(value):
    return lax.ppermute(value, "tensor", CORE_PAIRS)


def swap_x(value):
    return lax.ppermute(value, "tensor", X_PAIRS)


def gather_tokens(own):
    across = swap_x(own)
    return own, swap_core(own), across, swap_core(across)


def plus(left_side, right_side):
    return (left_side.astype(F32) + right_side.astype(F32)).astype(BF)


def sum_both(own, mate, across, far):
    across_chip = plus(across, swap_core(far))
    own_theirs = swap_x(across_chip)
    own_chip = plus(own, swap_core(mate))
    across_theirs = swap_x(own_chip)
    return (
        own_chip.astype(F32) + own_theirs.astype(F32),
        across_chip.astype(F32) + across_theirs.astype(F32),
    )


def sum_own(own, mate, across, far):
    theirs = swap_x(plus(across, swap_core(far)))
    return own.astype(F32) + swap_core(mate).astype(F32) + theirs.astype(F32)


def rope_tables(segment):
    places = jnp.arange(segment.shape[0], dtype=jnp.int32)
    previous = jnp.concatenate([segment[:1] - 1, segment[:-1]])
    opening = lax.cummax(jnp.where(segment != previous, places, 0), axis=0)
    position = (places - opening).astype(F32)
    inverse = jnp.exp(-(2.0 * jnp.arange(HALF, dtype=F32) / HD) * math.log(THETA))
    angle = inverse[:, None] * position[None, :]
    return jnp.cos(angle), jnp.sin(angle), opening[None, :]


def inverse_rms(values):
    return lax.rsqrt(jnp.mean(values * values, axis=-1, keepdims=True) + EPS)


def norm_back(scaled, values, inverse):
    return inverse * scaled - values * inverse * inverse * inverse * jnp.mean(
        scaled * values, axis=-1, keepdims=True
    )


def interleave(left_side, right_side, block):
    rows, columns = left_side.shape
    both = jnp.stack(
        [left_side.reshape(rows, -1, block), right_side.reshape(rows, -1, block)], axis=2
    )
    return both.reshape(rows, 2 * columns)


def separate(both, block):
    rows, columns = both.shape
    both = both.reshape(rows, -1, 2, block)
    return both[:, :, 0].reshape(rows, columns // 2), both[:, :, 1].reshape(rows, columns // 2)


def per_device(
    dp_count,
    hidden_in,
    segments,
    attn_gain,
    w_query,
    w_key,
    w_value,
    w_out,
    mlp_gain,
    w_gate,
    w_up,
    w_down,
    cotangent,
):
    ring = Ring(dp_count)
    device = lax.axis_index("tensor").astype(jnp.int32)
    places = [device ^ k for k in range(4)]
    rows, width = hidden_in.shape
    query_columns, key_columns = w_query.shape[1], w_key.shape[1]
    query_heads, key_heads = query_columns // HD, key_columns // HD
    qkv_columns = query_columns + 2 * key_columns
    block = min(256, w_gate.shape[1])
    gain_one = attn_gain.astype(F32)[:, None]
    gain_two = mlp_gain.astype(F32)[:, None]

    w_qkv = jnp.concatenate([w_query, w_key, w_value], axis=1)
    w_gate_up = interleave(w_gate, w_up, block)
    shard_qkv = (w_qkv.astype(F32) * gain_one).astype(BF)
    shard_gate_up = (w_gate_up.astype(F32) * gain_two).astype(BF)
    pieces_attn = gather_pieces(ring, jnp.concatenate([shard_qkv, w_out.T], axis=1))
    full_attn = assemble(ring, pieces_attn)
    full_gate_up = assemble(ring, gather_pieces(ring, shard_gate_up))
    full_down = assemble(ring, gather_pieces(ring, w_down.T))

    hidden = gather_tokens(hidden_in)
    grads = gather_tokens(cotangent)
    normed = jnp.zeros((4 * rows, width), BF)
    for piece, at in zip(hidden, places):
        part = piece.astype(F32)
        part = (part * inverse_rms(part)).astype(BF)
        normed = lax.dynamic_update_slice(normed, part, (at * rows, 0))
    cosine, sine, start = rope_tables(segments)
    qkv = project(normed, full_attn, cosine, sine, query_heads, key_heads, rows)
    heads_out, log_total = attend(qkv, start, query_heads, key_heads, rows)

    across_part, far_part = branch([places[2], places[3]], heads_out, full_attn, width, rows)
    own_part, mate_part = branch([places[0], places[1]], heads_out, full_attn, width, rows)
    sums = sum_both(own_part, mate_part, across_part, far_part)
    resid = [hidden[2 * k].astype(F32) + sums[k] for k in range(2)]
    inverse_two = [inverse_rms(value) for value in resid]
    normed_two, mlp = [], []
    for k in range(2):
        part = (resid[k] * inverse_two[k]).astype(BF)
        normed_two += [part, swap_core(part)]
        mlp.append(gate_up(part, normed_two[-1], full_gate_up, block))
    down_parts = [down(mlp[k][0], full_down, 256) for k in range(2)]
    output = resid[0] + sum_own(*down_parts[0], *down_parts[1])

    grad_down_w = scatter_sum(ring, weight_grad(grads, mlp[0][0], mlp[1][0], 2 * block))
    back = [
        mlp_back(grads[2 * k], grads[2 * k + 1], mlp[k][1], mlp[k][2], full_down, full_gate_up, block)
        for k in range(2)
    ]
    grad_gate_up_w = scatter_sum(ring, weight_grad(normed_two, back[0][0], back[1][0], 2 * block))
    sums = sum_both(*back[0][1:], *back[1][1:])
    grad_resid, grad_branch = [], []
    for k in range(2):
        grad_resid.append(
            grads[2 * k].astype(F32) + norm_back(sums[k], resid[k], inverse_two[k])
        )
        part = grad_resid[k].astype(BF)
        grad_branch += [part, swap_core(part)]

    grad_out = grad_heads(places, grad_branch, full_attn, query_columns)
    dq, dk, dv = attend_back(
        qkv, grad_out, heads_out, log_total, start, cosine, sine, query_heads, key_heads, rows
    )
    across_part, far_part = grad_x([places[2], places[3]], dq, dk, dv, full_attn, rows)
    own_part, mate_part = grad_x([places[0], places[1]], dq, dk, dv, full_attn, rows)
    scaled_one = sum_own(own_part, mate_part, across_part, far_part)
    grad_attn_w = scatter_sum(
        ring, attn_grad(places, normed, dq, dk, dv, heads_out, grad_branch)
    )
    own = hidden_in.astype(F32)
    hidden_grad = (grad_resid[0] + norm_back(scaled_one, own, inverse_rms(own))).astype(BF)

    grad_qkv_w = grad_attn_w[:, :qkv_columns]
    gain_parts = jnp.stack(
        [
            jnp.sum(grad_qkv_w * w_qkv.astype(F32), axis=1),
            jnp.sum(grad_gate_up_w * w_gate_up.astype(F32), axis=1),
        ]
    )
    gain_sums = lax.psum(gain_parts, "tensor")
    grad_qkv_w = grad_qkv_w * gain_one
    grad_gate_w, grad_up_w = separate(grad_gate_up_w * gain_two, block)
    return (
        output.astype(BF),
        hidden_grad,
        gain_sums[0],
        grad_qkv_w[:, :query_columns],
        grad_qkv_w[:, query_columns : query_columns + key_columns],
        grad_qkv_w[:, query_columns + key_columns :],
        grad_attn_w[:, qkv_columns:].T,
        gain_sums[1],
        grad_gate_w,
        grad_up_w,
        grad_down_w.T,
    )


def solution(mesh):
    tokens, split = P(("dp", "tensor"), None), P("dp", "tensor")
    in_specs = (
        tokens, P("dp"), P("dp"), split, split, split, P("tensor", "dp"),
        P("dp"), split, split, P("tensor", "dp"), tokens,
    )
    out_specs = (
        tokens, tokens, P("dp"), split, split, split, P("tensor", "dp"),
        P("dp"), split, split, P("tensor", "dp"),
    )
    body = functools.partial(per_device, mesh.shape["dp"])
    return jax.shard_map(body, mesh=mesh, in_specs=in_specs, out_specs=out_specs, check_vma=False)
```

```python
import functools
import math

import jax
import jax.numpy as jnp
from jax import lax
from jax.experimental import pallas as pl
from jax.experimental.pallas import tpu as pltpu
from jax.sharding import PartitionSpec as P

HD = 96
HALF = HD // 2
EPS = 1e-05
NEG = -1e30
THETA = 100000.0
SCALE = HD ** (-0.5)
LOG2E = math.log2(math.e)
BF = jnp.bfloat16
F32 = jnp.float32
MIB = 1024 * 1024

CORE_PAIRS = [(0, 1), (1, 0), (2, 3), (3, 2)]
X_PAIRS = [(0, 2), (2, 0), (1, 3), (3, 1)]


def dot(left_side, right_side):
    return jnp.dot(left_side, right_side, preferred_element_type=F32)


def dot_nt(left_side, right_side):
    return lax.dot_general(
        left_side, right_side, (((1,), (1,)), ((), ())), preferred_element_type=F32
    )


def turned(value):
    return value.astype(F32).T


class Order:
    def __init__(self):
        self.before = []

    def wait(self, *values):
        self.before += values
        return values[0] if len(values) == 1 else values

    def call(
        self, body, name, mib, args, in_specs, out_specs, out_shape, grid=(1,), scratch=(),
        prefetch=(), aliases=None,
    ):
        seen = [a for a in self.before if not any(a is b for b in args)]
        first, extra = len(prefetch) + len(args), len(seen)

        def kernel(*refs):
            body(*refs[:first], *refs[first + extra :])

        out = pl.pallas_call(
            kernel,
            grid_spec=pltpu.PrefetchScalarGridSpec(
                num_scalar_prefetch=len(prefetch),
                grid=grid,
                in_specs=[*in_specs, *[ANY] * extra],
                out_specs=out_specs,
                scratch_shapes=scratch,
            ),
            out_shape=out_shape,
            input_output_aliases=aliases or {},
            compiler_params=pltpu.CompilerParams(vmem_limit_bytes=mib * MIB),
            cost_estimate=pl.CostEstimate(flops=0, bytes_accessed=0, transcendentals=0),
            name=name,
        )(*prefetch, *args, *seen)
        self.before = [out[0]]
        return out


def full(shape):
    return pl.BlockSpec(tuple(shape), lambda *_: (0,) * len(shape))


def wholes(arrays):
    return [full(a.shape) for a in arrays]


def like(*shapes):
    return [jax.ShapeDtypeStruct(shape, dtype) for *shape, dtype in shapes]


ANY = pl.BlockSpec(memory_space=pl.ANY)
HBM = pl.BlockSpec(memory_space=pltpu.HBM)
VMEM = pl.BlockSpec(memory_space=pltpu.VMEM)


def column(row):
    return jnp.broadcast_to(row.astype(F32), (8, row.shape[1])).T[:, :1]


def put(outs, whole_ref, at, first, value):
    top, width = outs[0].shape[0], value.shape[1]
    outs[0][:, first : first + width] = value[:top]
    if len(outs) > 1:
        outs[1][:, first : first + width] = value[top:]
    whole_ref[pl.ds(at, value.shape[0]), first : first + width] = value


def shard_kernel(scaled, plain, place_ref, gain_ref, *refs):
    gain, first = column(gain_ref[...]), 0
    at = pl.multiple_of(place_ref[0], 16)
    inputs, outs = refs[: scaled + plain], refs[scaled + plain :]
    for k, ref in enumerate(inputs):
        value = (ref[...].astype(F32) * gain).astype(BF) if k < scaled else ref[...]
        put(outs[:-1], outs[-1], at, first, value)
        first += ref.shape[1]


def top_of(rows):
    return (rows // 2 + 15) // 16 * 16


def make_shard(order, ring, gain, scaled, plain, name, mib, split):
    rows = gain.shape[1]
    columns = sum(w.shape[1] for w in (*scaled, *plain))
    top = top_of(rows) if split else rows
    shapes = [(count, columns) for count in (top, rows - top) if count]
    whole = (ring.count * rows, columns)
    return order.call(
        functools.partial(shard_kernel, len(scaled), len(plain)), name, mib,
        (gain, *scaled, *plain), wholes((gain, *scaled, *plain)),
        [*[full(shape) for shape in shapes], VMEM],
        like(*[(*shape, BF) for shape in (*shapes, whole)]),
        prefetch=((ring.index(0) * rows)[None].astype(jnp.int32),),
    )


def relay_kernel(*refs):
    pass


def relay(order, *values):
    count = len(values)
    return order.call(
        relay_kernel, "relay", 2, values, [ANY] * count, [ANY] * count,
        like(*[(*value.shape, value.dtype) for value in values]),
        aliases={k: k for k in range(count)},
    )


def keep_kernel(spans, place_ref, *refs):
    count = len(spans)
    pieces, whole, sems = refs[:count], refs[2 * count + 1], refs[-1]
    copies = []
    for k, (first, width) in enumerate(spans):
        at = pl.multiple_of(place_ref[k], 16)
        where = whole.at[pl.ds(at, pieces[k].shape[0]), pl.ds(first, width)]
        copies.append(pltpu.make_async_copy(pieces[k], where, sems.at[k]))
    for copy in copies:
        copy.start()
    for copy in copies:
        copy.wait()


def keep(order, places, firsts, pieces, whole):
    count = len(pieces)
    spans = tuple((first, piece.shape[1]) for first, piece in zip(firsts, pieces))
    arrays = (*pieces, whole)
    *pieces, whole = order.call(
        functools.partial(keep_kernel, spans), "keep", 2, arrays, [*[ANY] * count, VMEM],
        [*[ANY] * count, VMEM], like(*[(*a.shape, BF) for a in arrays]),
        scratch=[pltpu.SemaphoreType.DMA((count,))],
        prefetch=(jnp.stack(places).astype(jnp.int32),),
        aliases={1 + k: k for k in range(count + 1)},
    )
    return pieces, whole


def halves_kernel(cut, a_ref, b_ref, c_ref, d_ref):
    c_ref[...] = a_ref[:, :cut]
    d_ref[...] = b_ref[:, cut:]


def halves(order, right, left, cut):
    rows, columns = right.shape
    shapes = (rows, cut), (rows, columns - cut)
    return order.call(
        functools.partial(halves_kernel, cut), "halves", 6, (right, left), wholes((right, left)),
        [full(shape) for shape in shapes], like(*[(*shape, BF) for shape in shapes]),
    )


def far_kernel(cut, index_ref, chunk_ref, c_ref, d_ref):
    c_ref[...] = chunk_ref[:, :cut]
    d_ref[...] = chunk_ref[:, cut:]


def far_chunk(order, whole, rows, first, width, index, cut):
    shapes = (rows, cut), (rows, width - cut)
    return order.call(
        functools.partial(far_kernel, cut), "far_chunk", 8, (whole,),
        [pl.BlockSpec((rows, width), lambda i, index: (index[0], first // width))],
        [full(shape) for shape in shapes], like(*[(*shape, BF) for shape in shapes]),
        prefetch=(index[None].astype(jnp.int32),),
    )


def rope_rows(values, cosine, sine):
    first, second = values[:HALF], values[HALF:]
    return first * cosine - second * sine, second * cosine + first * sine


def project_kernel(query_heads, key_heads, place_ref, x0_ref, x1_ref, w_ref, c_ref, s_ref, o_ref):
    def run(x_ref):
        turned_heads = dot(x_ref[...], w_ref[...]).T
        cosine, sine = c_ref[...], s_ref[...]
        for h in range(query_heads + key_heads):
            first, second = rope_rows(turned_heads[h * HD : (h + 1) * HD], cosine, sine)
            if h < query_heads:
                first, second = first * (SCALE * LOG2E), second * (SCALE * LOG2E)
            o_ref[h * HD : h * HD + HALF, :] = first.astype(BF)
            o_ref[h * HD + HALF : (h + 1) * HD, :] = second.astype(BF)
        done = (query_heads + key_heads) * HD
        o_ref[done:, :] = turned_heads[done:].astype(BF)

    pl.when(pl.program_id(0) < 2)(lambda: run(x0_ref))
    pl.when(pl.program_id(0) >= 2)(lambda: run(x1_ref))


def project(order, places, x0, x1, w, cosine, sine, query_heads, key_heads):
    block, d = x0.shape[0] // 2, x0.shape[1]
    columns = (query_heads + 2 * key_heads) * HD
    table = pl.BlockSpec((HALF, block), lambda i, place: (0, place[i]))
    return order.call(
        functools.partial(project_kernel, query_heads, key_heads), "project", 18,
        (x0, x1, w, cosine, sine),
        [
            pl.BlockSpec((block, d), lambda i, place: (jnp.minimum(i, 1), 0)),
            pl.BlockSpec((block, d), lambda i, place: (jnp.maximum(i - 2, 0), 0)),
            full((d, columns)),
            table,
            table,
        ],
        [pl.BlockSpec((columns, block), lambda i, place: (0, place[i]))],
        like((columns, 4 * block, BF)), grid=(4,), prefetch=(places,),
    )[0]


def side(ref, low, high):
    return jnp.concatenate(
        [ref[h * HD : (h + 1) * HD, low:high] for h in range(ref.shape[0] // HD)], axis=1
    )


def attend_kernel(block, q_ref, k_ref, v_ref, start_ref, o_ref, l_ref):
    n, group = q_ref.shape[1], q_ref.shape[0] // HD
    keys = turned(k_ref[...]).astype(BF)
    row = lax.broadcasted_iota(jnp.int32, (block, group * block), 0)
    column = lax.broadcasted_iota(jnp.int32, (block, group * block), 1) % block
    for i in range(n // block):
        low, high = i * block, (i + 1) * block
        start = jnp.concatenate([start_ref[:, low:high]] * group, axis=1)
        scores = dot(keys[:high], side(q_ref, low, high))
        at = lax.broadcasted_iota(jnp.int32, (high, group * block), 0)
        scores = jnp.where(at >= start, scores, NEG)
        near = jnp.where(row <= column, scores[low:], NEG)
        top = jnp.max(near, axis=0, keepdims=True)
        if i:
            top = jnp.maximum(top, jnp.max(scores[:low], axis=0, keepdims=True))
        near = jnp.exp2(near - top)
        total = jnp.sum(near, axis=0, keepdims=True)
        out = dot(v_ref[:, low:high], near.astype(BF))
        if i:
            far = jnp.exp2(scores[:low] - top)
            total = total + jnp.sum(far, axis=0, keepdims=True)
            out = out + dot(v_ref[:, :low], far.astype(BF))
        out = out * (1.0 / total)
        log_total = top + jnp.log2(total)
        for h in range(group):
            part = slice(h * block, (h + 1) * block)
            o_ref[h * HD : (h + 1) * HD, low:high] = out[:, part].astype(BF)
            l_ref[0, h : h + 1, low:high] = log_total[:, part]


def attend(order, qkv, start, query_heads, key_heads, block):
    n, group = qkv.shape[1], query_heads // key_heads
    return order.call(
        functools.partial(attend_kernel, block), "attend", 20, (qkv, qkv, qkv, start),
        [
            pl.BlockSpec((group * HD, n), lambda i: (i, 0)),
            pl.BlockSpec((HD, n), lambda i: (query_heads + i, 0)),
            pl.BlockSpec((HD, n), lambda i: (query_heads + key_heads + i, 0)),
            full((1, n)),
        ],
        [
            pl.BlockSpec((group * HD, n), lambda i: (i, 0)),
            pl.BlockSpec((1, group, n), lambda i: (i, 0, 0)),
        ],
        like((query_heads * HD, n, BF), (key_heads, group, n, F32)), grid=(key_heads,),
    )


def attend_back_kernel(
    block, q_ref, k_ref, v_ref, g_ref, h_ref, l_ref, start_ref, c_ref, s_ref,
    dq_ref, dk_ref, dv_ref, dk_sum, dv_sum,
):
    n, group = q_ref.shape[1], q_ref.shape[0] // HD
    keys = turned(k_ref[...]).astype(BF)
    values = turned(v_ref[...]).astype(BF)
    dk_sum[...] = jnp.zeros_like(dk_sum)
    dv_sum[...] = jnp.zeros_like(dv_sum)
    for i in range(n // block):
        low, high = i * block, (i + 1) * block
        queries, grads = side(q_ref, low, high), side(g_ref, low, high)
        outs = side(h_ref, low, high)
        query_rows, grad_rows = turned(queries).astype(BF), turned(grads).astype(BF)
        inner = jnp.sum(grads.astype(F32) * outs.astype(F32), axis=0, keepdims=True)
        log_total = jnp.concatenate([l_ref[0, h : h + 1, low:high] for h in range(group)], axis=1)
        start = jnp.concatenate([start_ref[:, low:high]] * group, axis=1)
        dq = jnp.zeros((HD, group * block), F32)
        for first, last in ([(0, low)] if i else []) + [(low, high)]:
            scores = dot(keys[first:last], queries)
            at = lax.broadcasted_iota(jnp.int32, scores.shape, 0) + first
            allowed = at >= start
            if first == low:
                column = lax.broadcasted_iota(jnp.int32, scores.shape, 1) % block + low
                allowed = allowed & (at <= column)
            probs = jnp.exp2(jnp.where(allowed, scores - log_total, NEG))
            dp = dot(values[first:last], grads)
            ds = (probs * (dp - inner)).astype(BF)
            dv_sum[first:last, :] += dot(probs.astype(BF), grad_rows)
            dk_sum[first:last, :] += dot(ds, query_rows)
            dq = dq + dot(k_ref[:, first:last], ds)
        dq = dq * SCALE
        cosine, sine = c_ref[:, low:high], s_ref[:, low:high]
        for h in range(group):
            top, bottom = rope_rows(dq[:, h * block : (h + 1) * block], cosine, -sine)
            dq_ref[h * HD : h * HD + HALF, low:high] = top.astype(BF)
            dq_ref[h * HD + HALF : (h + 1) * HD, low:high] = bottom.astype(BF)
    top, bottom = rope_rows(dk_sum[...].T * (1.0 / LOG2E), c_ref[...], -s_ref[...])
    dk_ref[:HALF, :] = top.astype(BF)
    dk_ref[HALF:, :] = bottom.astype(BF)
    dv_ref[...] = dv_sum[...].T.astype(BF)


def attend_back(order, qkv, grads, heads_out, log_total, start, cosine, sine, query_heads, key_heads, block):
    n, group = qkv.shape[1], query_heads // key_heads
    wide = pl.BlockSpec((group * HD, n), lambda i: (i, 0))
    narrow = pl.BlockSpec((HD, n), lambda i: (i, 0))
    return order.call(
        functools.partial(attend_back_kernel, block), "attend_back", 26,
        (qkv, qkv, qkv, grads, heads_out, log_total, start, cosine, sine),
        [
            wide,
            pl.BlockSpec((HD, n), lambda i: (query_heads + i, 0)),
            pl.BlockSpec((HD, n), lambda i: (query_heads + key_heads + i, 0)),
            wide,
            wide,
            pl.BlockSpec((1, group, n), lambda i: (i, 0, 0)),
            full((1, n)),
            full((HALF, n)),
            full((HALF, n)),
        ],
        [wide, narrow, narrow],
        like((query_heads * HD, n, BF), (key_heads * HD, n, BF), (key_heads * HD, n, BF)),
        grid=(key_heads,), scratch=[pltpu.VMEM((n, HD), F32), pltpu.VMEM((n, HD), F32)],
    )


def columns_of(ref, place, block):
    return ref[:, pl.ds(pl.multiple_of(place * block, block), block)]


def branch_kernel(place_ref, h_ref, w_ref, *out_refs):
    rows = out_refs[0].shape[0] // 2
    for k in range(4):
        heads = turned(columns_of(h_ref, place_ref[k], rows)).astype(BF)
        at = (k % 2) * rows
        out_refs[k // 2][at : at + rows] = dot_nt(heads, w_ref[...]).astype(BF)


def branch(order, places, heads_out, w_full):
    (depth, n), d = heads_out.shape, w_full.shape[0]
    last = w_full.shape[1] // depth - 1
    return order.call(
        branch_kernel, "branch", 18, (heads_out, w_full),
        [full((depth, n)), pl.BlockSpec((d, depth), lambda i, place: (0, last))],
        [full((n // 2, d))] * 2, like((n // 2, d, BF), (n // 2, d, BF)), prefetch=(places,),
    )


def gate_up_kernel(x_ref, wg_ref, wu_ref, act_ref, a_ref, b_ref):
    gate, up = dot(x_ref[...], wg_ref[...]), dot(x_ref[...], wu_ref[...])
    sigmoid = 1.0 / (1.0 + jnp.exp(-gate))
    silu = gate * sigmoid
    act_ref[...] = (silu * up).astype(BF)
    a_ref[...] = (up * sigmoid * (1.0 + gate * (1.0 - sigmoid))).astype(BF)
    b_ref[...] = silu.astype(BF)


def gate_up(order, x, w, block):
    rows, d = x.shape
    units = w.shape[1] // 2
    steps = units // block
    return order.call(
        gate_up_kernel, "gate_up", 24, (x, w, w),
        [
            full((rows, d)),
            pl.BlockSpec((d, block), lambda j: (0, j)),
            pl.BlockSpec((d, block), lambda j: (0, j + steps)),
        ],
        [pl.BlockSpec((rows, block), lambda j: (0, j))] * 3, like(*[(rows, units, BF)] * 3),
        grid=(steps,),
    )


def mlp_back_kernel(g_ref, a_ref, b_ref, wd_ref, wg_ref, wu_ref, u_ref, d_ref, total):
    step, last = pl.program_id(0), pl.num_programs(0) - 1
    grad_act = dot(g_ref[...], wd_ref[...])
    d_ref[0] = (grad_act * a_ref[...].astype(F32)).astype(BF)
    d_ref[1] = (grad_act * b_ref[...].astype(F32)).astype(BF)
    part = dot_nt(d_ref[0], wg_ref[...]) + dot_nt(d_ref[1], wu_ref[...])

    @pl.when(step == 0)
    def _():
        total[...] = part

    @pl.when((step > 0) & (step < last))
    def _():
        total[...] += part

    @pl.when(step == last)
    def _():
        u_ref[...] = (total[...] + part).astype(BF)


def mlp_back(order, g, a, b, w_down, w, block):
    rows, d = g.shape
    units = a.shape[1]
    steps = units // block
    assert steps > 1
    narrow = pl.BlockSpec((rows, block), lambda j: (0, j))
    return order.call(
        mlp_back_kernel, "mlp_back", 32, (g, a, b, w_down, w, w),
        [
            full((rows, d)),
            narrow,
            narrow,
            pl.BlockSpec((d, block), lambda j: (0, j)),
            pl.BlockSpec((d, block), lambda j: (0, j)),
            pl.BlockSpec((d, block), lambda j: (0, j + steps)),
        ],
        [full((rows, d)), pl.BlockSpec((2, rows, block), lambda j: (0, 0, j))],
        like((rows, d, BF), (2, rows, units, BF)), grid=(steps,),
        scratch=[pltpu.VMEM((rows, d), F32)],
    )


def weight_grad_kernel(x0_ref, x1_ref, d0_ref, d1_ref, o_ref, x_turned):
    rows = x0_ref.shape[0]

    @pl.when(pl.program_id(0) == 0)
    def _():
        for k, ref in enumerate((x0_ref, x1_ref)):
            x_turned[:, k * rows : (k + 1) * rows] = turned(ref[...]).astype(BF)

    o_ref[...] = (
        dot(x_turned[:, :rows], d0_ref[0]) + dot(x_turned[:, rows:], d1_ref[0])
    ).astype(BF)


def weight_grad(order, x0, x1, d0, d1, block):
    rows, d = x0.shape
    parts, _, columns = d0.shape
    steps = columns // block
    narrow = pl.BlockSpec((1, rows, block), lambda j: (j // steps, 0, j % steps))
    return order.call(
        weight_grad_kernel, "weight_grad", 26, (x0, x1, d0, d1),
        [full((rows, d)), full((rows, d)), narrow, narrow],
        [pl.BlockSpec((d, block), lambda j: (0, j))], like((d, parts * columns, BF)),
        grid=(parts * steps,), scratch=[pltpu.VMEM((d, 2 * rows), BF)],
    )[0]


def down_kernel(act_ref, w_ref, o_ref):
    o_ref[...] = dot_nt(act_ref[...], w_ref[...]).astype(BF)


def down(order, act, w_down, block):
    rows, units = act.shape
    d = w_down.shape[0]
    return order.call(
        down_kernel, "down", 14, (act, w_down),
        [full((rows, units)), pl.BlockSpec((block, units), lambda j: (j, 0))],
        [pl.BlockSpec((rows, block), lambda j: (0, j))], like((rows, d, BF)), grid=(d // block,),
    )[0]


def grad_heads_kernel(place_ref, g0_ref, g1_ref, w_ref, o_ref):
    rows = g0_ref.shape[0] // 2
    for k in range(4):
        ref, low = (g0_ref, g1_ref)[k // 2], (k % 2) * rows
        at = pl.multiple_of(place_ref[k] * rows, rows)
        o_ref[:, pl.ds(at, rows)] = dot(ref[low : low + rows], w_ref[...]).T.astype(BF)


def grad_heads(order, places, g0, g1, w_full, depth):
    d, n = w_full.shape[0], 2 * g0.shape[0]
    last = w_full.shape[1] // depth - 1
    return order.call(
        grad_heads_kernel, "grad_heads", 16, (g0, g1, w_full),
        [*wholes((g0, g1)), pl.BlockSpec((d, depth), lambda i, place: (0, last))],
        [full((depth, n))], like((depth, n, BF)), prefetch=(places,),
    )[0]


def grad_x_kernel(place_ref, q_ref, k_ref, v_ref, w_ref, *out_refs):
    rows = out_refs[0].shape[0] // 2
    for k in range(4):
        parts = [columns_of(ref, place_ref[k], rows).astype(F32) for ref in (q_ref, k_ref, v_ref)]
        grads = jnp.concatenate(parts, axis=0).T.astype(BF)
        at = (k % 2) * rows
        out_refs[k // 2][at : at + rows] = dot_nt(grads, w_ref[...]).astype(BF)


def grad_x(order, places, dq, dk, dv, w_full):
    d, n = w_full.shape[0], dq.shape[1]
    return order.call(
        grad_x_kernel, "grad_x", 22, (dq, dk, dv, w_full),
        [*wholes((dq, dk, dv)), full((d, dq.shape[0] + dk.shape[0] + dv.shape[0]))],
        [full((n // 2, d))] * 2, like((n // 2, d, BF), (n // 2, d, BF)), prefetch=(places,),
    )


def tokens_product(place_ref, left_ref, refs):
    rows = refs[0].shape[0] // 2
    total = None
    for k in range(4):
        at = (k % 2) * rows
        part = dot(columns_of(left_ref, place_ref[k], rows), refs[k // 2][at : at + rows])
        total = part if total is None else total + part
    return total


def turned_grad_kernel(count, place_ref, *refs):
    lefts, rights, out = refs[:count], refs[count : count + 2], refs[count + 2]
    at = 0
    for ref in lefts:
        size = ref.shape[0]
        out[:, at : at + size] = tokens_product(place_ref, ref, rights).T.astype(BF)
        at += size


def turned_grad(order, places, lefts, x0, x1, name):
    d, columns = x0.shape[1], sum(left.shape[0] for left in lefts)
    arrays = (*lefts, x0, x1)
    return order.call(
        functools.partial(turned_grad_kernel, len(lefts)), name, 26, arrays, wholes(arrays),
        [full((d, columns))], like((d, columns, BF)), prefetch=(places,),
    )[0]


def row_inverse(values):
    return lax.rsqrt(jnp.mean(values * values, axis=-1, keepdims=True) + EPS)


def first_norm_kernel(a_ref, b_ref, g_ref, o_ref, h_ref, copy_ref):
    def run(ref):
        hidden = ref[...].astype(F32)
        h_ref[...] = ref[...]
        o_ref[...] = (hidden * row_inverse(hidden)).astype(BF)

    near = pl.program_id(0) < pl.num_programs(0) // 2
    pl.when(near)(lambda: run(a_ref))
    pl.when(jnp.logical_not(near))(lambda: run(b_ref))
    pl.when(near)(lambda: copy_ref.__setitem__(..., g_ref[...]))


def first_norm(order, a, b, g):
    rows, d = a.shape
    block = min(128, rows)
    steps = rows // block
    near = pl.BlockSpec((block, d), lambda i: (jnp.minimum(i, steps - 1), 0))
    each = pl.BlockSpec((block, d), lambda i: (i, 0))
    return order.call(
        first_norm_kernel, "first_norm", 10, (a, b, g),
        [near, pl.BlockSpec((block, d), lambda i: (jnp.maximum(i - steps, 0), 0)), near],
        [each, each, near], like((2 * rows, d, BF), (2 * rows, d, BF), (rows, d, BF)),
        grid=(2 * steps,),
    )


def join_kernel(a_ref, b_ref, o_ref):
    near = pl.program_id(0) < pl.num_programs(0) // 2
    pl.when(near)(lambda: o_ref.__setitem__(..., a_ref[...]))
    pl.when(jnp.logical_not(near))(lambda: o_ref.__setitem__(..., b_ref[...]))


def joined(order, kernel, name, a, b, count):
    rows, d = a.shape
    block = min(128, rows)
    steps = rows // block
    return order.call(
        kernel, name, 8, (a, b),
        [
            pl.BlockSpec((block, d), lambda i: (jnp.minimum(i, steps - 1), 0)),
            pl.BlockSpec((block, d), lambda i: (jnp.maximum(i - steps, 0), 0)),
        ],
        [pl.BlockSpec((block, d), lambda i: (i, 0))] * count, like(*[(2 * rows, d, BF)] * count),
        grid=(2 * steps,),
    )


def norm_kernel(h_ref, a_ref, b_ref, o_ref, resid_ref):
    resid = h_ref[...].astype(F32) + (a_ref[...].astype(F32) + b_ref[...].astype(F32))
    resid_ref[...] = resid
    o_ref[...] = (resid * row_inverse(resid)).astype(BF)


def back_through_norm(scaled, values):
    inverse = row_inverse(values)
    inner = jnp.mean(scaled * values, axis=-1, keepdims=True)
    return inverse * scaled - values * (inverse * inverse * inverse * inner)


def norm_back_kernel(a_ref, g_ref, resid_ref, b_ref, o_ref, grad_ref):
    scaled = a_ref[...].astype(F32) + b_ref[...].astype(F32)
    grad = g_ref[...].astype(F32) + back_through_norm(scaled, resid_ref[...])
    grad_ref[...] = grad
    o_ref[...] = grad.astype(BF)


def output_kernel(resid_ref, a_ref, b_ref, c_ref, o_ref):
    total = a_ref[...].astype(F32) + b_ref[...].astype(F32) + c_ref[...].astype(F32)
    o_ref[...] = (resid_ref[...] + total).astype(BF)


def hidden_grad_kernel(grad_ref, h_ref, a_ref, b_ref, c_ref, o_ref):
    scaled = a_ref[...].astype(F32) + b_ref[...].astype(F32) + c_ref[...].astype(F32)
    grad = grad_ref[...] + back_through_norm(scaled, h_ref[...].astype(F32))
    o_ref[...] = grad.astype(BF)


def plus_kernel(a_ref, b_ref, o_ref):
    o_ref[...] = (a_ref[...].astype(F32) + b_ref[...].astype(F32)).astype(BF)


def by_rows(order, kernel, name, rows, arrays, outs, first=None):
    d = arrays[0].shape[1]
    block = min(128, rows)
    first = first or [0] * len(arrays)

    def spec(array, start):
        count = array.shape[0] // block
        skip = start // block
        return pl.BlockSpec((block, d), lambda i: (lax.rem(i + skip, count), 0))

    return order.call(
        kernel, name, 12, arrays, [spec(a, start) for a, start in zip(arrays, first)],
        [pl.BlockSpec((block, d), lambda i: (i, 0))] * len(outs),
        like(*[(rows, d, dtype) for dtype in outs]), grid=(rows // block,),
    )


def add_kernel(index_ref, left_chunk, right_chunk, left_ref, right_ref, to_right, to_left):
    columns, cut = to_right.shape[1], left_ref.shape[1]
    to_right[:, :cut] = (left_chunk[:, :cut].astype(F32) + left_ref[...].astype(F32)).astype(BF)
    if cut < columns:
        to_right[:, cut:] = left_chunk[:, cut:]
    cut = columns - right_ref.shape[1]
    to_left[:, cut:] = (right_chunk[:, cut:].astype(F32) + right_ref[...].astype(F32)).astype(BF)
    if cut > 0:
        to_left[:, :cut] = right_chunk[:, :cut]


def add_chunks(order, whole, rows, start, width, first, second, from_left, from_right):
    chunk = lambda k: pl.BlockSpec((rows, width), lambda i, index: (index[k], start // width))
    return order.call(
        add_kernel, "add_chunks", 10, (whole, whole, from_left, from_right),
        [chunk(0), chunk(1), *wholes((from_left, from_right))], [full((rows, width))] * 2,
        like((rows, width, BF), (rows, width, BF)),
        prefetch=(jnp.stack([first, second]).astype(jnp.int32),),
    )


def arrived_sum(chunk_ref, lefts, rights):
    left = jnp.concatenate([ref[...].astype(F32) for ref in lefts], axis=1)
    right = jnp.concatenate([ref[...].astype(F32) for ref in rights], axis=1)
    return chunk_ref[...].astype(F32) + left + right


def finish_kernel(parts, widths, index_ref, chunk_ref, *refs):
    grad = arrived_sum(chunk_ref, refs[:parts], refs[parts : 2 * parts])
    gain_ref, refs = refs[2 * parts], refs[2 * parts + 1 :]
    weights, outs = refs[: len(widths)], refs[len(widths) :]
    gain, total, at = column(gain_ref[...]), None, 0
    for k, width in enumerate(widths):
        part = grad[:, at : at + width]
        term = jnp.sum(part * weights[k][...].astype(F32), axis=1, keepdims=True)
        total = term if total is None else total + term
        outs[k][...] = part * gain
        at += width
    outs[-1][...] = total


def finish(order, whole, rows, own, lefts, rights, gain, weights):
    columns = whole.shape[1]
    widths = tuple(w.shape[1] for w in weights)
    return order.call(
        functools.partial(finish_kernel, len(lefts), widths), "finish", 16,
        (whole, *lefts, *rights, gain, *weights),
        [
            pl.BlockSpec((rows, columns), lambda i, index: (index[0], 0)),
            *wholes((*lefts, *rights, gain, *weights)),
        ],
        [*wholes(weights), full((rows, 1))],
        like(*[(*w.shape, F32) for w in weights], (rows, 1, F32)),
        prefetch=(own[None].astype(jnp.int32),),
    )


def finish_plain_kernel(parts, index_ref, chunk_ref, *refs):
    refs[-1][...] = arrived_sum(chunk_ref, refs[:parts], refs[parts : 2 * parts])


def finish_plain(order, whole, rows, own, lefts, rights):
    columns = whole.shape[1]
    return order.call(
        functools.partial(finish_plain_kernel, len(lefts)), "finish_plain", 12,
        (whole, *lefts, *rights),
        [
            pl.BlockSpec((rows, columns), lambda i, index: (index[0], 0)),
            *wholes((*lefts, *rights)),
        ],
        [full((rows, columns))], like((rows, columns, F32)),
        prefetch=(own[None].astype(jnp.int32),),
    )[0]


class Ring:
    def __init__(self, count):
        self.count = count
        self.half = count // 2
        order = [2 * k if k < self.half else 2 * (count - 1 - k) + 1 for k in range(count)]
        self.right = [(order[k], order[(k + 1) % count]) for k in range(count)]
        self.left = [(b, a) for a, b in self.right]
        me = lax.axis_index("dp")
        self.place = jnp.where(me % 2 == 0, me // 2, count - 1 - me // 2)

    def index(self, offset):
        place = (self.place + offset + self.count) % self.count
        return jnp.where(place < self.half, 2 * place, 2 * (self.count - 1 - place) + 1)

    def go_right(self, value):
        return lax.ppermute(value, "dp", self.right)

    def go_left(self, value):
        return lax.ppermute(value, "dp", self.left)


def cut_of(columns):
    return max(128, (columns // 2 + 127) // 128 * 128)


class Kept:
    def __init__(self, order, ring, parts, whole):
        self.order, self.ring, self.whole = order, ring, whole
        self.parts, self.rows = parts, sum(part.shape[0] for part in parts)
        self.waiting = []

    def put(self, skip, offsets, firsts, pieces, last_part):
        at = [self.ring.index(offset) * self.rows + skip for offset in offsets]
        self.waiting += zip(at, firsts, pieces)
        if not last_part:
            return pieces
        places, firsts, pieces = zip(*self.waiting)
        self.waiting = []
        pieces, self.whole = keep(self.order, places, firsts, pieces, self.whole)
        return pieces[-2:]


class Gather:
    def __init__(self, kept, which, start=lambda value: value):
        self.kept, self.order, self.ring, self.rounds = kept, kept.order, kept.ring, 1
        self.skip = kept.parts[0].shape[0] * which
        self.last_part = which == len(kept.parts) - 1
        shard = start(kept.parts[which])
        self.cut = cut_of(shard.shape[1])
        self.flying = self.ring.go_right(shard), self.ring.go_left(shard)

    def wait(self):
        arrived = self.order.wait(*self.flying)
        last = self.rounds == self.ring.half
        firsts = (0, self.cut if last else 0)
        self.rounds += 1
        if not last and not self.last_part:
            arrived = relay(self.order, *arrived)
        arrived = self.kept.put(
            self.skip, (1 - self.rounds, self.rounds - 1), firsts, arrived, self.last_part
        )
        if self.rounds == self.ring.half:
            arrived = halves(self.order, *arrived, self.cut)
        if not last:
            self.flying = self.ring.go_right(arrived[0]), self.ring.go_left(arrived[1])

    def middle(self):
        while self.rounds < self.ring.half - 3:
            self.wait()


class Scatter:
    def __init__(self, order, ring, whole, first, width):
        self.order, self.ring, self.whole = order, ring, whole
        self.first, self.width = first, width
        self.rows = whole.shape[0] // ring.count
        self.steps = ring.half - 1
        right, left = far_chunk(
            order, whole, self.rows, first, width, ring.index(ring.half), cut_of(width)
        )
        self.flying = ring.go_right(right), ring.go_left(left)

    def wait(self):
        step = self.steps
        right, left = add_chunks(
            self.order, self.whole, self.rows, self.first, self.width, self.ring.index(step),
            self.ring.index(-step), *self.order.wait(*self.flying),
        )
        self.steps -= 1
        self.flying = self.ring.go_right(right), self.ring.go_left(left)

    def middle(self):
        while self.steps > 3:
            self.wait()

    def last(self):
        while self.steps:
            self.wait()
        return self.order.wait(*self.flying)


def scaled_sum(sums, gain, weights):
    arrived = [part.last() for part in sums]
    part = sums[0]
    return finish(
        part.order, part.whole, part.rows, part.ring.index(0), [a for a, _ in arrived],
        [b for _, b in arrived], gain, weights,
    )


def plain_sum(sums):
    arrived = [part.last() for part in sums]
    part = sums[0]
    return finish_plain(
        part.order, part.whole, part.rows, part.ring.index(0), [a for a, _ in arrived],
        [b for _, b in arrived],
    )


def swap_core(value):
    return lax.ppermute(value, "tensor", CORE_PAIRS)


def swap_x(value):
    return lax.ppermute(value, "tensor", X_PAIRS)


def plus(order, left_side, right_side, rows, first=0):
    arrays = (left_side, right_side)
    return by_rows(order, plus_kernel, "plus", rows, arrays, (BF,), (first, first))[0]


def rope_tables(segment):
    places = jnp.arange(segment.shape[0], dtype=jnp.int32)
    previous = jnp.concatenate([segment[:1] - 1, segment[:-1]])
    opening = lax.cummax(jnp.where(segment != previous, places, 0), axis=0)
    position = (places - opening).astype(F32)
    inverse = jnp.exp(-(2.0 * jnp.arange(HALF, dtype=F32) / HD) * math.log(THETA))
    angle = inverse[:, None] * position[None, :]
    return jnp.cos(angle), jnp.sin(angle), opening[None, :]


def per_device(
    dp_count,
    hidden_in,
    segments,
    attn_gain,
    w_query,
    w_key,
    w_value,
    w_out,
    mlp_gain,
    w_gate,
    w_up,
    w_down,
    cotangent,
):
    ring = Ring(dp_count)
    device = lax.axis_index("tensor").astype(jnp.int32)
    places = jnp.stack([device, device ^ 2, device ^ 1, device ^ 3])
    rows = hidden_in.shape[0]
    query_columns, key_columns = w_query.shape[1], w_key.shape[1]
    query_heads, key_heads = query_columns // HD, key_columns // HD
    units = w_gate.shape[1]
    block = units // 2
    gain_one, gain_two = attn_gain[None], mlp_gain[None]
    order = Order()

    def go(value):
        return relay(order, value)[0]

    *parts, whole = make_shard(
        order, ring, gain_one, [w_query, w_key, w_value], [w_out.T], "attn_shard", 58, True
    )
    attn = Kept(order, ring, parts, whole)
    attn_top = Gather(attn, 0)
    attn_bottom = Gather(attn, 1)
    hidden_across = swap_x(hidden_in)
    attn_top.middle()
    attn_bottom.middle()
    attn_top.wait()
    attn_bottom.wait()
    *parts, whole = make_shard(
        order, ring, gain_two, [w_gate, w_up], [], "gate_up_shard", 14, True
    )
    gate_up_kept = Kept(order, ring, parts, whole)
    attn_top.wait()
    order.wait(hidden_across)
    normed_mine, hidden_mine, grads_own = first_norm(order, hidden_in, hidden_across, cotangent)
    attn_bottom.wait()
    normed_mine = go(normed_mine)
    normed_other = swap_core(normed_mine)
    grads_across = swap_x(grads_own)
    attn_top.wait()
    order.wait(normed_other)
    attn_bottom.wait()
    *parts, whole = make_shard(order, ring, gain_two, [], [w_down.T], "down_shard", 8, False)
    down_kept = Kept(order, ring, parts, whole)
    attn_top.wait()
    attn_bottom.wait()
    gate_up_top = Gather(gate_up_kept, 0, go)
    gate_up_bottom = Gather(gate_up_kept, 1, go)
    full_attn = attn.whole
    cosine, sine, start = order.wait(*rope_tables(segments))
    qkv = project(
        order, places, normed_mine, normed_other, full_attn, cosine, sine, query_heads, key_heads
    )
    gate_up_top.middle()
    gate_up_bottom.middle()
    order.wait(grads_across)
    grads_mine = joined(order, join_kernel, "join", cotangent, grads_across, 1)[0]
    gate_up_top.wait()
    grads_mine = go(grads_mine)
    grads_other = swap_core(grads_mine)
    heads_out, log_total = attend(order, qkv, start, query_heads, key_heads, rows)
    part_mine, part_other = branch(order, places, heads_out, full_attn)
    order.wait(grads_other)
    gate_up_bottom.wait()
    part_core = swap_core(go(part_other))
    order.wait(part_core)
    chip = plus(order, part_mine, part_core, 2 * rows)
    across = swap_x(chip)
    gate_up_top.wait()
    gate_up_bottom.wait()
    gate_up_top.wait()
    gate_up_bottom.wait()
    gate_up_top.wait()
    down_ring = Gather(down_kept, 0, go)
    gate_up_bottom.wait()
    full_gate_up = gate_up_kept.whole
    order.wait(across)
    normed_two_mine, resid = by_rows(
        order, norm_kernel, "norm", 2 * rows, (hidden_mine, chip, across), (BF, F32), (0, 0, rows)
    )
    down_ring.middle()
    normed_two_mine = go(normed_two_mine)
    normed_two_other = swap_core(normed_two_mine)
    mlp_mine = gate_up(order, normed_two_mine, full_gate_up, block)
    order.wait(normed_two_other)
    down_ring.wait()
    mlp_other = gate_up(order, normed_two_other, full_gate_up, block)
    down_ring.wait()
    down_grad = weight_grad(
        order, grads_mine, grads_other, mlp_mine[0][None], mlp_other[0][None], block
    )
    down_ring.wait()
    down_sum = Scatter(order, ring, down_grad, 0, units)
    down_ring.wait()
    full_down = down_kept.whole

    scaled_mine, grad_mine = mlp_back(
        order, grads_mine, mlp_mine[1], mlp_mine[2], full_down, full_gate_up, block
    )
    down_sum.middle()
    down_sum.wait()
    scaled_other, grad_other = mlp_back(
        order, grads_other, mlp_other[1], mlp_other[2], full_down, full_gate_up, block
    )
    down_sum.wait()
    scaled_core = swap_core(go(scaled_other))
    down_mine = down(order, mlp_mine[0], full_down, 512)
    order.wait(scaled_core)
    chip = plus(order, scaled_mine, scaled_core, 2 * rows)
    across = swap_x(chip)
    gate_up_grad = weight_grad(
        order, normed_two_mine, normed_two_other, grad_mine, grad_other, block
    )
    down_sum.wait()
    gate_sum = Scatter(order, ring, gate_up_grad, 0, units)
    down_other = down(order, mlp_other[0], full_down, 512)
    grad_down_w = plain_sum([down_sum])
    up_sum = Scatter(order, ring, gate_up_grad, units, units)
    gate_sum.middle()
    up_sum.middle()
    gate_sum.wait()
    order.wait(across)
    branch_mine, grad_resid = by_rows(
        order, norm_back_kernel, "norm_back", 2 * rows, (chip, grads_mine, resid, across),
        (BF, F32), (0, 0, 0, rows),
    )
    up_sum.wait()
    branch_mine = go(branch_mine)
    branch_other = swap_core(branch_mine)
    order.wait(branch_other)
    grad_out = grad_heads(order, places, branch_mine, branch_other, full_attn, query_columns)
    gate_sum.wait()
    down_core = swap_core(go(down_other))
    dq, dk, dv = attend_back(
        order, qkv, grad_out, heads_out, log_total, start, cosine, sine, query_heads, key_heads, rows
    )
    order.wait(down_core)
    up_sum.wait()
    down_theirs = swap_x(plus(order, down_mine, down_core, rows, rows))
    scaled_mine, scaled_other = grad_x(order, places, dq, dk, dv, full_attn)
    gate_sum.wait()
    scaled_core = swap_core(go(scaled_other))
    out_grad = turned_grad(order, places, [heads_out], branch_mine, branch_other, "out_grad")
    order.wait(scaled_core)
    up_sum.wait()
    scaled_theirs = swap_x(plus(order, scaled_mine, scaled_core, rows, rows))
    qkv_grad = turned_grad(order, places, [dq, dk, dv], normed_mine, normed_other, "qkv_grad")
    order.wait(*gate_sum.flying)
    qkv_sum = Scatter(order, ring, qkv_grad, 0, 2 * query_columns)
    order.wait(down_theirs)
    output = by_rows(
        order, output_kernel, "output", rows, (resid, down_mine, down_core, down_theirs), (BF,)
    )[0]
    order.wait(*up_sum.flying)
    out_sum = Scatter(order, ring, out_grad, 0, query_columns)
    qkv_sum.middle()
    out_sum.middle()
    qkv_sum.wait()
    grad_gate_w, grad_up_w, gain_two_part = scaled_sum([gate_sum, up_sum], gain_two, [w_gate, w_up])
    out_sum.wait()
    qkv_sum.wait()
    order.wait(scaled_theirs)
    hidden_grad = by_rows(
        order, hidden_grad_kernel, "hidden_grad", rows,
        (grad_resid, hidden_in, scaled_mine, scaled_core, scaled_theirs), (BF,),
    )[0]
    out_sum.wait()
    qkv_sum.wait()
    out_sum.wait()
    grad_q_w, grad_k_w, grad_v_w, gain_one_part = scaled_sum(
        [qkv_sum], gain_one, [w_query, w_key, w_value]
    )
    gains = lax.psum(jnp.concatenate([gain_one_part, gain_two_part], axis=1), "tensor")
    grad_out_w = plain_sum([out_sum])
    return (
        output,
        hidden_grad,
        gains[:, 0],
        grad_q_w,
        grad_k_w,
        grad_v_w,
        grad_out_w.T,
        gains[:, 1],
        grad_gate_w,
        grad_up_w,
        grad_down_w.T,
    )


def solution(mesh):
    tokens, split = P(("dp", "tensor"), None), P("dp", "tensor")
    in_specs = (
        tokens, P("dp"), P("dp"), split, split, split, P("tensor", "dp"),
        P("dp"), split, split, P("tensor", "dp"), tokens,
    )
    out_specs = (
        tokens, tokens, P("dp"), split, split, split, P("tensor", "dp"),
        P("dp"), split, split, P("tensor", "dp"),
    )
    body = functools.partial(per_device, mesh.shape["dp"])
    return jax.shard_map(body, mesh=mesh, in_specs=in_specs, out_specs=out_specs, check_vma=False)
```

```python
import functools
import math
import types

import jax
import jax.numpy as jnp
from jax import lax
from jax.experimental import pallas as pl
from jax.experimental.pallas import tpu as pltpu
from jax.sharding import PartitionSpec as P

HD = 96
HALF = HD // 2
DOCUMENTS = 5
EPS = 1e-05
NEG = -1e30
THETA = 100000.0
SCALE = HD ** (-0.5)
LOG2E = math.log2(math.e)
BF = jnp.bfloat16
F32 = jnp.float32
MIB = 1024 * 1024

CORE_PAIRS = [(0, 1), (1, 0), (2, 3), (3, 2)]
X_PAIRS = [(0, 2), (2, 0), (1, 3), (3, 1)]


def dot(left_side, right_side):
    return jnp.dot(left_side, right_side, preferred_element_type=F32)


def dot_nt(left_side, right_side):
    return lax.dot_general(
        left_side, right_side, (((1,), (1,)), ((), ())), preferred_element_type=F32
    )


def turned(value):
    return value.astype(F32).T


class Order:
    def __init__(self):
        self.waited, self.token = [], None

    def wait(self, *values):
        self.waited += values
        return values[0] if len(values) == 1 else values

    def call(
        self, body, name, mib, args, in_specs, out_specs, out_shape, grid=(1,), scratch=(),
        prefetch=(), aliases=None, far=(), near=(), far_out=(), near_out=(),
    ):
        seen = [a for a in self.waited if not any(a is b for b in args)]
        if self.token is not None:
            seen.append(pltpu.with_memory_space_constraint(self.token, pltpu.HBM))
        first, extra, count = len(prefetch) + len(args), len(seen), len(out_shape)
        args = list(args)
        for k in far:
            args[k] = pltpu.with_memory_space_constraint(args[k], pltpu.HBM)
        for k in near:
            args[k] = pltpu.with_memory_space_constraint(args[k], pltpu.VMEM)
        out_shape = list(out_shape)
        for k in far_out:
            out_shape[k] = pltpu.HBM(out_shape[k].shape, out_shape[k].dtype)
        for k in near_out:
            out_shape[k] = pltpu.VMEM(out_shape[k].shape, out_shape[k].dtype)

        def kernel(*refs):
            outs = refs[first + extra :]
            body(*refs[:first], *outs[:count], *outs[count + 1 :])

        *out, self.token = pl.pallas_call(
            kernel,
            grid_spec=pltpu.PrefetchScalarGridSpec(
                num_scalar_prefetch=len(prefetch),
                grid=grid,
                in_specs=[*in_specs, *[ANY] * extra],
                out_specs=[*out_specs, ANY],
                scratch_shapes=scratch,
            ),
            out_shape=[*out_shape, pltpu.HBM((8, 128), F32)],
            input_output_aliases=aliases or {},
            compiler_params=pltpu.CompilerParams(vmem_limit_bytes=mib * MIB),
            cost_estimate=pl.CostEstimate(flops=0, bytes_accessed=0, transcendentals=0),
            name=name,
        )(*prefetch, *args, *seen)
        self.waited = []
        return out


def full(shape):
    return pl.BlockSpec(tuple(shape), lambda *_: (0,) * len(shape))


def wholes(arrays):
    return [full(a.shape) for a in arrays]


def like(*shapes):
    return [jax.ShapeDtypeStruct(shape, dtype) for *shape, dtype in shapes]


ANY = pl.BlockSpec(memory_space=pl.ANY)
HBM = pl.BlockSpec(memory_space=pltpu.HBM)
VMEM = pl.BlockSpec(memory_space=pltpu.VMEM)


def column(row):
    return jnp.broadcast_to(row.astype(F32)[None], (8, row.shape[0])).T[:, :1]


def put(outs, first, value):
    top, width = outs[0].shape[0], value.shape[1]
    outs[0][:, first : first + width] = value[:top]
    if len(outs) > 1:
        outs[1][:, first : first + width] = value[top:]


def shard_kernel(scaled, plain, gain_ref, *refs):
    gain, first = column(gain_ref[...]), 0
    inputs, outs = refs[: scaled + plain], refs[scaled + plain :]
    for k, ref in enumerate(inputs):
        value = (ref[...].astype(F32) * gain).astype(BF) if k < scaled else ref[...]
        put(outs, first, value)
        first += ref.shape[1]


def top_of(rows):
    return (rows // 2 + 15) // 16 * 16


def make_shard(order, gain, scaled, plain, name, mib, split):
    rows = (*scaled, *plain)[0].shape[0]
    columns = sum(w.shape[1] for w in (*scaled, *plain))
    top = top_of(rows) if split else rows
    shapes = [(count, columns) for count in (top, rows - top) if count]
    return order.call(
        functools.partial(shard_kernel, len(scaled), len(plain)), name, mib,
        (gain, *scaled, *plain), wholes((gain, *scaled, *plain)), [full(shape) for shape in shapes],
        like(*[(*shape, BF) for shape in shapes]), far=range(1, 1 + len(scaled) + len(plain)),
    )


def relay_kernel(*refs):
    pass


def relay(order, *values):
    count = len(values)
    return order.call(
        relay_kernel, "relay", 2, values, [ANY] * count, [ANY] * count,
        like(*[(*value.shape, value.dtype) for value in values]),
        aliases={k: k for k in range(count)},
    )


def assemble_kernel(spans, place_ref, *refs):
    pieces, whole, sems = refs[: len(spans)], refs[len(spans)], refs[len(spans) + 1]
    copies = []
    for k, (first, width) in enumerate(spans):
        at = pl.multiple_of(place_ref[k], 16)
        where = whole.at[pl.ds(at, pieces[k].shape[0]), pl.ds(first, width)]
        copies.append(pltpu.make_async_copy(pieces[k], where, sems.at[k]))
    for copy in copies:
        copy.start()
    for copy in copies:
        copy.wait()


def assemble(order, rows, columns, places, firsts, pieces):
    count = len(pieces)
    spans = tuple((first, piece.shape[1]) for first, piece in zip(firsts, pieces))
    return order.call(
        functools.partial(assemble_kernel, spans), "assemble", 2, pieces, [ANY] * count, [VMEM],
        like((rows, columns, BF)), scratch=[pltpu.SemaphoreType.DMA((count,))],
        prefetch=(jnp.stack(places).astype(jnp.int32),), far=range(count), near_out=(0,),
    )[0]


def halves_kernel(cut, a_ref, b_ref, c_ref, d_ref):
    c_ref[...] = a_ref[:, :cut]
    d_ref[...] = b_ref[:, cut:]


def halves(order, right, left, cut):
    rows, columns = right.shape
    shapes = (rows, cut), (rows, columns - cut)
    return order.call(
        functools.partial(halves_kernel, cut), "halves", 6, (right, left), wholes((right, left)),
        [full(shape) for shape in shapes], like(*[(*shape, BF) for shape in shapes]),
    )


def far_kernel(cut, index_ref, chunk_ref, c_ref, d_ref):
    c_ref[...] = chunk_ref[:, :cut]
    d_ref[...] = chunk_ref[:, cut:]


def far_chunk(order, whole, rows, first, width, index, cut):
    shapes = (rows, cut), (rows, width - cut)
    return order.call(
        functools.partial(far_kernel, cut), "far_chunk", 8, (whole,),
        [pl.BlockSpec((rows, width), lambda i, index: (index[0], first // width))],
        [full(shape) for shape in shapes], like(*[(*shape, BF) for shape in shapes]),
        prefetch=(index[None].astype(jnp.int32),),
    )


def tables_kernel(segment_ref, c_ref, s_ref, opening_ref):
    segment = segment_ref[...]
    opening = jnp.zeros_like(segment)
    for number in range(DOCUMENTS - 1):
        count = jnp.sum((segment == number).astype(jnp.int32), axis=1, keepdims=True)
        opening += jnp.where(segment > number, count, 0)
    position = (lax.broadcasted_iota(jnp.int32, segment.shape, 1) - opening).astype(F32)
    place = lax.broadcasted_iota(jnp.int32, c_ref.shape, 0).astype(F32)
    angle = jnp.exp(-(2.0 * place / HD) * math.log(THETA)) * position
    c_ref[...] = jnp.cos(angle)
    s_ref[...] = jnp.sin(angle)
    opening_ref[...] = opening


def rope_tables(order, segments):
    n = segments.shape[0]
    shapes = (HALF, n), (HALF, n), (1, n)
    return order.call(
        tables_kernel, "rope_tables", 8, (segments[None],), [full((1, n))],
        [full(shape) for shape in shapes],
        like((HALF, n, F32), (HALF, n, F32), (1, n, jnp.int32)),
    )


def rope_rows(values, cosine, sine):
    first, second = values[:HALF], values[HALF:]
    return first * cosine - second * sine, second * cosine + first * sine


def project_kernel(query_heads, key_heads, place_ref, x0_ref, x1_ref, w_ref, c_ref, s_ref, o_ref):
    def run(x_ref):
        turned_heads = dot(x_ref[...], w_ref[...]).T
        cosine, sine = c_ref[...], s_ref[...]
        for h in range(query_heads + key_heads):
            first, second = rope_rows(turned_heads[h * HD : (h + 1) * HD], cosine, sine)
            if h < query_heads:
                first, second = first * (SCALE * LOG2E), second * (SCALE * LOG2E)
            o_ref[h * HD : h * HD + HALF, :] = first.astype(BF)
            o_ref[h * HD + HALF : (h + 1) * HD, :] = second.astype(BF)
        done = (query_heads + key_heads) * HD
        o_ref[done:, :] = turned_heads[done:].astype(BF)

    pl.when(pl.program_id(0) < 2)(lambda: run(x0_ref))
    pl.when(pl.program_id(0) >= 2)(lambda: run(x1_ref))


def project(order, places, x0, x1, w, cosine, sine, query_heads, key_heads):
    block, d = x0.shape[0] // 2, x0.shape[1]
    columns = (query_heads + 2 * key_heads) * HD
    table = pl.BlockSpec((HALF, block), lambda i, place: (0, place[i]))
    return order.call(
        functools.partial(project_kernel, query_heads, key_heads), "project", 18,
        (x0, x1, w, cosine, sine),
        [
            pl.BlockSpec((block, d), lambda i, place: (jnp.minimum(i, 1), 0)),
            pl.BlockSpec((block, d), lambda i, place: (jnp.maximum(i - 2, 0), 0)),
            full((d, columns)),
            table,
            table,
        ],
        [pl.BlockSpec((columns, block), lambda i, place: (0, place[i]))],
        like((columns, 4 * block, BF)), grid=(4,), prefetch=(places,),
    )[0]


def side(ref, low, high):
    return jnp.concatenate(
        [ref[h * HD : (h + 1) * HD, low:high] for h in range(ref.shape[0] // HD)], axis=1
    )


def attend_kernel(block, q_ref, k_ref, v_ref, start_ref, o_ref, l_ref):
    n, group = q_ref.shape[1], q_ref.shape[0] // HD
    keys = turned(k_ref[...]).astype(BF)
    row = lax.broadcasted_iota(jnp.int32, (block, group * block), 0)
    column = lax.broadcasted_iota(jnp.int32, (block, group * block), 1) % block
    for i in range(n // block):
        low, high = i * block, (i + 1) * block
        start = jnp.concatenate([start_ref[:, low:high]] * group, axis=1)
        scores = dot(keys[:high], side(q_ref, low, high))
        at = lax.broadcasted_iota(jnp.int32, (high, group * block), 0)
        scores = jnp.where(at >= start, scores, NEG)
        near = jnp.where(row <= column, scores[low:], NEG)
        top = jnp.max(near, axis=0, keepdims=True)
        if i:
            top = jnp.maximum(top, jnp.max(scores[:low], axis=0, keepdims=True))
        near = jnp.exp2(near - top)
        total = jnp.sum(near, axis=0, keepdims=True)
        out = dot(v_ref[:, low:high], near.astype(BF))
        if i:
            far = jnp.exp2(scores[:low] - top)
            total = total + jnp.sum(far, axis=0, keepdims=True)
            out = out + dot(v_ref[:, :low], far.astype(BF))
        out = out * (1.0 / total)
        log_total = top + jnp.log2(total)
        for h in range(group):
            part = slice(h * block, (h + 1) * block)
            o_ref[h * HD : (h + 1) * HD, low:high] = out[:, part].astype(BF)
            l_ref[0, h : h + 1, low:high] = log_total[:, part]


def attend(order, qkv, start, query_heads, key_heads, block):
    n, group = qkv.shape[1], query_heads // key_heads
    return order.call(
        functools.partial(attend_kernel, block), "attend", 20, (qkv, qkv, qkv, start),
        [
            pl.BlockSpec((group * HD, n), lambda i: (i, 0)),
            pl.BlockSpec((HD, n), lambda i: (query_heads + i, 0)),
            pl.BlockSpec((HD, n), lambda i: (query_heads + key_heads + i, 0)),
            full((1, n)),
        ],
        [
            pl.BlockSpec((group * HD, n), lambda i: (i, 0)),
            pl.BlockSpec((1, group, n), lambda i: (i, 0, 0)),
        ],
        like((query_heads * HD, n, BF), (key_heads, group, n, F32)), grid=(key_heads,),
    )


def attend_back_kernel(
    block, q_ref, k_ref, v_ref, g_ref, h_ref, l_ref, start_ref, c_ref, s_ref,
    dq_ref, dk_ref, dv_ref, dk_sum, dv_sum,
):
    n, group = q_ref.shape[1], q_ref.shape[0] // HD
    keys = turned(k_ref[...]).astype(BF)
    values = turned(v_ref[...]).astype(BF)
    dk_sum[...] = jnp.zeros_like(dk_sum)
    dv_sum[...] = jnp.zeros_like(dv_sum)
    for i in range(n // block):
        low, high = i * block, (i + 1) * block
        queries, grads = side(q_ref, low, high), side(g_ref, low, high)
        outs = side(h_ref, low, high)
        query_rows, grad_rows = turned(queries).astype(BF), turned(grads).astype(BF)
        inner = jnp.sum(grads.astype(F32) * outs.astype(F32), axis=0, keepdims=True)
        log_total = jnp.concatenate([l_ref[0, h : h + 1, low:high] for h in range(group)], axis=1)
        start = jnp.concatenate([start_ref[:, low:high]] * group, axis=1)
        dq = jnp.zeros((HD, group * block), F32)
        for first, last in ([(0, low)] if i else []) + [(low, high)]:
            scores = dot(keys[first:last], queries)
            at = lax.broadcasted_iota(jnp.int32, scores.shape, 0) + first
            allowed = at >= start
            if first == low:
                column = lax.broadcasted_iota(jnp.int32, scores.shape, 1) % block + low
                allowed = allowed & (at <= column)
            probs = jnp.exp2(jnp.where(allowed, scores - log_total, NEG))
            dp = dot(values[first:last], grads)
            ds = (probs * (dp - inner)).astype(BF)
            dv_sum[first:last, :] += dot(probs.astype(BF), grad_rows)
            dk_sum[first:last, :] += dot(ds, query_rows)
            dq = dq + dot(k_ref[:, first:last], ds)
        dq = dq * SCALE
        cosine, sine = c_ref[:, low:high], s_ref[:, low:high]
        for h in range(group):
            top, bottom = rope_rows(dq[:, h * block : (h + 1) * block], cosine, -sine)
            dq_ref[h * HD : h * HD + HALF, low:high] = top.astype(BF)
            dq_ref[h * HD + HALF : (h + 1) * HD, low:high] = bottom.astype(BF)
    top, bottom = rope_rows(dk_sum[...].T * (1.0 / LOG2E), c_ref[...], -s_ref[...])
    dk_ref[:HALF, :] = top.astype(BF)
    dk_ref[HALF:, :] = bottom.astype(BF)
    dv_ref[...] = dv_sum[...].T.astype(BF)


def attend_back(order, qkv, grads, heads_out, log_total, start, cosine, sine, query_heads, key_heads, block):
    n, group = qkv.shape[1], query_heads // key_heads
    wide = pl.BlockSpec((group * HD, n), lambda i: (i, 0))
    narrow = pl.BlockSpec((HD, n), lambda i: (i, 0))
    return order.call(
        functools.partial(attend_back_kernel, block), "attend_back", 26,
        (qkv, qkv, qkv, grads, heads_out, log_total, start, cosine, sine),
        [
            wide,
            pl.BlockSpec((HD, n), lambda i: (query_heads + i, 0)),
            pl.BlockSpec((HD, n), lambda i: (query_heads + key_heads + i, 0)),
            wide,
            wide,
            pl.BlockSpec((1, group, n), lambda i: (i, 0, 0)),
            full((1, n)),
            full((HALF, n)),
            full((HALF, n)),
        ],
        [wide, narrow, narrow],
        like((query_heads * HD, n, BF), (key_heads * HD, n, BF), (key_heads * HD, n, BF)),
        grid=(key_heads,), scratch=[pltpu.VMEM((n, HD), F32), pltpu.VMEM((n, HD), F32)],
    )


def columns_of(ref, place, block):
    return ref[:, pl.ds(pl.multiple_of(place * block, block), block)]


def branch_kernel(place_ref, h_ref, w_ref, *out_refs):
    rows = out_refs[0].shape[0] // 2
    for k in range(4):
        heads = turned(columns_of(h_ref, place_ref[k], rows)).astype(BF)
        at = (k % 2) * rows
        out_refs[k // 2][at : at + rows] = dot_nt(heads, w_ref[...]).astype(BF)


def branch(order, places, heads_out, w_full):
    (depth, n), d = heads_out.shape, w_full.shape[0]
    last = w_full.shape[1] // depth - 1
    return order.call(
        branch_kernel, "branch", 18, (heads_out, w_full),
        [full((depth, n)), pl.BlockSpec((d, depth), lambda i, place: (0, last))],
        [full((n // 2, d))] * 2, like((n // 2, d, BF), (n // 2, d, BF)), prefetch=(places,),
    )


def gate_up_kernel(x_ref, wg_ref, wu_ref, act_ref, a_ref, b_ref):
    gate, up = dot(x_ref[...], wg_ref[...]), dot(x_ref[...], wu_ref[...])
    sigmoid = 1.0 / (1.0 + jnp.exp(-gate))
    silu = gate * sigmoid
    act_ref[...] = (silu * up).astype(BF)
    a_ref[...] = (up * sigmoid * (1.0 + gate * (1.0 - sigmoid))).astype(BF)
    b_ref[...] = silu.astype(BF)


def gate_up(order, x, w, block):
    rows, d = x.shape
    units = w.shape[1] // 2
    steps = units // block
    return order.call(
        gate_up_kernel, "gate_up", 24, (x, w, w),
        [
            full((rows, d)),
            pl.BlockSpec((d, block), lambda j: (0, j)),
            pl.BlockSpec((d, block), lambda j: (0, j + steps)),
        ],
        [pl.BlockSpec((rows, block), lambda j: (0, j))] * 3, like(*[(rows, units, BF)] * 3),
        grid=(steps,),
    )


def mlp_back_kernel(g_ref, a_ref, b_ref, wd_ref, wg_ref, wu_ref, u_ref, d_ref, total):
    step, last = pl.program_id(0), pl.num_programs(0) - 1
    grad_act = dot(g_ref[...], wd_ref[...])
    d_ref[0] = (grad_act * a_ref[...].astype(F32)).astype(BF)
    d_ref[1] = (grad_act * b_ref[...].astype(F32)).astype(BF)
    part = dot_nt(d_ref[0], wg_ref[...]) + dot_nt(d_ref[1], wu_ref[...])

    @pl.when(step == 0)
    def _():
        total[...] = part

    @pl.when((step > 0) & (step < last))
    def _():
        total[...] += part

    @pl.when(step == last)
    def _():
        u_ref[...] = (total[...] + part).astype(BF)


def mlp_back(order, g, a, b, w_down, w, block):
    rows, d = g.shape
    units = a.shape[1]
    steps = units // block
    assert steps > 1
    narrow = pl.BlockSpec((rows, block), lambda j: (0, j))
    return order.call(
        mlp_back_kernel, "mlp_back", 32, (g, a, b, w_down, w, w),
        [
            full((rows, d)),
            narrow,
            narrow,
            pl.BlockSpec((d, block), lambda j: (0, j)),
            pl.BlockSpec((d, block), lambda j: (0, j)),
            pl.BlockSpec((d, block), lambda j: (0, j + steps)),
        ],
        [full((rows, d)), pl.BlockSpec((2, rows, block), lambda j: (0, 0, j))],
        like((rows, d, BF), (2, rows, units, BF)), grid=(steps,),
        scratch=[pltpu.VMEM((rows, d), F32)],
    )


def weight_grad_kernel(x0_ref, x1_ref, d0_ref, d1_ref, o_ref, x_turned):
    rows = x0_ref.shape[0]

    @pl.when(pl.program_id(0) == 0)
    def _():
        for k, ref in enumerate((x0_ref, x1_ref)):
            x_turned[:, k * rows : (k + 1) * rows] = turned(ref[...]).astype(BF)

    o_ref[...] = (
        dot(x_turned[:, :rows], d0_ref[0]) + dot(x_turned[:, rows:], d1_ref[0])
    ).astype(BF)


def weight_grad(order, x0, x1, d0, d1, block):
    rows, d = x0.shape
    parts, _, columns = d0.shape
    steps = columns // block
    narrow = pl.BlockSpec((1, rows, block), lambda j: (j // steps, 0, j % steps))
    return order.call(
        weight_grad_kernel, "weight_grad", 26, (x0, x1, d0, d1),
        [full((rows, d)), full((rows, d)), narrow, narrow],
        [pl.BlockSpec((d, block), lambda j: (0, j))], like((d, parts * columns, BF)),
        grid=(parts * steps,), scratch=[pltpu.VMEM((d, 2 * rows), BF)],
    )[0]


def down_kernel(act_ref, w_ref, o_ref):
    o_ref[...] = dot_nt(act_ref[...], w_ref[...]).astype(BF)


def down(order, act, w_down, block):
    rows, units = act.shape
    d = w_down.shape[0]
    return order.call(
        down_kernel, "down", 14, (act, w_down),
        [full((rows, units)), pl.BlockSpec((block, units), lambda j: (j, 0))],
        [pl.BlockSpec((rows, block), lambda j: (0, j))], like((rows, d, BF)), grid=(d // block,),
    )[0]


def grad_heads_kernel(place_ref, g0_ref, g1_ref, w_ref, o_ref):
    rows = g0_ref.shape[0] // 2
    for k in range(4):
        ref, low = (g0_ref, g1_ref)[k // 2], (k % 2) * rows
        at = pl.multiple_of(place_ref[k] * rows, rows)
        o_ref[:, pl.ds(at, rows)] = dot(ref[low : low + rows], w_ref[...]).T.astype(BF)


def grad_heads(order, places, g0, g1, w_full, depth):
    d, n = w_full.shape[0], 2 * g0.shape[0]
    last = w_full.shape[1] // depth - 1
    return order.call(
        grad_heads_kernel, "grad_heads", 16, (g0, g1, w_full),
        [*wholes((g0, g1)), pl.BlockSpec((d, depth), lambda i, place: (0, last))],
        [full((depth, n))], like((depth, n, BF)), prefetch=(places,),
    )[0]


def grad_x_kernel(place_ref, q_ref, k_ref, v_ref, w_ref, *out_refs):
    rows = out_refs[0].shape[0] // 2
    for k in range(4):
        parts = [columns_of(ref, place_ref[k], rows).astype(F32) for ref in (q_ref, k_ref, v_ref)]
        grads = jnp.concatenate(parts, axis=0).T.astype(BF)
        at = (k % 2) * rows
        out_refs[k // 2][at : at + rows] = dot_nt(grads, w_ref[...]).astype(BF)


def grad_x(order, places, dq, dk, dv, w_full):
    d, n = w_full.shape[0], dq.shape[1]
    return order.call(
        grad_x_kernel, "grad_x", 22, (dq, dk, dv, w_full),
        [*wholes((dq, dk, dv)), full((d, dq.shape[0] + dk.shape[0] + dv.shape[0]))],
        [full((n // 2, d))] * 2, like((n // 2, d, BF), (n // 2, d, BF)), prefetch=(places,),
    )


def tokens_product(place_ref, left_ref, refs):
    rows = refs[0].shape[0] // 2
    total = None
    for k in range(4):
        at = (k % 2) * rows
        part = dot(columns_of(left_ref, place_ref[k], rows), refs[k // 2][at : at + rows])
        total = part if total is None else total + part
    return total


def turned_grad_kernel(count, place_ref, *refs):
    lefts, rights, out = refs[:count], refs[count : count + 2], refs[count + 2]
    at = 0
    for ref in lefts:
        size = ref.shape[0]
        out[:, at : at + size] = tokens_product(place_ref, ref, rights).T.astype(BF)
        at += size


def turned_grad(order, places, lefts, x0, x1, name):
    d, columns = x0.shape[1], sum(left.shape[0] for left in lefts)
    arrays = (*lefts, x0, x1)
    return order.call(
        functools.partial(turned_grad_kernel, len(lefts)), name, 26, arrays, wholes(arrays),
        [full((d, columns))], like((d, columns, BF)), prefetch=(places,),
    )[0]


def row_inverse(values):
    return lax.rsqrt(jnp.mean(values * values, axis=-1, keepdims=True) + EPS)


def first_norm_kernel(a_ref, b_ref, g_ref, o_ref, h_ref, copy_ref):
    def run(ref):
        hidden = ref[...].astype(F32)
        h_ref[...] = ref[...]
        o_ref[...] = (hidden * row_inverse(hidden)).astype(BF)

    near = pl.program_id(0) < pl.num_programs(0) // 2
    pl.when(near)(lambda: run(a_ref))
    pl.when(jnp.logical_not(near))(lambda: run(b_ref))
    pl.when(near)(lambda: copy_ref.__setitem__(..., g_ref[...]))


def first_norm(order, a, b, g):
    rows, d = a.shape
    block = min(128, rows)
    steps = rows // block
    near = pl.BlockSpec((block, d), lambda i: (jnp.minimum(i, steps - 1), 0))
    each = pl.BlockSpec((block, d), lambda i: (i, 0))
    return order.call(
        first_norm_kernel, "first_norm", 10, (a, b, g),
        [near, pl.BlockSpec((block, d), lambda i: (jnp.maximum(i - steps, 0), 0)), near],
        [each, each, near], like((2 * rows, d, BF), (2 * rows, d, BF), (rows, d, BF)),
        grid=(2 * steps,), far=(0, 2),
    )


def join_kernel(a_ref, b_ref, o_ref):
    near = pl.program_id(0) < pl.num_programs(0) // 2
    pl.when(near)(lambda: o_ref.__setitem__(..., a_ref[...]))
    pl.when(jnp.logical_not(near))(lambda: o_ref.__setitem__(..., b_ref[...]))


def joined(order, kernel, name, a, b, count):
    rows, d = a.shape
    block = min(128, rows)
    steps = rows // block
    return order.call(
        kernel, name, 8, (a, b),
        [
            pl.BlockSpec((block, d), lambda i: (jnp.minimum(i, steps - 1), 0)),
            pl.BlockSpec((block, d), lambda i: (jnp.maximum(i - steps, 0), 0)),
        ],
        [pl.BlockSpec((block, d), lambda i: (i, 0))] * count, like(*[(2 * rows, d, BF)] * count),
        grid=(2 * steps,),
    )


def norm_kernel(h_ref, a_ref, b_ref, o_ref, resid_ref):
    resid = h_ref[...].astype(F32) + (a_ref[...].astype(F32) + b_ref[...].astype(F32))
    resid_ref[...] = resid
    o_ref[...] = (resid * row_inverse(resid)).astype(BF)


def back_through_norm(scaled, values):
    inverse = row_inverse(values)
    inner = jnp.mean(scaled * values, axis=-1, keepdims=True)
    return inverse * scaled - values * (inverse * inverse * inverse * inner)


def norm_back_kernel(a_ref, g_ref, resid_ref, b_ref, o_ref, grad_ref):
    scaled = a_ref[...].astype(F32) + b_ref[...].astype(F32)
    grad = g_ref[...].astype(F32) + back_through_norm(scaled, resid_ref[...])
    grad_ref[...] = grad
    o_ref[...] = grad.astype(BF)


def output_kernel(resid_ref, a_ref, b_ref, c_ref, o_ref):
    total = a_ref[...].astype(F32) + b_ref[...].astype(F32) + c_ref[...].astype(F32)
    o_ref[...] = (resid_ref[...] + total).astype(BF)


def hidden_grad_kernel(grad_ref, h_ref, a_ref, b_ref, c_ref, o_ref):
    scaled = a_ref[...].astype(F32) + b_ref[...].astype(F32) + c_ref[...].astype(F32)
    grad = grad_ref[...] + back_through_norm(scaled, h_ref[...].astype(F32))
    o_ref[...] = grad.astype(BF)


def plus_kernel(a_ref, b_ref, o_ref):
    o_ref[...] = (a_ref[...].astype(F32) + b_ref[...].astype(F32)).astype(BF)


def by_rows(order, kernel, name, rows, arrays, outs, first=None, far=(), far_out=()):
    d = arrays[0].shape[1]
    block = min(128, rows)
    first = first or [0] * len(arrays)

    def spec(array, start):
        count = array.shape[0] // block
        skip = start // block
        return pl.BlockSpec((block, d), lambda i: (lax.rem(i + skip, count), 0))

    return order.call(
        kernel, name, 12, arrays, [spec(a, start) for a, start in zip(arrays, first)],
        [pl.BlockSpec((block, d), lambda i: (i, 0))] * len(outs),
        like(*[(rows, d, dtype) for dtype in outs]), grid=(rows // block,), far=far,
        far_out=far_out,
    )


def add_kernel(index_ref, left_chunk, right_chunk, left_ref, right_ref, to_right, to_left):
    columns, cut = to_right.shape[1], left_ref.shape[1]
    to_right[:, :cut] = (left_chunk[:, :cut].astype(F32) + left_ref[...].astype(F32)).astype(BF)
    if cut < columns:
        to_right[:, cut:] = left_chunk[:, cut:]
    cut = columns - right_ref.shape[1]
    to_left[:, cut:] = (right_chunk[:, cut:].astype(F32) + right_ref[...].astype(F32)).astype(BF)
    if cut > 0:
        to_left[:, :cut] = right_chunk[:, :cut]


def add_chunks(order, whole, rows, start, width, first, second, from_left, from_right):
    chunk = lambda k: pl.BlockSpec((rows, width), lambda i, index: (index[k], start // width))
    return order.call(
        add_kernel, "add_chunks", 10, (whole, whole, from_left, from_right),
        [chunk(0), chunk(1), *wholes((from_left, from_right))], [full((rows, width))] * 2,
        like((rows, width, BF), (rows, width, BF)),
        prefetch=(jnp.stack([first, second]).astype(jnp.int32),),
    )


def arrived_sum(chunk_ref, lefts, rights):
    left = jnp.concatenate([ref[...].astype(F32) for ref in lefts], axis=1)
    right = jnp.concatenate([ref[...].astype(F32) for ref in rights], axis=1)
    return chunk_ref[...].astype(F32) + left + right


def finish_kernel(parts, widths, index_ref, chunk_ref, *refs):
    grad = arrived_sum(chunk_ref, refs[:parts], refs[parts : 2 * parts])
    gain_ref, refs = refs[2 * parts], refs[2 * parts + 1 :]
    weights, outs = refs[: len(widths)], refs[len(widths) :]
    gain, total, at = column(gain_ref[...]), None, 0
    for k, width in enumerate(widths):
        part = grad[:, at : at + width]
        term = jnp.sum(part * weights[k][...].astype(F32), axis=1, keepdims=True)
        total = term if total is None else total + term
        outs[k][...] = part * gain
        at += width
    outs[-1][...] = jnp.broadcast_to(total, (total.shape[0], 128)).T[:1]


def finish(order, whole, rows, own, lefts, rights, gain, weights):
    columns = whole.shape[1]
    widths = tuple(w.shape[1] for w in weights)
    return order.call(
        functools.partial(finish_kernel, len(lefts), widths), "finish", 16,
        (whole, *lefts, *rights, gain, *weights),
        [
            pl.BlockSpec((rows, columns), lambda i, index: (index[0], 0)),
            *wholes((*lefts, *rights, gain, *weights)),
        ],
        [*wholes(weights), full((1, rows))],
        like(*[(*w.shape, F32) for w in weights], (1, rows, F32)),
        prefetch=(own[None].astype(jnp.int32),), far=range(1 + 2 * len(lefts), 2 + 2 * len(lefts) + len(weights)),
        far_out=range(len(weights)),
    )


def finish_plain_kernel(parts, index_ref, chunk_ref, *refs):
    refs[-1][...] = arrived_sum(chunk_ref, refs[:parts], refs[parts : 2 * parts])


def finish_plain(order, whole, rows, own, lefts, rights):
    columns = whole.shape[1]
    return order.call(
        functools.partial(finish_plain_kernel, len(lefts)), "finish_plain", 12,
        (whole, *lefts, *rights),
        [
            pl.BlockSpec((rows, columns), lambda i, index: (index[0], 0)),
            *wholes((*lefts, *rights)),
        ],
        [full((rows, columns))], like((rows, columns, F32)),
        prefetch=(own[None].astype(jnp.int32),), far_out=(0,),
    )[0]


class Ring:
    def __init__(self, count):
        self.count = count
        self.half = count // 2
        order = [2 * k if k < self.half else 2 * (count - 1 - k) + 1 for k in range(count)]
        self.right = [(order[k], order[(k + 1) % count]) for k in range(count)]
        self.left = [(b, a) for a, b in self.right]
        me = lax.axis_index("dp")
        self.place = jnp.where(me % 2 == 0, me // 2, count - 1 - me // 2)

    def index(self, offset):
        place = (self.place + offset + self.count) % self.count
        return jnp.where(place < self.half, 2 * place, 2 * (self.count - 1 - place) + 1)

    def go_right(self, value):
        return lax.ppermute(value, "dp", self.right)

    def go_left(self, value):
        return lax.ppermute(value, "dp", self.left)


def cut_of(columns):
    return max(128, (columns // 2 + 127) // 128 * 128)


class Kept:
    def __init__(self, order, ring, parts):
        self.order, self.ring = order, ring
        self.parts, self.rows = parts, sum(part.shape[0] for part in parts)
        self.pieces, self.whole = [], None

    def put(self, which, offset, first, piece):
        skip = self.parts[0].shape[0] * which
        self.pieces.append((self.ring.index(offset) * self.rows + skip, first, piece))

    def finish(self):
        count, columns = self.ring.count * self.rows, self.parts[0].shape[1]
        self.whole = assemble(self.order, count, columns, *zip(*self.pieces))


class Gather:
    def __init__(self, kept, which):
        self.kept, self.order, self.ring, self.rounds = kept, kept.order, kept.ring, 1
        self.which = which
        shard = relay(self.order, kept.parts[which])[0]
        kept.put(which, 0, 0, shard)
        self.cut = cut_of(shard.shape[1])
        self.flying = self.ring.go_right(shard), self.ring.go_left(shard)

    def wait(self):
        while self.rounds < self.ring.half - 3:
            self.wait_one()
        self.wait_one()

    def wait_one(self):
        arrived = self.order.wait(*self.flying)
        last = self.rounds == self.ring.half
        if not last:
            arrived = relay(self.order, *arrived)
        self.kept.put(self.which, -self.rounds, 0, arrived[0])
        self.kept.put(self.which, self.rounds, self.cut if last else 0, arrived[1])
        self.rounds += 1
        if self.rounds == self.ring.half:
            arrived = halves(self.order, *arrived, self.cut)
        if not last:
            self.flying = self.ring.go_right(arrived[0]), self.ring.go_left(arrived[1])


class Turns:
    def __init__(self, make):
        self.make, self.ring = make, None

    def start(self):
        self.ring = self.make()

    def wait(self):
        self.ring.wait()


class Scatter:
    def __init__(self, order, ring, whole, first, width):
        self.order, self.ring, self.whole = order, ring, whole
        self.first, self.width = first, width
        self.rows = whole.shape[0] // ring.count
        self.steps = ring.half - 1
        right, left = far_chunk(
            order, whole, self.rows, first, width, ring.index(ring.half), cut_of(width)
        )
        self.flying = ring.go_right(right), ring.go_left(left)

    def wait(self):
        while self.steps > 3:
            self.wait_one()
        self.wait_one()

    def wait_one(self):
        step = self.steps
        right, left = add_chunks(
            self.order, self.whole, self.rows, self.first, self.width, self.ring.index(step),
            self.ring.index(-step), *self.order.wait(*self.flying),
        )
        self.steps -= 1
        self.flying = self.ring.go_right(right), self.ring.go_left(left)

    def last(self):
        while self.steps:
            self.wait_one()
        return self.order.wait(*self.flying)


def scaled_sum(sums, gain, weights):
    arrived = [part.last() for part in sums]
    part = sums[0]
    return finish(
        part.order, part.whole, part.rows, part.ring.index(0), [a for a, _ in arrived],
        [b for _, b in arrived], gain, weights,
    )


def plain_sum(sums):
    arrived = [part.last() for part in sums]
    part = sums[0]
    return finish_plain(
        part.order, part.whole, part.rows, part.ring.index(0), [a for a, _ in arrived],
        [b for _, b in arrived],
    )


def swap_core(value):
    return lax.ppermute(value, "tensor", CORE_PAIRS)


def swap_x(value):
    return lax.ppermute(value, "tensor", X_PAIRS)


def plus(order, left_side, right_side, rows, first=0):
    arrays = (left_side, right_side)
    return by_rows(order, plus_kernel, "plus", rows, arrays, (BF,), (first, first))[0]


def per_device(
    dp_count,
    hidden_in,
    segments,
    attn_gain,
    w_query,
    w_key,
    w_value,
    w_out,
    mlp_gain,
    w_gate,
    w_up,
    w_down,
    cotangent,
):
    ring = Ring(dp_count)
    device = lax.axis_index("tensor").astype(jnp.int32)
    places = jnp.stack([device, device ^ 2, device ^ 1, device ^ 3])
    rows = hidden_in.shape[0]
    both = 2 * rows
    query_columns = w_query.shape[1]
    heads = query_columns // HD, w_key.shape[1] // HD
    units = w_gate.shape[1]
    block = units // 2
    order = Order()
    v = types.SimpleNamespace()

    def go(value):
        return relay(order, value)[0]

    A = Turns(lambda: Gather(v.A, 0))
    B = Turns(lambda: Gather(v.B, 0))
    C = Turns(lambda: Gather(v.C, 0))
    D = Turns(lambda: Scatter(order, ring, v.down_grad, 0, units))
    G = Turns(lambda: Scatter(order, ring, v.gate_up_grad, 0, units))
    U = Turns(lambda: Scatter(order, ring, v.gate_up_grad, units, units))
    Q = Turns(lambda: Scatter(order, ring, v.qkv_grad, 0, 2 * query_columns))
    O = Turns(lambda: Scatter(order, ring, v.out_grad, 0, query_columns))

    def A_all():
        v.A.finish()

    def B_all():
        v.B.finish()

    def C_all():
        v.C.finish()

    def shard_a():
        weights = [w_query, w_key, w_value]
        shard = make_shard(order, attn_gain, weights, [w_out.T], "attn_shard", 14, False)
        v.A = Kept(order, ring, shard)

    def shard_b():
        shard = make_shard(order, mlp_gain, [w_gate, w_up], [], "gate_up_shard", 14, False)
        v.B = Kept(order, ring, shard)

    def shard_c():
        shard = make_shard(order, mlp_gain, [], [w_down.T], "down_shard", 8, False)
        v.C = Kept(order, ring, shard)

    def hidden_x():
        v.hidden_across = swap_x(hidden_in)

    def tables():
        v.cos, v.sin, v.start = rope_tables(order, segments)

    def norm_one():
        order.wait(v.hidden_across)
        v.normed, v.hidden, v.grads_own = first_norm(
            order, hidden_in, v.hidden_across, cotangent
        )

    def normed_core():
        v.normed = go(v.normed)
        v.normed_other = swap_core(v.normed)

    def grads_x():
        v.grads_own = go(v.grads_own)
        v.grads_across = swap_x(v.grads_own)

    def qkv():
        order.wait(v.normed_other)
        v.qkv = project(
            order, places, v.normed, v.normed_other, v.A.whole, v.cos, v.sin, *heads
        )

    def grads_join():
        order.wait(v.grads_across)
        v.grads = joined(order, join_kernel, "join", cotangent, v.grads_across, 1)[0]

    def grads_core():
        v.grads = go(v.grads)
        v.grads_other = swap_core(v.grads)

    def attention():
        v.heads_out, v.log_total = attend(order, v.qkv, v.start, *heads, rows)

    def out_part():
        v.part, v.part_other = branch(order, places, v.heads_out, v.A.whole)

    def part_core():
        v.part_other = go(v.part_other)
        v.part_core = swap_core(v.part_other)

    def part_x():
        order.wait(v.part_core)
        v.chip = plus(order, v.part, v.part_core, both)
        v.across = swap_x(v.chip)

    def norm_two():
        order.wait(v.across)
        v.normed_two, v.resid = by_rows(
            order, norm_kernel, "norm", both, (v.hidden, v.chip, v.across), (BF, F32),
            (0, 0, rows),
        )

    def normed_two_core():
        v.normed_two = go(v.normed_two)
        v.normed_two_other = swap_core(v.normed_two)

    def mlp_mine():
        v.act, v.da, v.db = gate_up(order, v.normed_two, v.B.whole, block)

    def mlp_other():
        order.wait(v.normed_two_other)
        v.act_other, v.da_other, v.db_other = gate_up(
            order, v.normed_two_other, v.B.whole, block
        )

    def grad_down():
        order.wait(v.grads_other)
        v.down_grad = weight_grad(
            order, v.grads, v.grads_other, v.act[None], v.act_other[None], block
        )

    def down_mine():
        v.down = down(order, v.act, v.C.whole, 512)

    def down_other():
        v.down_other = down(order, v.act_other, v.C.whole, 512)

    def down_core():
        v.down_other = go(v.down_other)
        v.down_core = swap_core(v.down_other)

    def down_x():
        order.wait(v.down_core)
        v.down_theirs = swap_x(plus(order, v.down, v.down_core, rows, rows))

    def finish_output():
        order.wait(v.down_theirs)
        arrays = (v.resid, v.down, v.down_core, v.down_theirs)
        v.output = by_rows(
            order, output_kernel, "output", rows, arrays, (BF,), far_out=(0,)
        )[0]

    def back_mine():
        v.scaled, v.d = mlp_back(
            order, v.grads, v.da, v.db, v.C.whole, v.B.whole, block
        )

    def back_other():
        v.scaled_other, v.d_other = mlp_back(
            order, v.grads_other, v.da_other, v.db_other, v.C.whole, v.B.whole, block
        )

    def scaled_core():
        v.scaled_other = go(v.scaled_other)
        v.scaled_core = swap_core(v.scaled_other)

    def scaled_x():
        order.wait(v.scaled_core)
        v.chip_back = plus(order, v.scaled, v.scaled_core, both)
        v.across_back = swap_x(v.chip_back)

    def grad_gate_up():
        v.gate_up_grad = weight_grad(
            order, v.normed_two, v.normed_two_other, v.d, v.d_other, block
        )

    def norm_two_back():
        order.wait(v.across_back)
        v.branch, v.grad_resid = by_rows(
            order, norm_back_kernel, "norm_back", both,
            (v.chip_back, v.grads, v.resid, v.across_back), (BF, F32), (0, 0, 0, rows),
        )

    def branch_core():
        v.branch = go(v.branch)
        v.branch_other = swap_core(v.branch)

    def heads_back():
        order.wait(v.branch_other)
        v.grad_heads = grad_heads(
            order, places, v.branch, v.branch_other, v.A.whole, query_columns
        )

    def attention_back():
        v.dq, v.dk, v.dv = attend_back(
            order, v.qkv, v.grad_heads, v.heads_out, v.log_total, v.start, v.cos,
            v.sin, *heads, rows,
        )

    def grad_out():
        v.out_grad = turned_grad(
            order, places, [v.heads_out], v.branch, v.branch_other, "out_grad"
        )

    def grad_qkv():
        v.qkv_grad = turned_grad(
            order, places, [v.dq, v.dk, v.dv], v.normed, v.normed_other, "qkv_grad"
        )

    def grad_hidden():
        v.u, v.u_other = grad_x(order, places, v.dq, v.dk, v.dv, v.A.whole)

    def u_core():
        v.u_other = go(v.u_other)
        v.u_core = swap_core(v.u_other)

    def u_x():
        order.wait(v.u_core)
        v.u_theirs = swap_x(plus(order, v.u, v.u_core, rows, rows))

    def finish_hidden():
        order.wait(v.u_theirs)
        arrays = (v.grad_resid, hidden_in, v.u, v.u_core, v.u_theirs)
        v.hidden_grad = by_rows(
            order, hidden_grad_kernel, "hidden_grad", rows, arrays, (BF,), far=(1,), far_out=(0,)
        )[0]

    def finish_down():
        v.down_w = plain_sum([D.ring])

    def finish_gate_up():
        sums = [G.ring, U.ring]
        v.gate_w, v.up_w, v.gain_two = scaled_sum(sums, mlp_gain, [w_gate, w_up])

    def finish_qkv():
        v.query_w, v.key_w, v.value_w, v.gain_one = scaled_sum(
            [Q.ring], attn_gain, [w_query, w_key, w_value]
        )

    def finish_out():
        v.out_w = plain_sum([O.ring])

    def wait_g():
        order.wait(*G.ring.flying)

    def wait_u():
        order.wait(*U.ring.flying)

    schedule = (
        shard_a, A.start, shard_b, hidden_x, shard_c, C.start, tables, B.start, A.wait, A.wait,
        norm_one, grads_x, B.wait, grads_join, A.wait, C.wait, A.wait, normed_core, A_all, qkv,
        attention, out_part, B.wait, part_core, part_x, B.wait, B.wait, C.wait, B_all, norm_two,
        normed_two_core, mlp_mine, C.wait, grads_core, mlp_other, grad_down, D.start, C.wait,
        C_all, back_other, D.wait, scaled_core, back_mine, scaled_x, D.wait, grad_gate_up,
        U.start, D.wait, down_mine, G.start, finish_down, U.wait, G.wait, norm_two_back,
        branch_core, heads_back, attention_back, U.wait, grad_out, down_other, G.wait, grad_qkv,
        Q.start, U.wait, grad_hidden, O.start, G.wait, u_core, Q.wait, O.wait, down_core, u_x,
        down_x, Q.wait, O.wait, Q.wait, O.wait, finish_output, finish_gate_up, finish_qkv,
        wait_u, finish_hidden, wait_g, finish_out,
    )
    for run in schedule:
        run()
    gains = lax.psum(jnp.concatenate([v.gain_one, v.gain_two], axis=0), "tensor")
    return (
        v.output,
        v.hidden_grad,
        gains[0],
        v.query_w,
        v.key_w,
        v.value_w,
        v.out_w.T,
        gains[1],
        v.gate_w,
        v.up_w,
        v.down_w.T,
    )


def solution(mesh):
    tokens, split = P(("dp", "tensor"), None), P("dp", "tensor")
    in_specs = (
        tokens, P("dp"), P("dp"), split, split, split, P("tensor", "dp"),
        P("dp"), split, split, P("tensor", "dp"), tokens,
    )
    out_specs = (
        tokens, tokens, P("dp"), split, split, split, P("tensor", "dp"),
        P("dp"), split, split, P("tensor", "dp"),
    )
    body = functools.partial(per_device, mesh.shape["dp"])
    return jax.shard_map(body, mesh=mesh, in_specs=in_specs, out_specs=out_specs, check_vma=False)
```

```python
import functools
import math
import types

import jax
import jax.numpy as jnp
from jax import lax
from jax.experimental import pallas as pl
from jax.experimental.pallas import tpu as pltpu
from jax.sharding import PartitionSpec as P

HD = 96
HALF = HD // 2
DOCUMENTS = 5
EPS = 1e-05
NEG = -1e30
THETA = 100000.0
SCALE = HD ** (-0.5)
LOG2E = math.log2(math.e)
BF = jnp.bfloat16
F32 = jnp.float32
MIB = 1024 * 1024

CORE_PAIRS = [(0, 1), (1, 0), (2, 3), (3, 2)]
X_PAIRS = [(0, 2), (2, 0), (1, 3), (3, 1)]


def dot(left_side, right_side):
    return jnp.dot(left_side, right_side, preferred_element_type=F32)


def dot_nt(left_side, right_side):
    return lax.dot_general(
        left_side, right_side, (((1,), (1,)), ((), ())), preferred_element_type=F32
    )


def turned(value):
    return value.astype(F32).T


class Order:
    def __init__(self):
        self.waited, self.token = [], None

    def wait(self, *values):
        self.waited += values
        return values[0] if len(values) == 1 else values

    def call(
        self, body, name, mib, args, in_specs, out_specs, out_shape, grid=(1,), scratch=(),
        prefetch=(), aliases=None, far=(), near=(), far_out=(), near_out=(),
    ):
        seen = [a for a in self.waited if not any(a is b for b in args)]
        if self.token is not None:
            seen.append(pltpu.with_memory_space_constraint(self.token, pltpu.HBM))
        first, extra, count = len(prefetch) + len(args), len(seen), len(out_shape)
        args = list(args)
        for k in far:
            args[k] = pltpu.with_memory_space_constraint(args[k], pltpu.HBM)
        for k in near:
            args[k] = pltpu.with_memory_space_constraint(args[k], pltpu.VMEM)
        out_shape = list(out_shape)
        for k in far_out:
            out_shape[k] = pltpu.HBM(out_shape[k].shape, out_shape[k].dtype)
        for k in near_out:
            out_shape[k] = pltpu.VMEM(out_shape[k].shape, out_shape[k].dtype)

        def kernel(*refs):
            outs = refs[first + extra :]
            body(*refs[:first], *outs[:count], *outs[count + 1 :])

        *out, self.token = pl.pallas_call(
            kernel,
            grid_spec=pltpu.PrefetchScalarGridSpec(
                num_scalar_prefetch=len(prefetch),
                grid=grid,
                in_specs=[*in_specs, *[ANY] * extra],
                out_specs=[*out_specs, ANY],
                scratch_shapes=scratch,
            ),
            out_shape=[*out_shape, pltpu.HBM((8, 128), F32)],
            input_output_aliases=aliases or {},
            compiler_params=pltpu.CompilerParams(vmem_limit_bytes=mib * MIB),
            cost_estimate=pl.CostEstimate(flops=0, bytes_accessed=0, transcendentals=0),
            name=name,
        )(*prefetch, *args, *seen)
        self.waited = []
        return out


def full(shape):
    return pl.BlockSpec(tuple(shape), lambda *_: (0,) * len(shape))


def wholes(arrays):
    return [full(a.shape) for a in arrays]


def like(*shapes):
    return [jax.ShapeDtypeStruct(shape, dtype) for *shape, dtype in shapes]


ANY = pl.BlockSpec(memory_space=pl.ANY)
HBM = pl.BlockSpec(memory_space=pltpu.HBM)
VMEM = pl.BlockSpec(memory_space=pltpu.VMEM)


def column(row):
    return jnp.broadcast_to(row.astype(F32)[None], (8, row.shape[0])).T[:, :1]


def put(outs, first, value):
    top, width = outs[0].shape[0], value.shape[1]
    outs[0][:, first : first + width] = value[:top]
    if len(outs) > 1:
        outs[1][:, first : first + width] = value[top:]


def shard_kernel(scaled, plain, gain_ref, *refs):
    gain, first = column(gain_ref[...]), 0
    inputs, outs = refs[: scaled + plain], refs[scaled + plain :]
    for k, ref in enumerate(inputs):
        value = (ref[...].astype(F32) * gain).astype(BF) if k < scaled else ref[...]
        put(outs, first, value)
        first += ref.shape[1]


def top_of(rows):
    return (rows // 2 + 15) // 16 * 16


def make_shard(order, gain, scaled, plain, name, mib, split):
    rows = (*scaled, *plain)[0].shape[0]
    columns = sum(w.shape[1] for w in (*scaled, *plain))
    top = top_of(rows) if split else rows
    shapes = [(count, columns) for count in (top, rows - top) if count]
    return order.call(
        functools.partial(shard_kernel, len(scaled), len(plain)), name, mib,
        (gain, *scaled, *plain), wholes((gain, *scaled, *plain)), [full(shape) for shape in shapes],
        like(*[(*shape, BF) for shape in shapes]), far=range(1, 1 + len(scaled) + len(plain)),
    )


def relay_kernel(*refs):
    pass


def relay(order, *values):
    count = len(values)
    return order.call(
        relay_kernel, "relay", 2, values, [ANY] * count, [ANY] * count,
        like(*[(*value.shape, value.dtype) for value in values]),
        aliases={k: k for k in range(count)},
    )


def assemble_kernel(spans, place_ref, *refs):
    pieces, whole, sems = refs[: len(spans)], refs[len(spans)], refs[len(spans) + 1]
    copies = []
    for k, (first, width) in enumerate(spans):
        at = pl.multiple_of(place_ref[k], 16)
        where = whole.at[pl.ds(at, pieces[k].shape[0]), pl.ds(first, width)]
        copies.append(pltpu.make_async_copy(pieces[k], where, sems.at[k]))
    for copy in copies:
        copy.start()
    for copy in copies:
        copy.wait()


def assemble(order, rows, columns, places, firsts, pieces):
    count = len(pieces)
    spans = tuple((first, piece.shape[1]) for first, piece in zip(firsts, pieces))
    return order.call(
        functools.partial(assemble_kernel, spans), "assemble", 2, pieces, [ANY] * count, [VMEM],
        like((rows, columns, BF)), scratch=[pltpu.SemaphoreType.DMA((count,))],
        prefetch=(jnp.stack(places).astype(jnp.int32),), far=range(count), near_out=(0,),
    )[0]


def halves_kernel(cut, a_ref, b_ref, c_ref, d_ref):
    c_ref[...] = a_ref[:, :cut]
    d_ref[...] = b_ref[:, cut:]


def halves(order, right, left, cut):
    rows, columns = right.shape
    shapes = (rows, cut), (rows, columns - cut)
    return order.call(
        functools.partial(halves_kernel, cut), "halves", 6, (right, left), wholes((right, left)),
        [full(shape) for shape in shapes], like(*[(*shape, BF) for shape in shapes]),
    )


def far_kernel(cut, index_ref, chunk_ref, c_ref, d_ref):
    c_ref[...] = chunk_ref[:, :cut]
    d_ref[...] = chunk_ref[:, cut:]


def far_chunk(order, whole, rows, first, width, index, cut):
    shapes = (rows, cut), (rows, width - cut)
    return order.call(
        functools.partial(far_kernel, cut), "far_chunk", 8, (whole,),
        [pl.BlockSpec((rows, width), lambda i, index: (index[0], first // width))],
        [full(shape) for shape in shapes], like(*[(*shape, BF) for shape in shapes]),
        prefetch=(index[None].astype(jnp.int32),),
    )


def tables_kernel(segment_ref, c_ref, s_ref, opening_ref):
    segment = segment_ref[...]
    opening = jnp.zeros_like(segment)
    for number in range(DOCUMENTS - 1):
        count = jnp.sum((segment == number).astype(jnp.int32), axis=1, keepdims=True)
        opening += jnp.where(segment > number, count, 0)
    position = (lax.broadcasted_iota(jnp.int32, segment.shape, 1) - opening).astype(F32)
    place = lax.broadcasted_iota(jnp.int32, c_ref.shape, 0).astype(F32)
    angle = jnp.exp(-(2.0 * place / HD) * math.log(THETA)) * position
    c_ref[...] = jnp.cos(angle)
    s_ref[...] = jnp.sin(angle)
    opening_ref[...] = opening


def rope_tables(order, segments):
    n = segments.shape[0]
    shapes = (HALF, n), (HALF, n), (1, n)
    return order.call(
        tables_kernel, "rope_tables", 8, (segments[None],), [full((1, n))],
        [full(shape) for shape in shapes],
        like((HALF, n, F32), (HALF, n, F32), (1, n, jnp.int32)),
    )


def rope_rows(values, cosine, sine):
    first, second = values[:HALF], values[HALF:]
    return first * cosine - second * sine, second * cosine + first * sine


def project_kernel(query_heads, key_heads, place_ref, x0_ref, x1_ref, w_ref, c_ref, s_ref, o_ref):
    def run(x_ref):
        turned_heads = dot(x_ref[...], w_ref[...]).T
        cosine, sine = c_ref[...], s_ref[...]
        for h in range(query_heads + key_heads):
            first, second = rope_rows(turned_heads[h * HD : (h + 1) * HD], cosine, sine)
            if h < query_heads:
                first, second = first * (SCALE * LOG2E), second * (SCALE * LOG2E)
            o_ref[h * HD : h * HD + HALF, :] = first.astype(BF)
            o_ref[h * HD + HALF : (h + 1) * HD, :] = second.astype(BF)
        done = (query_heads + key_heads) * HD
        o_ref[done:, :] = turned_heads[done:].astype(BF)

    pl.when(pl.program_id(0) < 2)(lambda: run(x0_ref))
    pl.when(pl.program_id(0) >= 2)(lambda: run(x1_ref))


def project(order, places, x0, x1, w, cosine, sine, query_heads, key_heads):
    block, d = x0.shape[0] // 2, x0.shape[1]
    columns = (query_heads + 2 * key_heads) * HD
    table = pl.BlockSpec((HALF, block), lambda i, place: (0, place[i]))
    return order.call(
        functools.partial(project_kernel, query_heads, key_heads), "project", 18,
        (x0, x1, w, cosine, sine),
        [
            pl.BlockSpec((block, d), lambda i, place: (jnp.minimum(i, 1), 0)),
            pl.BlockSpec((block, d), lambda i, place: (jnp.maximum(i - 2, 0), 0)),
            full((d, columns)),
            table,
            table,
        ],
        [pl.BlockSpec((columns, block), lambda i, place: (0, place[i]))],
        like((columns, 4 * block, BF)), grid=(4,), prefetch=(places,),
    )[0]


def side(ref, low, high):
    return jnp.concatenate(
        [ref[h * HD : (h + 1) * HD, low:high] for h in range(ref.shape[0] // HD)], axis=1
    )


def attend_kernel(block, q_ref, k_ref, v_ref, start_ref, o_ref, l_ref):
    n, group = q_ref.shape[1], q_ref.shape[0] // HD
    keys = turned(k_ref[...]).astype(BF)
    row = lax.broadcasted_iota(jnp.int32, (block, group * block), 0)
    column = lax.broadcasted_iota(jnp.int32, (block, group * block), 1) % block
    for i in range(n // block):
        low, high = i * block, (i + 1) * block
        start = jnp.concatenate([start_ref[:, low:high]] * group, axis=1)
        scores = dot(keys[:high], side(q_ref, low, high))
        at = lax.broadcasted_iota(jnp.int32, (high, group * block), 0)
        scores = jnp.where(at >= start, scores, NEG)
        near = jnp.where(row <= column, scores[low:], NEG)
        top = jnp.max(near, axis=0, keepdims=True)
        if i:
            top = jnp.maximum(top, jnp.max(scores[:low], axis=0, keepdims=True))
        near = jnp.exp2(near - top)
        total = jnp.sum(near, axis=0, keepdims=True)
        out = dot(v_ref[:, low:high], near.astype(BF))
        if i:
            far = jnp.exp2(scores[:low] - top)
            total = total + jnp.sum(far, axis=0, keepdims=True)
            out = out + dot(v_ref[:, :low], far.astype(BF))
        out = out * (1.0 / total)
        log_total = top + jnp.log2(total)
        for h in range(group):
            part = slice(h * block, (h + 1) * block)
            o_ref[h * HD : (h + 1) * HD, low:high] = out[:, part].astype(BF)
            l_ref[0, h : h + 1, low:high] = log_total[:, part]


def attend(order, qkv, start, query_heads, key_heads, block):
    n, group = qkv.shape[1], query_heads // key_heads
    return order.call(
        functools.partial(attend_kernel, block), "attend", 20, (qkv, qkv, qkv, start),
        [
            pl.BlockSpec((group * HD, n), lambda i: (i, 0)),
            pl.BlockSpec((HD, n), lambda i: (query_heads + i, 0)),
            pl.BlockSpec((HD, n), lambda i: (query_heads + key_heads + i, 0)),
            full((1, n)),
        ],
        [
            pl.BlockSpec((group * HD, n), lambda i: (i, 0)),
            pl.BlockSpec((1, group, n), lambda i: (i, 0, 0)),
        ],
        like((query_heads * HD, n, BF), (key_heads, group, n, F32)), grid=(key_heads,),
    )


def attend_back_kernel(
    block, q_ref, k_ref, v_ref, g_ref, h_ref, l_ref, start_ref, c_ref, s_ref,
    dq_ref, dk_ref, dv_ref, dk_sum, dv_sum,
):
    n, group = q_ref.shape[1], q_ref.shape[0] // HD
    keys = turned(k_ref[...]).astype(BF)
    values = turned(v_ref[...]).astype(BF)
    dk_sum[...] = jnp.zeros_like(dk_sum)
    dv_sum[...] = jnp.zeros_like(dv_sum)
    for i in range(n // block):
        low, high = i * block, (i + 1) * block
        queries, grads = side(q_ref, low, high), side(g_ref, low, high)
        outs = side(h_ref, low, high)
        query_rows, grad_rows = turned(queries).astype(BF), turned(grads).astype(BF)
        inner = jnp.sum(grads.astype(F32) * outs.astype(F32), axis=0, keepdims=True)
        log_total = jnp.concatenate([l_ref[0, h : h + 1, low:high] for h in range(group)], axis=1)
        start = jnp.concatenate([start_ref[:, low:high]] * group, axis=1)
        dq = jnp.zeros((HD, group * block), F32)
        for first, last in ([(0, low)] if i else []) + [(low, high)]:
            scores = dot(keys[first:last], queries)
            at = lax.broadcasted_iota(jnp.int32, scores.shape, 0) + first
            allowed = at >= start
            if first == low:
                column = lax.broadcasted_iota(jnp.int32, scores.shape, 1) % block + low
                allowed = allowed & (at <= column)
            probs = jnp.exp2(jnp.where(allowed, scores - log_total, NEG))
            dp = dot(values[first:last], grads)
            ds = (probs * (dp - inner)).astype(BF)
            dv_sum[first:last, :] += dot(probs.astype(BF), grad_rows)
            dk_sum[first:last, :] += dot(ds, query_rows)
            dq = dq + dot(k_ref[:, first:last], ds)
        dq = dq * SCALE
        cosine, sine = c_ref[:, low:high], s_ref[:, low:high]
        for h in range(group):
            top, bottom = rope_rows(dq[:, h * block : (h + 1) * block], cosine, -sine)
            dq_ref[h * HD : h * HD + HALF, low:high] = top.astype(BF)
            dq_ref[h * HD + HALF : (h + 1) * HD, low:high] = bottom.astype(BF)
    top, bottom = rope_rows(dk_sum[...].T * (1.0 / LOG2E), c_ref[...], -s_ref[...])
    dk_ref[:HALF, :] = top.astype(BF)
    dk_ref[HALF:, :] = bottom.astype(BF)
    dv_ref[...] = dv_sum[...].T.astype(BF)


def attend_back(order, qkv, grads, heads_out, log_total, start, cosine, sine, query_heads, key_heads, block):
    n, group = qkv.shape[1], query_heads // key_heads
    wide = pl.BlockSpec((group * HD, n), lambda i: (i, 0))
    narrow = pl.BlockSpec((HD, n), lambda i: (i, 0))
    return order.call(
        functools.partial(attend_back_kernel, block), "attend_back", 26,
        (qkv, qkv, qkv, grads, heads_out, log_total, start, cosine, sine),
        [
            wide,
            pl.BlockSpec((HD, n), lambda i: (query_heads + i, 0)),
            pl.BlockSpec((HD, n), lambda i: (query_heads + key_heads + i, 0)),
            wide,
            wide,
            pl.BlockSpec((1, group, n), lambda i: (i, 0, 0)),
            full((1, n)),
            full((HALF, n)),
            full((HALF, n)),
        ],
        [wide, narrow, narrow],
        like((query_heads * HD, n, BF), (key_heads * HD, n, BF), (key_heads * HD, n, BF)),
        grid=(key_heads,), scratch=[pltpu.VMEM((n, HD), F32), pltpu.VMEM((n, HD), F32)],
    )


def columns_of(ref, place, block):
    return ref[:, pl.ds(pl.multiple_of(place * block, block), block)]


def branch_kernel(place_ref, h_ref, w_ref, *out_refs):
    rows = out_refs[0].shape[0] // 2
    for k in range(4):
        heads = turned(columns_of(h_ref, place_ref[k], rows)).astype(BF)
        at = (k % 2) * rows
        out_refs[k // 2][at : at + rows] = dot_nt(heads, w_ref[...]).astype(BF)


def branch(order, places, heads_out, w_full):
    (depth, n), d = heads_out.shape, w_full.shape[0]
    last = w_full.shape[1] // depth - 1
    return order.call(
        branch_kernel, "branch", 18, (heads_out, w_full),
        [full((depth, n)), pl.BlockSpec((d, depth), lambda i, place: (0, last))],
        [full((n // 2, d))] * 2, like((n // 2, d, BF), (n // 2, d, BF)), prefetch=(places,),
    )


def gate_up_kernel(x_ref, wg_ref, wu_ref, act_ref, a_ref, b_ref):
    gate, up = dot(x_ref[...], wg_ref[...]), dot(x_ref[...], wu_ref[...])
    sigmoid = 1.0 / (1.0 + jnp.exp(-gate))
    silu = gate * sigmoid
    act_ref[...] = (silu * up).astype(BF)
    a_ref[...] = (up * sigmoid * (1.0 + gate * (1.0 - sigmoid))).astype(BF)
    b_ref[...] = silu.astype(BF)


def gate_up(order, x, w, block):
    rows, d = x.shape
    units = w.shape[1] // 2
    steps = units // block
    return order.call(
        gate_up_kernel, "gate_up", 24, (x, w, w),
        [
            full((rows, d)),
            pl.BlockSpec((d, block), lambda j: (0, j)),
            pl.BlockSpec((d, block), lambda j: (0, j + steps)),
        ],
        [pl.BlockSpec((rows, block), lambda j: (0, j))] * 3, like(*[(rows, units, BF)] * 3),
        grid=(steps,),
    )


def mlp_back_kernel(g_ref, a_ref, b_ref, wd_ref, wg_ref, wu_ref, u_ref, d_ref, total):
    step, last = pl.program_id(0), pl.num_programs(0) - 1
    grad_act = dot(g_ref[...], wd_ref[...])
    d_ref[0] = (grad_act * a_ref[...].astype(F32)).astype(BF)
    d_ref[1] = (grad_act * b_ref[...].astype(F32)).astype(BF)
    part = dot_nt(d_ref[0], wg_ref[...]) + dot_nt(d_ref[1], wu_ref[...])

    @pl.when(step == 0)
    def _():
        total[...] = part

    @pl.when((step > 0) & (step < last))
    def _():
        total[...] += part

    @pl.when(step == last)
    def _():
        u_ref[...] = (total[...] + part).astype(BF)


def mlp_back(order, g, a, b, w_down, w, block):
    rows, d = g.shape
    units = a.shape[1]
    steps = units // block
    assert steps > 1
    narrow = pl.BlockSpec((rows, block), lambda j: (0, j))
    return order.call(
        mlp_back_kernel, "mlp_back", 32, (g, a, b, w_down, w, w),
        [
            full((rows, d)),
            narrow,
            narrow,
            pl.BlockSpec((d, block), lambda j: (0, j)),
            pl.BlockSpec((d, block), lambda j: (0, j)),
            pl.BlockSpec((d, block), lambda j: (0, j + steps)),
        ],
        [full((rows, d)), pl.BlockSpec((2, rows, block), lambda j: (0, 0, j))],
        like((rows, d, BF), (2, rows, units, BF)), grid=(steps,),
        scratch=[pltpu.VMEM((rows, d), F32)],
    )


def weight_grad_kernel(x0_ref, x1_ref, d0_ref, d1_ref, o_ref, x_turned):
    rows = x0_ref.shape[0]

    @pl.when(pl.program_id(0) == 0)
    def _():
        for k, ref in enumerate((x0_ref, x1_ref)):
            x_turned[:, k * rows : (k + 1) * rows] = turned(ref[...]).astype(BF)

    o_ref[...] = (
        dot(x_turned[:, :rows], d0_ref[0]) + dot(x_turned[:, rows:], d1_ref[0])
    ).astype(BF)


def weight_grad(order, x0, x1, d0, d1, block):
    rows, d = x0.shape
    parts, _, columns = d0.shape
    steps = columns // block
    narrow = pl.BlockSpec((1, rows, block), lambda j: (j // steps, 0, j % steps))
    return order.call(
        weight_grad_kernel, "weight_grad", 26, (x0, x1, d0, d1),
        [full((rows, d)), full((rows, d)), narrow, narrow],
        [pl.BlockSpec((d, block), lambda j: (0, j))], like((d, parts * columns, BF)),
        grid=(parts * steps,), scratch=[pltpu.VMEM((d, 2 * rows), BF)],
    )[0]


def down_kernel(act_ref, w_ref, o_ref):
    o_ref[...] = dot_nt(act_ref[...], w_ref[...]).astype(BF)


def down(order, act, w_down, block):
    rows, units = act.shape
    d = w_down.shape[0]
    return order.call(
        down_kernel, "down", 14, (act, w_down),
        [full((rows, units)), pl.BlockSpec((block, units), lambda j: (j, 0))],
        [pl.BlockSpec((rows, block), lambda j: (0, j))], like((rows, d, BF)), grid=(d // block,),
    )[0]


def grad_heads_kernel(place_ref, g0_ref, g1_ref, w_ref, o_ref):
    rows = g0_ref.shape[0] // 2
    for k in range(4):
        ref, low = (g0_ref, g1_ref)[k // 2], (k % 2) * rows
        at = pl.multiple_of(place_ref[k] * rows, rows)
        o_ref[:, pl.ds(at, rows)] = dot(ref[low : low + rows], w_ref[...]).T.astype(BF)


def grad_heads(order, places, g0, g1, w_full, depth):
    d, n = w_full.shape[0], 2 * g0.shape[0]
    last = w_full.shape[1] // depth - 1
    return order.call(
        grad_heads_kernel, "grad_heads", 16, (g0, g1, w_full),
        [*wholes((g0, g1)), pl.BlockSpec((d, depth), lambda i, place: (0, last))],
        [full((depth, n))], like((depth, n, BF)), prefetch=(places,),
    )[0]


def grad_x_kernel(place_ref, q_ref, k_ref, v_ref, w_ref, *out_refs):
    rows = out_refs[0].shape[0] // 2
    for k in range(4):
        parts = [columns_of(ref, place_ref[k], rows).astype(F32) for ref in (q_ref, k_ref, v_ref)]
        grads = jnp.concatenate(parts, axis=0).T.astype(BF)
        at = (k % 2) * rows
        out_refs[k // 2][at : at + rows] = dot_nt(grads, w_ref[...]).astype(BF)


def grad_x(order, places, dq, dk, dv, w_full):
    d, n = w_full.shape[0], dq.shape[1]
    return order.call(
        grad_x_kernel, "grad_x", 22, (dq, dk, dv, w_full),
        [*wholes((dq, dk, dv)), full((d, dq.shape[0] + dk.shape[0] + dv.shape[0]))],
        [full((n // 2, d))] * 2, like((n // 2, d, BF), (n // 2, d, BF)), prefetch=(places,),
    )


def tokens_product(place_ref, left_ref, refs):
    rows = refs[0].shape[0] // 2
    total = None
    for k in range(4):
        at = (k % 2) * rows
        part = dot(columns_of(left_ref, place_ref[k], rows), refs[k // 2][at : at + rows])
        total = part if total is None else total + part
    return total


def turned_grad_kernel(count, place_ref, *refs):
    lefts, rights, out = refs[:count], refs[count : count + 2], refs[count + 2]
    at = 0
    for ref in lefts:
        size = ref.shape[0]
        out[:, at : at + size] = tokens_product(place_ref, ref, rights).T.astype(BF)
        at += size


def turned_grad(order, places, lefts, x0, x1, name):
    d, columns = x0.shape[1], sum(left.shape[0] for left in lefts)
    arrays = (*lefts, x0, x1)
    return order.call(
        functools.partial(turned_grad_kernel, len(lefts)), name, 26, arrays, wholes(arrays),
        [full((d, columns))], like((d, columns, BF)), prefetch=(places,),
    )[0]


def row_inverse(values):
    return lax.rsqrt(jnp.mean(values * values, axis=-1, keepdims=True) + EPS)


def first_norm_kernel(a_ref, b_ref, g_ref, o_ref, h_ref, copy_ref):
    def run(ref):
        hidden = ref[...].astype(F32)
        h_ref[...] = ref[...]
        o_ref[...] = (hidden * row_inverse(hidden)).astype(BF)

    near = pl.program_id(0) < pl.num_programs(0) // 2
    pl.when(near)(lambda: run(a_ref))
    pl.when(jnp.logical_not(near))(lambda: run(b_ref))
    pl.when(near)(lambda: copy_ref.__setitem__(..., g_ref[...]))


def first_norm(order, a, b, g):
    rows, d = a.shape
    block = min(128, rows)
    steps = rows // block
    near = pl.BlockSpec((block, d), lambda i: (jnp.minimum(i, steps - 1), 0))
    each = pl.BlockSpec((block, d), lambda i: (i, 0))
    return order.call(
        first_norm_kernel, "first_norm", 10, (a, b, g),
        [near, pl.BlockSpec((block, d), lambda i: (jnp.maximum(i - steps, 0), 0)), near],
        [each, each, near], like((2 * rows, d, BF), (2 * rows, d, BF), (rows, d, BF)),
        grid=(2 * steps,), far=(0, 2),
    )


def join_kernel(a_ref, b_ref, o_ref):
    near = pl.program_id(0) < pl.num_programs(0) // 2
    pl.when(near)(lambda: o_ref.__setitem__(..., a_ref[...]))
    pl.when(jnp.logical_not(near))(lambda: o_ref.__setitem__(..., b_ref[...]))


def joined(order, kernel, name, a, b, count):
    rows, d = a.shape
    block = min(128, rows)
    steps = rows // block
    return order.call(
        kernel, name, 8, (a, b),
        [
            pl.BlockSpec((block, d), lambda i: (jnp.minimum(i, steps - 1), 0)),
            pl.BlockSpec((block, d), lambda i: (jnp.maximum(i - steps, 0), 0)),
        ],
        [pl.BlockSpec((block, d), lambda i: (i, 0))] * count, like(*[(2 * rows, d, BF)] * count),
        grid=(2 * steps,),
    )


def norm_kernel(h_ref, a_ref, b_ref, o_ref, resid_ref):
    resid = h_ref[...].astype(F32) + (a_ref[...].astype(F32) + b_ref[...].astype(F32))
    resid_ref[...] = resid.astype(BF)
    o_ref[...] = (resid * row_inverse(resid)).astype(BF)


def back_through_norm(scaled, values):
    inverse = row_inverse(values)
    inner = jnp.mean(scaled * values, axis=-1, keepdims=True)
    return inverse * scaled - values * (inverse * inverse * inverse * inner)


def norm_back_kernel(a_ref, g_ref, resid_ref, b_ref, o_ref):
    scaled = a_ref[...].astype(F32) + b_ref[...].astype(F32)
    back = back_through_norm(scaled, resid_ref[...].astype(F32))
    o_ref[...] = (g_ref[...].astype(F32) + back).astype(BF)


def output_kernel(resid_ref, a_ref, b_ref, c_ref, o_ref):
    total = a_ref[...].astype(F32) + b_ref[...].astype(F32) + c_ref[...].astype(F32)
    o_ref[...] = (resid_ref[...].astype(F32) + total).astype(BF)


def hidden_grad_kernel(grad_ref, h_ref, a_ref, b_ref, c_ref, o_ref):
    scaled = a_ref[...].astype(F32) + b_ref[...].astype(F32) + c_ref[...].astype(F32)
    grad = grad_ref[...].astype(F32) + back_through_norm(scaled, h_ref[...].astype(F32))
    o_ref[...] = grad.astype(BF)


def plus_kernel(a_ref, b_ref, o_ref):
    o_ref[...] = (a_ref[...].astype(F32) + b_ref[...].astype(F32)).astype(BF)


def by_rows(order, kernel, name, rows, arrays, outs, first=None, far=(), far_out=()):
    d = arrays[0].shape[1]
    block = min(128, rows)
    first = first or [0] * len(arrays)

    def spec(array, start):
        count = array.shape[0] // block
        skip = start // block
        return pl.BlockSpec((block, d), lambda i: (lax.rem(i + skip, count), 0))

    return order.call(
        kernel, name, 12, arrays, [spec(a, start) for a, start in zip(arrays, first)],
        [pl.BlockSpec((block, d), lambda i: (i, 0))] * len(outs),
        like(*[(rows, d, dtype) for dtype in outs]), grid=(rows // block,), far=far,
        far_out=far_out,
    )


def add_kernel(index_ref, left_chunk, right_chunk, left_ref, right_ref, to_right, to_left):
    columns, cut = to_right.shape[1], left_ref.shape[1]
    to_right[:, :cut] = (left_chunk[:, :cut].astype(F32) + left_ref[...].astype(F32)).astype(BF)
    if cut < columns:
        to_right[:, cut:] = left_chunk[:, cut:]
    cut = columns - right_ref.shape[1]
    to_left[:, cut:] = (right_chunk[:, cut:].astype(F32) + right_ref[...].astype(F32)).astype(BF)
    if cut > 0:
        to_left[:, :cut] = right_chunk[:, :cut]


def add_chunks(order, whole, rows, start, width, first, second, from_left, from_right):
    chunk = lambda k: pl.BlockSpec((rows, width), lambda i, index: (index[k], start // width))
    return order.call(
        add_kernel, "add_chunks", 10, (whole, whole, from_left, from_right),
        [chunk(0), chunk(1), *wholes((from_left, from_right))], [full((rows, width))] * 2,
        like((rows, width, BF), (rows, width, BF)),
        prefetch=(jnp.stack([first, second]).astype(jnp.int32),),
    )


def arrived_sum(chunk_ref, lefts, rights):
    left = jnp.concatenate([ref[...].astype(F32) for ref in lefts], axis=1)
    right = jnp.concatenate([ref[...].astype(F32) for ref in rights], axis=1)
    return chunk_ref[...].astype(F32) + left + right


def finish_kernel(parts, widths, index_ref, chunk_ref, *refs):
    grad = arrived_sum(chunk_ref, refs[:parts], refs[parts : 2 * parts])
    gain_ref, refs = refs[2 * parts], refs[2 * parts + 1 :]
    weights, outs = refs[: len(widths)], refs[len(widths) :]
    gain, total, at = column(gain_ref[...]), None, 0
    for k, width in enumerate(widths):
        part = grad[:, at : at + width]
        term = jnp.sum(part * weights[k][...].astype(F32), axis=1, keepdims=True)
        total = term if total is None else total + term
        outs[k][...] = part * gain
        at += width
    outs[-1][...] = jnp.broadcast_to(total, (total.shape[0], 128)).T[:1]


def finish(order, whole, rows, own, lefts, rights, gain, weights):
    columns = whole.shape[1]
    widths = tuple(w.shape[1] for w in weights)
    return order.call(
        functools.partial(finish_kernel, len(lefts), widths), "finish", 16,
        (whole, *lefts, *rights, gain, *weights),
        [
            pl.BlockSpec((rows, columns), lambda i, index: (index[0], 0)),
            *wholes((*lefts, *rights, gain, *weights)),
        ],
        [*wholes(weights), full((1, rows))],
        like(*[(*w.shape, F32) for w in weights], (1, rows, F32)),
        prefetch=(own[None].astype(jnp.int32),), far=range(1 + 2 * len(lefts), 2 + 2 * len(lefts) + len(weights)),
        far_out=range(len(weights)),
    )


def finish_plain_kernel(parts, index_ref, chunk_ref, *refs):
    refs[-1][...] = arrived_sum(chunk_ref, refs[:parts], refs[parts : 2 * parts])


def finish_plain(order, whole, rows, own, lefts, rights):
    columns = whole.shape[1]
    return order.call(
        functools.partial(finish_plain_kernel, len(lefts)), "finish_plain", 12,
        (whole, *lefts, *rights),
        [
            pl.BlockSpec((rows, columns), lambda i, index: (index[0], 0)),
            *wholes((*lefts, *rights)),
        ],
        [full((rows, columns))], like((rows, columns, F32)),
        prefetch=(own[None].astype(jnp.int32),), far_out=(0,),
    )[0]


class Ring:
    def __init__(self, count):
        self.count = count
        self.half = count // 2
        order = [2 * k if k < self.half else 2 * (count - 1 - k) + 1 for k in range(count)]
        self.right = [(order[k], order[(k + 1) % count]) for k in range(count)]
        self.left = [(b, a) for a, b in self.right]
        me = lax.axis_index("dp")
        self.place = jnp.where(me % 2 == 0, me // 2, count - 1 - me // 2)

    def index(self, offset):
        place = (self.place + offset + self.count) % self.count
        return jnp.where(place < self.half, 2 * place, 2 * (self.count - 1 - place) + 1)

    def go_right(self, value):
        return lax.ppermute(value, "dp", self.right)

    def go_left(self, value):
        return lax.ppermute(value, "dp", self.left)


def cut_of(columns):
    return max(128, (columns // 2 + 127) // 128 * 128)


class Kept:
    def __init__(self, order, ring, parts):
        self.order, self.ring = order, ring
        self.parts, self.rows = parts, sum(part.shape[0] for part in parts)
        self.pieces, self.whole = [], None

    def put(self, which, offset, first, piece):
        skip = self.parts[0].shape[0] * which
        self.pieces.append((self.ring.index(offset) * self.rows + skip, first, piece))

    def finish(self):
        count, columns = self.ring.count * self.rows, self.parts[0].shape[1]
        self.whole = assemble(self.order, count, columns, *zip(*self.pieces))


class Gather:
    def __init__(self, kept, which):
        self.kept, self.order, self.ring, self.rounds = kept, kept.order, kept.ring, 1
        self.which = which
        shard = relay(self.order, kept.parts[which])[0]
        kept.put(which, 0, 0, shard)
        self.cut = cut_of(shard.shape[1])
        self.flying = self.ring.go_right(shard), self.ring.go_left(shard)

    def wait(self):
        while self.rounds < self.ring.half - 3:
            self.wait_one()
        self.wait_one()

    def wait_one(self):
        arrived = self.order.wait(*self.flying)
        last = self.rounds == self.ring.half
        if not last:
            arrived = relay(self.order, *arrived)
        self.kept.put(self.which, -self.rounds, 0, arrived[0])
        self.kept.put(self.which, self.rounds, self.cut if last else 0, arrived[1])
        self.rounds += 1
        if self.rounds == self.ring.half:
            arrived = halves(self.order, *arrived, self.cut)
        if not last:
            self.flying = self.ring.go_right(arrived[0]), self.ring.go_left(arrived[1])


class Turns:
    def __init__(self, make):
        self.make, self.ring = make, None

    def start(self):
        self.ring = self.make()

    def wait(self):
        self.ring.wait()


class Scatter:
    def __init__(self, order, ring, whole, first, width):
        self.order, self.ring, self.whole = order, ring, whole
        self.first, self.width = first, width
        self.rows = whole.shape[0] // ring.count
        self.steps = ring.half - 1
        right, left = far_chunk(
            order, whole, self.rows, first, width, ring.index(ring.half), cut_of(width)
        )
        self.flying = ring.go_right(right), ring.go_left(left)

    def wait(self):
        while self.steps > 3:
            self.wait_one()
        self.wait_one()

    def wait_one(self):
        step = self.steps
        right, left = add_chunks(
            self.order, self.whole, self.rows, self.first, self.width, self.ring.index(step),
            self.ring.index(-step), *self.order.wait(*self.flying),
        )
        self.steps -= 1
        self.flying = self.ring.go_right(right), self.ring.go_left(left)

    def last(self):
        while self.steps:
            self.wait_one()
        return self.order.wait(*self.flying)


def scaled_sum(sums, gain, weights):
    arrived = [part.last() for part in sums]
    part = sums[0]
    return finish(
        part.order, part.whole, part.rows, part.ring.index(0), [a for a, _ in arrived],
        [b for _, b in arrived], gain, weights,
    )


def plain_sum(sums):
    arrived = [part.last() for part in sums]
    part = sums[0]
    return finish_plain(
        part.order, part.whole, part.rows, part.ring.index(0), [a for a, _ in arrived],
        [b for _, b in arrived],
    )


def swap_core(value):
    return lax.ppermute(value, "tensor", CORE_PAIRS)


def swap_x(value):
    return lax.ppermute(value, "tensor", X_PAIRS)


def plus(order, left_side, right_side, rows, first=0):
    arrays = (left_side, right_side)
    return by_rows(order, plus_kernel, "plus", rows, arrays, (BF,), (first, first))[0]


def per_device(
    dp_count,
    hidden_in,
    segments,
    attn_gain,
    w_query,
    w_key,
    w_value,
    w_out,
    mlp_gain,
    w_gate,
    w_up,
    w_down,
    cotangent,
):
    ring = Ring(dp_count)
    device = lax.axis_index("tensor").astype(jnp.int32)
    places = jnp.stack([device, device ^ 2, device ^ 1, device ^ 3])
    rows = hidden_in.shape[0]
    both = 2 * rows
    query_columns = w_query.shape[1]
    heads = query_columns // HD, w_key.shape[1] // HD
    units = w_gate.shape[1]
    block = units // 2
    order = Order()
    v = types.SimpleNamespace()

    def go(value):
        return relay(order, value)[0]

    A = Turns(lambda: Gather(v.A, 0))
    B = Turns(lambda: Gather(v.B, 0))
    C = Turns(lambda: Gather(v.C, 0))
    D = Turns(lambda: Scatter(order, ring, v.down_grad, 0, units))
    G = Turns(lambda: Scatter(order, ring, v.gate_up_grad, 0, units))
    U = Turns(lambda: Scatter(order, ring, v.gate_up_grad, units, units))
    Q = Turns(lambda: Scatter(order, ring, v.qkv_grad, 0, 2 * query_columns))
    O = Turns(lambda: Scatter(order, ring, v.out_grad, 0, query_columns))

    def A_keep():
        v.A.finish()

    def B_keep():
        v.B.finish()

    def C_keep():
        v.C.finish()

    def shard_a():
        weights = [w_query, w_key, w_value]
        shard = make_shard(order, attn_gain, weights, [w_out.T], "attn_shard", 14, False)
        v.A = Kept(order, ring, shard)

    def shard_b():
        shard = make_shard(order, mlp_gain, [w_gate, w_up], [], "gate_up_shard", 14, False)
        v.B = Kept(order, ring, shard)

    def shard_c():
        shard = make_shard(order, mlp_gain, [], [w_down.T], "down_shard", 8, False)
        v.C = Kept(order, ring, shard)

    def hidden_x():
        v.hidden_across = swap_x(hidden_in)

    def tables():
        v.cos, v.sin, v.start = rope_tables(order, segments)

    def norm_one():
        order.wait(v.hidden_across)
        v.normed, v.hidden, v.grads_own = first_norm(
            order, hidden_in, v.hidden_across, cotangent
        )

    def normed_core():
        v.normed = go(v.normed)
        v.normed_other = swap_core(v.normed)

    def grads_x():
        v.grads_own = go(v.grads_own)
        v.grads_across = swap_x(v.grads_own)

    def qkv():
        order.wait(v.normed_other)
        v.qkv = project(
            order, places, v.normed, v.normed_other, v.A.whole, v.cos, v.sin, *heads
        )

    def grads_join():
        order.wait(v.grads_across)
        v.grads = joined(order, join_kernel, "join", cotangent, v.grads_across, 1)[0]

    def grads_core():
        v.grads = go(v.grads)
        v.grads_other = swap_core(v.grads)

    def attention():
        v.heads_out, v.log_total = attend(order, v.qkv, v.start, *heads, rows)

    def out_part():
        v.part, v.part_other = branch(order, places, v.heads_out, v.A.whole)

    def part_core():
        v.part_other = go(v.part_other)
        v.part_core = swap_core(v.part_other)

    def part_x():
        order.wait(v.part_core)
        v.chip = plus(order, v.part, v.part_core, both)
        v.across = swap_x(v.chip)

    def norm_two():
        order.wait(v.across)
        v.normed_two, v.resid = by_rows(
            order, norm_kernel, "norm", both, (v.hidden, v.chip, v.across), (BF, BF),
            (0, 0, rows),
        )

    def normed_two_core():
        v.normed_two = go(v.normed_two)
        v.normed_two_other = swap_core(v.normed_two)

    def mlp_mine():
        v.act, v.da, v.db = gate_up(order, v.normed_two, v.B.whole, block)

    def mlp_other():
        order.wait(v.normed_two_other)
        v.act_other, v.da_other, v.db_other = gate_up(
            order, v.normed_two_other, v.B.whole, block
        )

    def grad_down():
        order.wait(v.grads_other)
        v.down_grad = weight_grad(
            order, v.grads, v.grads_other, v.act[None], v.act_other[None], block
        )

    def down_mine():
        v.down = down(order, v.act, v.C.whole, 512)

    def down_other():
        v.down_other = down(order, v.act_other, v.C.whole, 512)

    def down_core():
        v.down_other = go(v.down_other)
        v.down_core = swap_core(v.down_other)

    def down_x():
        order.wait(v.down_core)
        v.down_theirs = swap_x(plus(order, v.down, v.down_core, rows, rows))

    def finish_output():
        order.wait(v.down_theirs)
        arrays = (v.resid, v.down, v.down_core, v.down_theirs)
        v.output = by_rows(
            order, output_kernel, "output", rows, arrays, (BF,), far=range(4), far_out=(0,)
        )[0]

    def back_mine():
        v.scaled, v.d = mlp_back(
            order, v.grads, v.da, v.db, v.C.whole, v.B.whole, block
        )

    def back_other():
        v.scaled_other, v.d_other = mlp_back(
            order, v.grads_other, v.da_other, v.db_other, v.C.whole, v.B.whole, block
        )

    def scaled_core():
        v.scaled_other = go(v.scaled_other)
        v.scaled_core = swap_core(v.scaled_other)

    def scaled_x():
        order.wait(v.scaled_core)
        v.chip_back = plus(order, v.scaled, v.scaled_core, both)
        v.across_back = swap_x(v.chip_back)

    def grad_gate_up():
        v.gate_up_grad = weight_grad(
            order, v.normed_two, v.normed_two_other, v.d, v.d_other, block
        )

    def norm_two_back():
        order.wait(v.across_back)
        v.branch = by_rows(
            order, norm_back_kernel, "norm_back", both,
            (v.chip_back, v.grads, v.resid, v.across_back), (BF,), (0, 0, 0, rows),
        )[0]

    def branch_core():
        v.branch = go(v.branch)
        v.branch_other = swap_core(v.branch)

    def heads_back():
        order.wait(v.branch_other)
        v.grad_heads = grad_heads(
            order, places, v.branch, v.branch_other, v.A.whole, query_columns
        )

    def attention_back():
        v.dq, v.dk, v.dv = attend_back(
            order, v.qkv, v.grad_heads, v.heads_out, v.log_total, v.start, v.cos,
            v.sin, *heads, rows,
        )

    def grad_out():
        v.out_grad = turned_grad(
            order, places, [v.heads_out], v.branch, v.branch_other, "out_grad"
        )

    def grad_qkv():
        v.qkv_grad = turned_grad(
            order, places, [v.dq, v.dk, v.dv], v.normed, v.normed_other, "qkv_grad"
        )

    def grad_hidden():
        v.u, v.u_other = grad_x(order, places, v.dq, v.dk, v.dv, v.A.whole)

    def u_core():
        v.u_other = go(v.u_other)
        v.u_core = swap_core(v.u_other)

    def u_x():
        order.wait(v.u_core)
        v.u_theirs = swap_x(plus(order, v.u, v.u_core, rows, rows))

    def finish_hidden():
        order.wait(v.u_theirs)
        arrays = (v.branch, hidden_in, v.u, v.u_core, v.u_theirs)
        v.hidden_grad = by_rows(
            order, hidden_grad_kernel, "hidden_grad", rows, arrays, (BF,), far=range(5),
            far_out=(0,),
        )[0]

    def finish_down():
        v.down_w = plain_sum([D.ring])

    def finish_gate_up():
        sums = [G.ring, U.ring]
        v.gate_w, v.up_w, v.gain_two = scaled_sum(sums, mlp_gain, [w_gate, w_up])

    def finish_qkv():
        v.query_w, v.key_w, v.value_w, v.gain_one = scaled_sum(
            [Q.ring], attn_gain, [w_query, w_key, w_value]
        )

    def finish_out():
        v.out_w = plain_sum([O.ring])

    def wait_g():
        order.wait(*G.ring.flying)

    def wait_u():
        order.wait(*U.ring.flying)

    schedule = (
        shard_a, A.start, shard_b, B.start, A.wait, shard_c, C.start, hidden_x, tables,
        norm_one, normed_core, B.wait, A.wait, A.wait, C.wait, A.wait, grads_x, A_keep, qkv,
        attention, out_part, grads_join, B.wait, part_core, part_x, B.wait, B.wait, C.wait,
        B_keep, norm_two, normed_two_core, mlp_mine, C.wait, grads_core, mlp_other, grad_down,
        C.wait, C_keep, back_other, D.start, scaled_core, back_mine, D.wait, scaled_x,
        grad_gate_up, G.start, U.start, D.wait, G.wait, down_mine, U.wait, down_other,
        down_core, G.wait, norm_two_back, U.wait, branch_core, heads_back, attention_back,
        D.wait, grad_qkv, G.wait, grad_out, finish_down, Q.start, down_x, O.start, grad_hidden,
        U.wait, Q.wait, O.wait, u_core, u_x, Q.wait, O.wait, finish_gate_up, finish_output,
        Q.wait, wait_u, finish_qkv, O.wait, wait_g, finish_hidden, finish_out,
    )
    for run in schedule:
        run()
    gains = lax.psum(jnp.concatenate([v.gain_one, v.gain_two], axis=0), "tensor")
    return (
        v.output,
        v.hidden_grad,
        gains[0],
        v.query_w,
        v.key_w,
        v.value_w,
        v.out_w.T,
        gains[1],
        v.gate_w,
        v.up_w,
        v.down_w.T,
    )


def solution(mesh):
    tokens, split = P(("dp", "tensor"), None), P("dp", "tensor")
    in_specs = (
        tokens, P("dp"), P("dp"), split, split, split, P("tensor", "dp"),
        P("dp"), split, split, P("tensor", "dp"), tokens,
    )
    out_specs = (
        tokens, tokens, P("dp"), split, split, split, P("tensor", "dp"),
        P("dp"), split, split, P("tensor", "dp"),
    )
    body = functools.partial(per_device, mesh.shape["dp"])
    return jax.shard_map(body, mesh=mesh, in_specs=in_specs, out_specs=out_specs, check_vma=False)
```

```python
import functools
import math
import types

import jax
import jax.numpy as jnp
from jax import lax
from jax.experimental import pallas as pl
from jax.experimental.pallas import tpu as pltpu
from jax.sharding import PartitionSpec as P

HD = 96
HALF = HD // 2
DOCUMENTS = 5
EPS = 1e-05
NEG = -1e30
THETA = 100000.0
SCALE = HD ** (-0.5)
LOG2E = math.log2(math.e)
BF = jnp.bfloat16
F32 = jnp.float32
MIB = 1024 * 1024

CORE_PAIRS = [(0, 1), (1, 0), (2, 3), (3, 2)]
X_PAIRS = [(0, 2), (2, 0), (1, 3), (3, 1)]


def dot(left_side, right_side):
    return jnp.dot(left_side, right_side, preferred_element_type=F32)


def dot_nt(left_side, right_side):
    return lax.dot_general(
        left_side, right_side, (((1,), (1,)), ((), ())), preferred_element_type=F32
    )


def turned(value):
    return value.astype(F32).T


class Order:
    def __init__(self):
        self.waited, self.token = [], None

    def wait(self, *values):
        self.waited += values
        return values[0] if len(values) == 1 else values

    def call(
        self, body, name, mib, args, in_specs, out_specs, out_shape, grid=(1,), scratch=(),
        prefetch=(), aliases=None, far=(), near=(), far_out=(), near_out=(),
    ):
        seen = [a for a in self.waited if not any(a is b for b in args)]
        if self.token is not None:
            seen.append(pltpu.with_memory_space_constraint(self.token, pltpu.HBM))
        first, extra, count = len(prefetch) + len(args), len(seen), len(out_shape)
        args = list(args)
        for k in far:
            args[k] = pltpu.with_memory_space_constraint(args[k], pltpu.HBM)
        for k in near:
            args[k] = pltpu.with_memory_space_constraint(args[k], pltpu.VMEM)
        out_shape = list(out_shape)
        for k in far_out:
            out_shape[k] = pltpu.HBM(out_shape[k].shape, out_shape[k].dtype)
        for k in near_out:
            out_shape[k] = pltpu.VMEM(out_shape[k].shape, out_shape[k].dtype)

        def kernel(*refs):
            outs = refs[first + extra :]
            body(*refs[:first], *outs[:count], *outs[count + 1 :])

        *out, self.token = pl.pallas_call(
            kernel,
            grid_spec=pltpu.PrefetchScalarGridSpec(
                num_scalar_prefetch=len(prefetch),
                grid=grid,
                in_specs=[*in_specs, *[ANY] * extra],
                out_specs=[*out_specs, ANY],
                scratch_shapes=scratch,
            ),
            out_shape=[*out_shape, pltpu.HBM((8, 128), F32)],
            input_output_aliases=aliases or {},
            compiler_params=pltpu.CompilerParams(vmem_limit_bytes=mib * MIB),
            cost_estimate=pl.CostEstimate(flops=0, bytes_accessed=0, transcendentals=0),
            name=name,
        )(*prefetch, *args, *seen)
        self.waited = []
        return out


def full(shape):
    return pl.BlockSpec(tuple(shape), lambda *_: (0,) * len(shape))


def wholes(arrays):
    return [full(a.shape) for a in arrays]


def like(*shapes):
    return [jax.ShapeDtypeStruct(shape, dtype) for *shape, dtype in shapes]


ANY = pl.BlockSpec(memory_space=pl.ANY)
HBM = pl.BlockSpec(memory_space=pltpu.HBM)
VMEM = pl.BlockSpec(memory_space=pltpu.VMEM)


def column(row):
    return jnp.broadcast_to(row.astype(F32)[None], (8, row.shape[0])).T[:, :1]


def put(outs, first, value):
    top, width = outs[0].shape[0], value.shape[1]
    outs[0][:, first : first + width] = value[:top]
    if len(outs) > 1:
        outs[1][:, first : first + width] = value[top:]


def shard_kernel(scaled, plain, gain_ref, *refs):
    gain, first = column(gain_ref[...]), 0
    inputs, outs = refs[: scaled + plain], refs[scaled + plain :]
    for k, ref in enumerate(inputs):
        value = (ref[...].astype(F32) * gain).astype(BF) if k < scaled else ref[...]
        put(outs, first, value)
        first += ref.shape[1]


def top_of(rows):
    return (rows // 2 + 15) // 16 * 16


def make_shard(order, gain, scaled, plain, name, mib, split):
    rows = (*scaled, *plain)[0].shape[0]
    columns = sum(w.shape[1] for w in (*scaled, *plain))
    top = top_of(rows) if split else rows
    shapes = [(count, columns) for count in (top, rows - top) if count]
    return order.call(
        functools.partial(shard_kernel, len(scaled), len(plain)), name, mib,
        (gain, *scaled, *plain), wholes((gain, *scaled, *plain)), [full(shape) for shape in shapes],
        like(*[(*shape, BF) for shape in shapes]), far=range(1, 1 + len(scaled) + len(plain)),
    )


def relay_kernel(*refs):
    pass


def relay(order, *values):
    count = len(values)
    return order.call(
        relay_kernel, "relay", 2, values, [ANY] * count, [ANY] * count,
        like(*[(*value.shape, value.dtype) for value in values]),
        aliases={k: k for k in range(count)},
    )


def assemble_kernel(spans, place_ref, *refs):
    pieces, whole, sems = refs[: len(spans)], refs[len(spans)], refs[len(spans) + 1]
    copies = []
    for k, (first, width) in enumerate(spans):
        at = pl.multiple_of(place_ref[k], 16)
        where = whole.at[pl.ds(at, pieces[k].shape[0]), pl.ds(first, width)]
        copies.append(pltpu.make_async_copy(pieces[k], where, sems.at[k]))
    for copy in copies:
        copy.start()
    for copy in copies:
        copy.wait()


def assemble(order, rows, columns, places, firsts, pieces):
    count = len(pieces)
    spans = tuple((first, piece.shape[1]) for first, piece in zip(firsts, pieces))
    return order.call(
        functools.partial(assemble_kernel, spans), "assemble", 2, pieces, [ANY] * count, [VMEM],
        like((rows, columns, BF)), scratch=[pltpu.SemaphoreType.DMA((count,))],
        prefetch=(jnp.stack(places).astype(jnp.int32),), far=range(count), near_out=(0,),
    )[0]


def halves_kernel(cut, a_ref, b_ref, c_ref, d_ref):
    c_ref[...] = a_ref[:, :cut]
    d_ref[...] = b_ref[:, cut:]


def halves(order, right, left, cut):
    rows, columns = right.shape
    shapes = (rows, cut), (rows, columns - cut)
    return order.call(
        functools.partial(halves_kernel, cut), "halves", 6, (right, left), wholes((right, left)),
        [full(shape) for shape in shapes], like(*[(*shape, BF) for shape in shapes]),
    )


def far_kernel(cut, index_ref, chunk_ref, c_ref, d_ref):
    c_ref[...] = chunk_ref[:, :cut]
    d_ref[...] = chunk_ref[:, cut:]


def far_chunk(order, whole, rows, first, width, index, cut):
    shapes = (rows, cut), (rows, width - cut)
    return order.call(
        functools.partial(far_kernel, cut), "far_chunk", 8, (whole,),
        [pl.BlockSpec((rows, width), lambda i, index: (index[0], first // width))],
        [full(shape) for shape in shapes], like(*[(*shape, BF) for shape in shapes]),
        prefetch=(index[None].astype(jnp.int32),),
    )


def tables_kernel(segment_ref, c_ref, s_ref, opening_ref):
    segment = segment_ref[...]
    opening = jnp.zeros_like(segment)
    for number in range(DOCUMENTS - 1):
        count = jnp.sum((segment == number).astype(jnp.int32), axis=1, keepdims=True)
        opening += jnp.where(segment > number, count, 0)
    position = (lax.broadcasted_iota(jnp.int32, segment.shape, 1) - opening).astype(F32)
    place = lax.broadcasted_iota(jnp.int32, c_ref.shape, 0).astype(F32)
    angle = jnp.exp(-(2.0 * place / HD) * math.log(THETA)) * position
    c_ref[...] = jnp.cos(angle)
    s_ref[...] = jnp.sin(angle)
    opening_ref[...] = opening


def rope_tables(order, segments):
    n = segments.shape[0]
    shapes = (HALF, n), (HALF, n), (1, n)
    return order.call(
        tables_kernel, "rope_tables", 8, (segments[None],), [full((1, n))],
        [full(shape) for shape in shapes],
        like((HALF, n, F32), (HALF, n, F32), (1, n, jnp.int32)),
    )


def rope_rows(values, cosine, sine):
    first, second = values[:HALF], values[HALF:]
    return first * cosine - second * sine, second * cosine + first * sine


def project_kernel(query_heads, key_heads, place_ref, x0_ref, x1_ref, w_ref, c_ref, s_ref, o_ref):
    def run(x_ref):
        turned_heads = dot(x_ref[...], w_ref[...]).T
        cosine, sine = c_ref[...], s_ref[...]
        for h in range(query_heads + key_heads):
            first, second = rope_rows(turned_heads[h * HD : (h + 1) * HD], cosine, sine)
            if h < query_heads:
                first, second = first * (SCALE * LOG2E), second * (SCALE * LOG2E)
            o_ref[h * HD : h * HD + HALF, :] = first.astype(BF)
            o_ref[h * HD + HALF : (h + 1) * HD, :] = second.astype(BF)
        done = (query_heads + key_heads) * HD
        o_ref[done:, :] = turned_heads[done:].astype(BF)

    pl.when(pl.program_id(0) < 2)(lambda: run(x0_ref))
    pl.when(pl.program_id(0) >= 2)(lambda: run(x1_ref))


def project(order, places, x0, x1, w, cosine, sine, query_heads, key_heads):
    block, d = x0.shape[0] // 2, x0.shape[1]
    columns = (query_heads + 2 * key_heads) * HD
    table = pl.BlockSpec((HALF, block), lambda i, place: (0, place[i]))
    return order.call(
        functools.partial(project_kernel, query_heads, key_heads), "project", 18,
        (x0, x1, w, cosine, sine),
        [
            pl.BlockSpec((block, d), lambda i, place: (jnp.minimum(i, 1), 0)),
            pl.BlockSpec((block, d), lambda i, place: (jnp.maximum(i - 2, 0), 0)),
            full((d, columns)),
            table,
            table,
        ],
        [pl.BlockSpec((columns, block), lambda i, place: (0, place[i]))],
        like((columns, 4 * block, BF)), grid=(4,), prefetch=(places,),
    )[0]


def side(ref, low, high):
    return jnp.concatenate(
        [ref[h * HD : (h + 1) * HD, low:high] for h in range(ref.shape[0] // HD)], axis=1
    )


def attend_kernel(block, q_ref, k_ref, v_ref, start_ref, o_ref, l_ref):
    n, group = q_ref.shape[1], q_ref.shape[0] // HD
    keys = turned(k_ref[...]).astype(BF)
    row = lax.broadcasted_iota(jnp.int32, (block, group * block), 0)
    column = lax.broadcasted_iota(jnp.int32, (block, group * block), 1) % block
    for i in range(n // block):
        low, high = i * block, (i + 1) * block
        start = jnp.concatenate([start_ref[:, low:high]] * group, axis=1)
        scores = dot(keys[:high], side(q_ref, low, high))
        at = lax.broadcasted_iota(jnp.int32, (high, group * block), 0)
        scores = jnp.where(at >= start, scores, NEG)
        near = jnp.where(row <= column, scores[low:], NEG)
        top = jnp.max(near, axis=0, keepdims=True)
        if i:
            top = jnp.maximum(top, jnp.max(scores[:low], axis=0, keepdims=True))
        near = jnp.exp2(near - top)
        total = jnp.sum(near, axis=0, keepdims=True)
        out = dot(v_ref[:, low:high], near.astype(BF))
        if i:
            far = jnp.exp2(scores[:low] - top)
            total = total + jnp.sum(far, axis=0, keepdims=True)
            out = out + dot(v_ref[:, :low], far.astype(BF))
        out = out * (1.0 / total)
        log_total = top + jnp.log2(total)
        for h in range(group):
            part = slice(h * block, (h + 1) * block)
            o_ref[h * HD : (h + 1) * HD, low:high] = out[:, part].astype(BF)
            l_ref[0, h : h + 1, low:high] = log_total[:, part]


def attend(order, qkv, start, query_heads, key_heads, block):
    n, group = qkv.shape[1], query_heads // key_heads
    return order.call(
        functools.partial(attend_kernel, block), "attend", 16, (qkv, qkv, qkv, start),
        [
            pl.BlockSpec((group * HD, n), lambda i: (i, 0)),
            pl.BlockSpec((HD, n), lambda i: (query_heads + i, 0)),
            pl.BlockSpec((HD, n), lambda i: (query_heads + key_heads + i, 0)),
            full((1, n)),
        ],
        [
            pl.BlockSpec((group * HD, n), lambda i: (i, 0)),
            pl.BlockSpec((1, group, n), lambda i: (i, 0, 0)),
        ],
        like((query_heads * HD, n, BF), (key_heads, group, n, F32)), grid=(key_heads,),
    )


def attend_back_kernel(
    block, q_ref, k_ref, v_ref, g_ref, h_ref, l_ref, start_ref, c_ref, s_ref,
    dq_ref, dk_ref, dv_ref, dk_sum, dv_sum,
):
    n, group = q_ref.shape[1], q_ref.shape[0] // HD
    keys = turned(k_ref[...]).astype(BF)
    values = turned(v_ref[...]).astype(BF)
    dk_sum[...] = jnp.zeros_like(dk_sum)
    dv_sum[...] = jnp.zeros_like(dv_sum)
    for i in range(n // block):
        low, high = i * block, (i + 1) * block
        queries, grads = side(q_ref, low, high), side(g_ref, low, high)
        outs = side(h_ref, low, high)
        query_rows, grad_rows = turned(queries).astype(BF), turned(grads).astype(BF)
        inner = jnp.sum(grads.astype(F32) * outs.astype(F32), axis=0, keepdims=True)
        log_total = jnp.concatenate([l_ref[0, h : h + 1, low:high] for h in range(group)], axis=1)
        start = jnp.concatenate([start_ref[:, low:high]] * group, axis=1)
        dq = jnp.zeros((HD, group * block), F32)
        for first, last in ([(0, low)] if i else []) + [(low, high)]:
            scores = dot(keys[first:last], queries)
            at = lax.broadcasted_iota(jnp.int32, scores.shape, 0) + first
            allowed = at >= start
            if first == low:
                column = lax.broadcasted_iota(jnp.int32, scores.shape, 1) % block + low
                allowed = allowed & (at <= column)
            probs = jnp.exp2(jnp.where(allowed, scores - log_total, NEG))
            dp = dot(values[first:last], grads)
            ds = (probs * (dp - inner)).astype(BF)
            dv_sum[first:last, :] += dot(probs.astype(BF), grad_rows)
            dk_sum[first:last, :] += dot(ds, query_rows)
            dq = dq + dot(k_ref[:, first:last], ds)
        dq = dq * SCALE
        cosine, sine = c_ref[:, low:high], s_ref[:, low:high]
        for h in range(group):
            top, bottom = rope_rows(dq[:, h * block : (h + 1) * block], cosine, -sine)
            dq_ref[h * HD : h * HD + HALF, low:high] = top.astype(BF)
            dq_ref[h * HD + HALF : (h + 1) * HD, low:high] = bottom.astype(BF)
    top, bottom = rope_rows(dk_sum[...].T * (1.0 / LOG2E), c_ref[...], -s_ref[...])
    dk_ref[:HALF, :] = top.astype(BF)
    dk_ref[HALF:, :] = bottom.astype(BF)
    dv_ref[...] = dv_sum[...].T.astype(BF)


def attend_back(order, qkv, grads, heads_out, log_total, start, cosine, sine, query_heads, key_heads, block):
    n, group = qkv.shape[1], query_heads // key_heads
    wide = pl.BlockSpec((group * HD, n), lambda i: (i, 0))
    narrow = pl.BlockSpec((HD, n), lambda i: (i, 0))
    return order.call(
        functools.partial(attend_back_kernel, block), "attend_back", 20,
        (qkv, qkv, qkv, grads, heads_out, log_total, start, cosine, sine),
        [
            wide,
            pl.BlockSpec((HD, n), lambda i: (query_heads + i, 0)),
            pl.BlockSpec((HD, n), lambda i: (query_heads + key_heads + i, 0)),
            wide,
            wide,
            pl.BlockSpec((1, group, n), lambda i: (i, 0, 0)),
            full((1, n)),
            full((HALF, n)),
            full((HALF, n)),
        ],
        [wide, narrow, narrow],
        like((query_heads * HD, n, BF), (key_heads * HD, n, BF), (key_heads * HD, n, BF)),
        grid=(key_heads,), scratch=[pltpu.VMEM((n, HD), F32), pltpu.VMEM((n, HD), F32)],
    )


def columns_of(ref, place, block):
    return ref[:, pl.ds(pl.multiple_of(place * block, block), block)]


def branch_kernel(place_ref, h_ref, w_ref, *out_refs):
    rows = out_refs[0].shape[0] // 2
    for k in range(4):
        heads = turned(columns_of(h_ref, place_ref[k], rows)).astype(BF)
        at = (k % 2) * rows
        out_refs[k // 2][at : at + rows] = dot_nt(heads, w_ref[...]).astype(BF)


def branch(order, places, heads_out, w_full):
    (depth, n), d = heads_out.shape, w_full.shape[0]
    last = w_full.shape[1] // depth - 1
    return order.call(
        branch_kernel, "branch", 18, (heads_out, w_full),
        [full((depth, n)), pl.BlockSpec((d, depth), lambda i, place: (0, last))],
        [full((n // 2, d))] * 2, like((n // 2, d, BF), (n // 2, d, BF)), prefetch=(places,),
    )


def gate_up_kernel(x_ref, wg_ref, wu_ref, act_ref, a_ref, b_ref):
    gate, up = dot(x_ref[...], wg_ref[...]), dot(x_ref[...], wu_ref[...])
    sigmoid = 1.0 / (1.0 + jnp.exp(-gate))
    silu = gate * sigmoid
    act_ref[...] = (silu * up).astype(BF)
    a_ref[...] = (up * sigmoid * (1.0 + gate * (1.0 - sigmoid))).astype(BF)
    b_ref[...] = silu.astype(BF)


def gate_up(order, x, w, block):
    rows, d = x.shape
    units = w.shape[1] // 2
    steps = units // block
    return order.call(
        gate_up_kernel, "gate_up", 20, (x, w, w),
        [
            full((rows, d)),
            pl.BlockSpec((d, block), lambda j: (0, j)),
            pl.BlockSpec((d, block), lambda j: (0, j + steps)),
        ],
        [pl.BlockSpec((rows, block), lambda j: (0, j))] * 3, like(*[(rows, units, BF)] * 3),
        grid=(steps,),
    )


def mlp_back_kernel(g_ref, a_ref, b_ref, wd_ref, wg_ref, wu_ref, u_ref, d_ref, total):
    step, last = pl.program_id(0), pl.num_programs(0) - 1
    grad_act = dot(g_ref[...], wd_ref[...])
    d_ref[0] = (grad_act * a_ref[...].astype(F32)).astype(BF)
    d_ref[1] = (grad_act * b_ref[...].astype(F32)).astype(BF)
    part = dot_nt(d_ref[0], wg_ref[...]) + dot_nt(d_ref[1], wu_ref[...])

    @pl.when(step == 0)
    def _():
        total[...] = part

    @pl.when((step > 0) & (step < last))
    def _():
        total[...] += part

    @pl.when(step == last)
    def _():
        u_ref[...] = (total[...] + part).astype(BF)


def mlp_back(order, g, a, b, w_down, w, block):
    rows, d = g.shape
    units = a.shape[1]
    steps = units // block
    assert steps > 1
    narrow = pl.BlockSpec((rows, block), lambda j: (0, j))
    return order.call(
        mlp_back_kernel, "mlp_back", 28, (g, a, b, w_down, w, w),
        [
            full((rows, d)),
            narrow,
            narrow,
            pl.BlockSpec((d, block), lambda j: (0, j)),
            pl.BlockSpec((d, block), lambda j: (0, j)),
            pl.BlockSpec((d, block), lambda j: (0, j + steps)),
        ],
        [full((rows, d)), pl.BlockSpec((2, rows, block), lambda j: (0, 0, j))],
        like((rows, d, BF), (2, rows, units, BF)), grid=(steps,),
        scratch=[pltpu.VMEM((rows, d), F32)],
    )


def weight_grad_kernel(x0_ref, x1_ref, d0_ref, d1_ref, o_ref, x_turned):
    rows = x0_ref.shape[0]

    @pl.when(pl.program_id(0) == 0)
    def _():
        for k, ref in enumerate((x0_ref, x1_ref)):
            x_turned[:, k * rows : (k + 1) * rows] = turned(ref[...]).astype(BF)

    o_ref[...] = (
        dot(x_turned[:, :rows], d0_ref[0]) + dot(x_turned[:, rows:], d1_ref[0])
    ).astype(BF)


def weight_grad(order, x0, x1, d0, d1, block):
    rows, d = x0.shape
    parts, _, columns = d0.shape
    steps = columns // block
    narrow = pl.BlockSpec((1, rows, block), lambda j: (j // steps, 0, j % steps))
    return order.call(
        weight_grad_kernel, "weight_grad", 21, (x0, x1, d0, d1),
        [full((rows, d)), full((rows, d)), narrow, narrow],
        [pl.BlockSpec((d, block), lambda j: (0, j))], like((d, parts * columns, BF)),
        grid=(parts * steps,), scratch=[pltpu.VMEM((d, 2 * rows), BF)],
    )[0]


def down_kernel(act_ref, w_ref, o_ref):
    o_ref[...] = dot_nt(act_ref[...], w_ref[...]).astype(BF)


def down(order, act, w_down, block):
    rows, units = act.shape
    d = w_down.shape[0]
    return order.call(
        down_kernel, "down", 14, (act, w_down),
        [full((rows, units)), pl.BlockSpec((block, units), lambda j: (j, 0))],
        [pl.BlockSpec((rows, block), lambda j: (0, j))], like((rows, d, BF)), grid=(d // block,),
    )[0]


def grad_heads_kernel(place_ref, g0_ref, g1_ref, w_ref, o_ref):
    rows = g0_ref.shape[0] // 2
    for k in range(4):
        ref, low = (g0_ref, g1_ref)[k // 2], (k % 2) * rows
        at = pl.multiple_of(place_ref[k] * rows, rows)
        o_ref[:, pl.ds(at, rows)] = dot(ref[low : low + rows], w_ref[...]).T.astype(BF)


def grad_heads(order, places, g0, g1, w_full, depth):
    d, n = w_full.shape[0], 2 * g0.shape[0]
    last = w_full.shape[1] // depth - 1
    return order.call(
        grad_heads_kernel, "grad_heads", 16, (g0, g1, w_full),
        [*wholes((g0, g1)), pl.BlockSpec((d, depth), lambda i, place: (0, last))],
        [full((depth, n))], like((depth, n, BF)), prefetch=(places,),
    )[0]


def grad_x_kernel(place_ref, q_ref, k_ref, v_ref, w_ref, *out_refs):
    rows = out_refs[0].shape[0] // 2
    for k in range(4):
        parts = [columns_of(ref, place_ref[k], rows).astype(F32) for ref in (q_ref, k_ref, v_ref)]
        grads = jnp.concatenate(parts, axis=0).T.astype(BF)
        at = (k % 2) * rows
        out_refs[k // 2][at : at + rows] = dot_nt(grads, w_ref[...]).astype(BF)


def grad_x(order, places, dq, dk, dv, w_full):
    d, n = w_full.shape[0], dq.shape[1]
    return order.call(
        grad_x_kernel, "grad_x", 18, (dq, dk, dv, w_full),
        [*wholes((dq, dk, dv)), full((d, dq.shape[0] + dk.shape[0] + dv.shape[0]))],
        [full((n // 2, d))] * 2, like((n // 2, d, BF), (n // 2, d, BF)), prefetch=(places,),
    )


def tokens_product(place_ref, left_ref, refs):
    rows = refs[0].shape[0] // 2
    total = None
    for k in range(4):
        at = (k % 2) * rows
        part = dot(columns_of(left_ref, place_ref[k], rows), refs[k // 2][at : at + rows])
        total = part if total is None else total + part
    return total


def turned_grad_kernel(count, place_ref, *refs):
    lefts, rights, out = refs[:count], refs[count : count + 2], refs[count + 2]
    at = 0
    for ref in lefts:
        size = ref.shape[0]
        out[:, at : at + size] = tokens_product(place_ref, ref, rights).T.astype(BF)
        at += size


def turned_grad(order, places, lefts, x0, x1, name):
    d, columns = x0.shape[1], sum(left.shape[0] for left in lefts)
    arrays = (*lefts, x0, x1)
    return order.call(
        functools.partial(turned_grad_kernel, len(lefts)), name, 20, arrays, wholes(arrays),
        [full((d, columns))], like((d, columns, BF)), prefetch=(places,),
    )[0]


def row_inverse(values):
    return lax.rsqrt(jnp.mean(values * values, axis=-1, keepdims=True) + EPS)


def first_norm_kernel(a_ref, b_ref, g_ref, o_ref, h_ref, copy_ref):
    def run(ref):
        hidden = ref[...].astype(F32)
        h_ref[...] = ref[...]
        o_ref[...] = (hidden * row_inverse(hidden)).astype(BF)

    near = pl.program_id(0) < pl.num_programs(0) // 2
    pl.when(near)(lambda: run(a_ref))
    pl.when(jnp.logical_not(near))(lambda: run(b_ref))
    pl.when(near)(lambda: copy_ref.__setitem__(..., g_ref[...]))


def first_norm(order, a, b, g):
    rows, d = a.shape
    block = min(128, rows)
    steps = rows // block
    near = pl.BlockSpec((block, d), lambda i: (jnp.minimum(i, steps - 1), 0))
    each = pl.BlockSpec((block, d), lambda i: (i, 0))
    return order.call(
        first_norm_kernel, "first_norm", 10, (a, b, g),
        [near, pl.BlockSpec((block, d), lambda i: (jnp.maximum(i - steps, 0), 0)), near],
        [each, each, near], like((2 * rows, d, BF), (2 * rows, d, BF), (rows, d, BF)),
        grid=(2 * steps,), far=(0, 2),
    )


def join_kernel(a_ref, b_ref, o_ref):
    near = pl.program_id(0) < pl.num_programs(0) // 2
    pl.when(near)(lambda: o_ref.__setitem__(..., a_ref[...]))
    pl.when(jnp.logical_not(near))(lambda: o_ref.__setitem__(..., b_ref[...]))


def joined(order, kernel, name, a, b, count):
    rows, d = a.shape
    block = min(128, rows)
    steps = rows // block
    return order.call(
        kernel, name, 8, (a, b),
        [
            pl.BlockSpec((block, d), lambda i: (jnp.minimum(i, steps - 1), 0)),
            pl.BlockSpec((block, d), lambda i: (jnp.maximum(i - steps, 0), 0)),
        ],
        [pl.BlockSpec((block, d), lambda i: (i, 0))] * count, like(*[(2 * rows, d, BF)] * count),
        grid=(2 * steps,),
    )


def norm_kernel(h_ref, a_ref, b_ref, o_ref, resid_ref):
    resid = h_ref[...].astype(F32) + (a_ref[...].astype(F32) + b_ref[...].astype(F32))
    resid_ref[...] = resid.astype(BF)
    o_ref[...] = (resid * row_inverse(resid)).astype(BF)


def back_through_norm(scaled, values):
    inverse = row_inverse(values)
    inner = jnp.mean(scaled * values, axis=-1, keepdims=True)
    return inverse * scaled - values * (inverse * inverse * inverse * inner)


def norm_back_kernel(a_ref, g_ref, resid_ref, b_ref, o_ref):
    scaled = a_ref[...].astype(F32) + b_ref[...].astype(F32)
    back = back_through_norm(scaled, resid_ref[...].astype(F32))
    o_ref[...] = (g_ref[...].astype(F32) + back).astype(BF)


def output_kernel(resid_ref, a_ref, b_ref, c_ref, o_ref):
    total = a_ref[...].astype(F32) + b_ref[...].astype(F32) + c_ref[...].astype(F32)
    o_ref[...] = (resid_ref[...].astype(F32) + total).astype(BF)


def hidden_grad_kernel(grad_ref, h_ref, a_ref, b_ref, c_ref, o_ref):
    scaled = a_ref[...].astype(F32) + b_ref[...].astype(F32) + c_ref[...].astype(F32)
    grad = grad_ref[...].astype(F32) + back_through_norm(scaled, h_ref[...].astype(F32))
    o_ref[...] = grad.astype(BF)


def plus_kernel(a_ref, b_ref, o_ref):
    o_ref[...] = (a_ref[...].astype(F32) + b_ref[...].astype(F32)).astype(BF)


def by_rows(order, kernel, name, rows, arrays, outs, first=None, far=(), far_out=()):
    d = arrays[0].shape[1]
    block = min(128, rows)
    first = first or [0] * len(arrays)

    def spec(array, start):
        count = array.shape[0] // block
        skip = start // block
        return pl.BlockSpec((block, d), lambda i: (lax.rem(i + skip, count), 0))

    return order.call(
        kernel, name, 12, arrays, [spec(a, start) for a, start in zip(arrays, first)],
        [pl.BlockSpec((block, d), lambda i: (i, 0))] * len(outs),
        like(*[(rows, d, dtype) for dtype in outs]), grid=(rows // block,), far=far,
        far_out=far_out,
    )


def add_kernel(index_ref, left_chunk, right_chunk, left_ref, right_ref, to_right, to_left):
    columns, cut = to_right.shape[1], left_ref.shape[1]
    to_right[:, :cut] = (left_chunk[:, :cut].astype(F32) + left_ref[...].astype(F32)).astype(BF)
    if cut < columns:
        to_right[:, cut:] = left_chunk[:, cut:]
    cut = columns - right_ref.shape[1]
    to_left[:, cut:] = (right_chunk[:, cut:].astype(F32) + right_ref[...].astype(F32)).astype(BF)
    if cut > 0:
        to_left[:, :cut] = right_chunk[:, :cut]


def add_chunks(order, whole, rows, start, width, first, second, from_left, from_right):
    chunk = lambda k: pl.BlockSpec((rows, width), lambda i, index: (index[k], start // width))
    return order.call(
        add_kernel, "add_chunks", 10, (whole, whole, from_left, from_right),
        [chunk(0), chunk(1), *wholes((from_left, from_right))], [full((rows, width))] * 2,
        like((rows, width, BF), (rows, width, BF)),
        prefetch=(jnp.stack([first, second]).astype(jnp.int32),),
    )


def arrived_sum(chunk_ref, lefts, rights):
    left = jnp.concatenate([ref[...].astype(F32) for ref in lefts], axis=1)
    right = jnp.concatenate([ref[...].astype(F32) for ref in rights], axis=1)
    return chunk_ref[...].astype(F32) + left + right


def finish_kernel(parts, widths, index_ref, chunk_ref, *refs):
    grad = arrived_sum(chunk_ref, refs[:parts], refs[parts : 2 * parts])
    gain_ref, refs = refs[2 * parts], refs[2 * parts + 1 :]
    weights, outs = refs[: len(widths)], refs[len(widths) :]
    gain, total, at = column(gain_ref[...]), None, 0
    for k, width in enumerate(widths):
        part = grad[:, at : at + width]
        term = jnp.sum(part * weights[k][...].astype(F32), axis=1, keepdims=True)
        total = term if total is None else total + term
        outs[k][...] = part * gain
        at += width
    outs[-1][...] = jnp.broadcast_to(total, (total.shape[0], 128)).T[:1]


def finish(order, whole, rows, own, lefts, rights, gain, weights):
    columns = whole.shape[1]
    widths = tuple(w.shape[1] for w in weights)
    return order.call(
        functools.partial(finish_kernel, len(lefts), widths), "finish", 16,
        (whole, *lefts, *rights, gain, *weights),
        [
            pl.BlockSpec((rows, columns), lambda i, index: (index[0], 0)),
            *wholes((*lefts, *rights, gain, *weights)),
        ],
        [*wholes(weights), full((1, rows))],
        like(*[(*w.shape, F32) for w in weights], (1, rows, F32)),
        prefetch=(own[None].astype(jnp.int32),), far=range(1 + 2 * len(lefts), 2 + 2 * len(lefts) + len(weights)),
        far_out=range(len(weights)),
    )


def finish_plain_kernel(parts, index_ref, chunk_ref, *refs):
    refs[-1][...] = arrived_sum(chunk_ref, refs[:parts], refs[parts : 2 * parts])


def finish_plain(order, whole, rows, own, lefts, rights):
    columns = whole.shape[1]
    return order.call(
        functools.partial(finish_plain_kernel, len(lefts)), "finish_plain", 12,
        (whole, *lefts, *rights),
        [
            pl.BlockSpec((rows, columns), lambda i, index: (index[0], 0)),
            *wholes((*lefts, *rights)),
        ],
        [full((rows, columns))], like((rows, columns, F32)),
        prefetch=(own[None].astype(jnp.int32),), far_out=(0,),
    )[0]


class Ring:
    def __init__(self, count):
        self.count = count
        self.half = count // 2
        order = [2 * k if k < self.half else 2 * (count - 1 - k) + 1 for k in range(count)]
        self.right = [(order[k], order[(k + 1) % count]) for k in range(count)]
        self.left = [(b, a) for a, b in self.right]
        me = lax.axis_index("dp")
        self.place = jnp.where(me % 2 == 0, me // 2, count - 1 - me // 2)

    def index(self, offset):
        place = (self.place + offset + self.count) % self.count
        return jnp.where(place < self.half, 2 * place, 2 * (self.count - 1 - place) + 1)

    def go_right(self, value):
        return lax.ppermute(value, "dp", self.right)

    def go_left(self, value):
        return lax.ppermute(value, "dp", self.left)


def cut_of(columns):
    return max(128, (columns // 2 + 127) // 128 * 128)


class Kept:
    def __init__(self, order, ring, parts):
        self.order, self.ring = order, ring
        self.parts, self.rows = parts, sum(part.shape[0] for part in parts)
        self.pieces, self.whole = [], None

    def put(self, which, offset, first, piece):
        skip = self.parts[0].shape[0] * which
        self.pieces.append((self.ring.index(offset) * self.rows + skip, first, piece))

    def finish(self):
        count, columns = self.ring.count * self.rows, self.parts[0].shape[1]
        self.whole = assemble(self.order, count, columns, *zip(*self.pieces))


class Gather:
    def __init__(self, kept, which):
        self.kept, self.order, self.ring, self.rounds = kept, kept.order, kept.ring, 1
        self.which = which
        shard = relay(self.order, kept.parts[which])[0]
        kept.put(which, 0, 0, shard)
        self.cut = cut_of(shard.shape[1])
        self.flying = self.ring.go_right(shard), self.ring.go_left(shard)

    def wait(self):
        while self.rounds < self.ring.half - 3:
            self.wait_one()
        self.wait_one()

    def wait_one(self):
        arrived = self.order.wait(*self.flying)
        last = self.rounds == self.ring.half
        if not last:
            arrived = relay(self.order, *arrived)
        self.kept.put(self.which, -self.rounds, 0, arrived[0])
        self.kept.put(self.which, self.rounds, self.cut if last else 0, arrived[1])
        self.rounds += 1
        if self.rounds == self.ring.half:
            arrived = halves(self.order, *arrived, self.cut)
        if not last:
            self.flying = self.ring.go_right(arrived[0]), self.ring.go_left(arrived[1])


class Turns:
    def __init__(self, make):
        self.make, self.ring = make, None

    def start(self):
        self.ring = self.make()

    def wait(self):
        self.ring.wait()


class Scatter:
    def __init__(self, order, ring, whole, first, width):
        self.order, self.ring, self.whole = order, ring, whole
        self.first, self.width = first, width
        self.rows = whole.shape[0] // ring.count
        self.steps = ring.half - 1
        right, left = far_chunk(
            order, whole, self.rows, first, width, ring.index(ring.half), cut_of(width)
        )
        self.flying = ring.go_right(right), ring.go_left(left)

    def wait(self):
        while self.steps > 3:
            self.wait_one()
        self.wait_one()

    def wait_one(self):
        step = self.steps
        right, left = add_chunks(
            self.order, self.whole, self.rows, self.first, self.width, self.ring.index(step),
            self.ring.index(-step), *self.order.wait(*self.flying),
        )
        self.steps -= 1
        self.flying = self.ring.go_right(right), self.ring.go_left(left)

    def last(self):
        while self.steps:
            self.wait_one()
        return self.order.wait(*self.flying)


def scaled_sum(sums, gain, weights):
    arrived = [part.last() for part in sums]
    part = sums[0]
    return finish(
        part.order, part.whole, part.rows, part.ring.index(0), [a for a, _ in arrived],
        [b for _, b in arrived], gain, weights,
    )


def plain_sum(sums):
    arrived = [part.last() for part in sums]
    part = sums[0]
    return finish_plain(
        part.order, part.whole, part.rows, part.ring.index(0), [a for a, _ in arrived],
        [b for _, b in arrived],
    )


def swap_core(value):
    return lax.ppermute(value, "tensor", CORE_PAIRS)


def swap_x(value):
    return lax.ppermute(value, "tensor", X_PAIRS)


def plus(order, left_side, right_side, rows, first=0):
    arrays = (left_side, right_side)
    return by_rows(order, plus_kernel, "plus", rows, arrays, (BF,), (first, first))[0]


def per_device(
    dp_count,
    hidden_in,
    segments,
    attn_gain,
    w_query,
    w_key,
    w_value,
    w_out,
    mlp_gain,
    w_gate,
    w_up,
    w_down,
    cotangent,
):
    ring = Ring(dp_count)
    device = lax.axis_index("tensor").astype(jnp.int32)
    places = jnp.stack([device, device ^ 2, device ^ 1, device ^ 3])
    rows = hidden_in.shape[0]
    both = 2 * rows
    query_columns = w_query.shape[1]
    heads = query_columns // HD, w_key.shape[1] // HD
    units = w_gate.shape[1]
    block = units // 2
    order = Order()
    v = types.SimpleNamespace()

    def go(value):
        return relay(order, value)[0]

    A = Turns(lambda: Gather(v.A, 0))
    B = Turns(lambda: Gather(v.B, 0))
    C = Turns(lambda: Gather(v.C, 0))
    D = Turns(lambda: Scatter(order, ring, v.down_grad, 0, units))
    G = Turns(lambda: Scatter(order, ring, v.gate_up_grad, 0, units))
    U = Turns(lambda: Scatter(order, ring, v.gate_up_grad, units, units))
    Q = Turns(lambda: Scatter(order, ring, v.qkv_grad, 0, 2 * query_columns))
    O = Turns(lambda: Scatter(order, ring, v.out_grad, 0, query_columns))

    def A_keep():
        v.A.finish()

    def B_keep():
        v.B.finish()

    def C_keep():
        v.C.finish()

    def shard_a():
        weights = [w_query, w_key, w_value]
        shard = make_shard(order, attn_gain, weights, [w_out.T], "attn_shard", 14, False)
        v.A = Kept(order, ring, shard)

    def shard_b():
        shard = make_shard(order, mlp_gain, [w_gate, w_up], [], "gate_up_shard", 14, False)
        v.B = Kept(order, ring, shard)

    def shard_c():
        shard = make_shard(order, mlp_gain, [], [w_down.T], "down_shard", 8, False)
        v.C = Kept(order, ring, shard)

    def hidden_x():
        v.hidden_across = swap_x(hidden_in)

    def tables():
        v.cos, v.sin, v.start = rope_tables(order, segments)

    def norm_one():
        order.wait(v.hidden_across)
        v.normed, v.hidden, v.grads_own = first_norm(
            order, hidden_in, v.hidden_across, cotangent
        )

    def normed_core():
        v.normed = go(v.normed)
        v.normed_other = swap_core(v.normed)

    def grads_x():
        v.grads_own = go(v.grads_own)
        v.grads_across = swap_x(v.grads_own)

    def qkv():
        order.wait(v.normed_other)
        v.qkv = project(
            order, places, v.normed, v.normed_other, v.A.whole, v.cos, v.sin, *heads
        )

    def grads_join():
        order.wait(v.grads_across)
        v.grads = joined(order, join_kernel, "join", cotangent, v.grads_across, 1)[0]

    def grads_core():
        v.grads = go(v.grads)
        v.grads_other = swap_core(v.grads)

    def attention():
        v.heads_out, v.log_total = attend(order, v.qkv, v.start, *heads, rows)

    def out_part():
        v.part, v.part_other = branch(order, places, v.heads_out, v.A.whole)

    def part_core():
        v.part_other = go(v.part_other)
        v.part_core = swap_core(v.part_other)

    def part_x():
        order.wait(v.part_core)
        v.chip = plus(order, v.part, v.part_core, both)
        v.across = swap_x(v.chip)

    def norm_two():
        order.wait(v.across)
        v.normed_two, v.resid = by_rows(
            order, norm_kernel, "norm", both, (v.hidden, v.chip, v.across), (BF, BF),
            (0, 0, rows),
        )

    def normed_two_core():
        v.normed_two = go(v.normed_two)
        v.normed_two_other = swap_core(v.normed_two)

    def mlp_mine():
        v.act, v.da, v.db = gate_up(order, v.normed_two, v.B.whole, block)

    def mlp_other():
        order.wait(v.normed_two_other)
        v.act_other, v.da_other, v.db_other = gate_up(
            order, v.normed_two_other, v.B.whole, block
        )

    def grad_down():
        order.wait(v.grads_other)
        v.down_grad = weight_grad(
            order, v.grads, v.grads_other, v.act[None], v.act_other[None], block
        )

    def down_mine():
        v.down = down(order, v.act, v.C.whole, 512)

    def down_other():
        v.down_other = down(order, v.act_other, v.C.whole, 512)

    def down_core():
        v.down_other = go(v.down_other)
        v.down_core = swap_core(v.down_other)

    def down_x():
        order.wait(v.down_core)
        v.down_theirs = swap_x(plus(order, v.down, v.down_core, rows, rows))

    def finish_output():
        order.wait(v.down_theirs)
        arrays = (v.resid, v.down, v.down_core, v.down_theirs)
        v.output = by_rows(
            order, output_kernel, "output", rows, arrays, (BF,), far=range(4), far_out=(0,)
        )[0]

    def back_mine():
        v.scaled, v.d = mlp_back(
            order, v.grads, v.da, v.db, v.C.whole, v.B.whole, block
        )

    def back_other():
        v.scaled_other, v.d_other = mlp_back(
            order, v.grads_other, v.da_other, v.db_other, v.C.whole, v.B.whole, block
        )

    def scaled_core():
        v.scaled_other = go(v.scaled_other)
        v.scaled_core = swap_core(v.scaled_other)

    def scaled_x():
        order.wait(v.scaled_core)
        v.chip_back = plus(order, v.scaled, v.scaled_core, both)
        v.across_back = swap_x(v.chip_back)

    def grad_gate_up():
        v.gate_up_grad = weight_grad(
            order, v.normed_two, v.normed_two_other, v.d, v.d_other, block
        )

    def norm_two_back():
        order.wait(v.across_back)
        v.branch = by_rows(
            order, norm_back_kernel, "norm_back", both,
            (v.chip_back, v.grads, v.resid, v.across_back), (BF,), (0, 0, 0, rows),
        )[0]

    def branch_core():
        v.branch = go(v.branch)
        v.branch_other = swap_core(v.branch)

    def heads_back():
        order.wait(v.branch_other)
        v.grad_heads = grad_heads(
            order, places, v.branch, v.branch_other, v.A.whole, query_columns
        )

    def attention_back():
        v.dq, v.dk, v.dv = attend_back(
            order, v.qkv, v.grad_heads, v.heads_out, v.log_total, v.start, v.cos,
            v.sin, *heads, rows,
        )

    def grad_out():
        v.out_grad = turned_grad(
            order, places, [v.heads_out], v.branch, v.branch_other, "out_grad"
        )

    def grad_qkv():
        v.qkv_grad = turned_grad(
            order, places, [v.dq, v.dk, v.dv], v.normed, v.normed_other, "qkv_grad"
        )

    def grad_hidden():
        v.u, v.u_other = grad_x(order, places, v.dq, v.dk, v.dv, v.A.whole)

    def u_core():
        v.u_other = go(v.u_other)
        v.u_core = swap_core(v.u_other)

    def u_x():
        order.wait(v.u_core)
        v.u_theirs = swap_x(plus(order, v.u, v.u_core, rows, rows))

    def finish_hidden():
        order.wait(v.u_theirs)
        arrays = (v.branch, hidden_in, v.u, v.u_core, v.u_theirs)
        v.hidden_grad = by_rows(
            order, hidden_grad_kernel, "hidden_grad", rows, arrays, (BF,), far=range(5),
            far_out=(0,),
        )[0]

    def finish_down():
        v.down_w = plain_sum([D.ring])

    def finish_gate_up():
        sums = [G.ring, U.ring]
        v.gate_w, v.up_w, v.gain_two = scaled_sum(sums, mlp_gain, [w_gate, w_up])

    def finish_qkv():
        v.query_w, v.key_w, v.value_w, v.gain_one = scaled_sum(
            [Q.ring], attn_gain, [w_query, w_key, w_value]
        )

    def finish_out():
        v.out_w = plain_sum([O.ring])

    def wait_g():
        order.wait(*G.ring.flying)

    def wait_u():
        order.wait(*U.ring.flying)

    schedule = (
        shard_a, A.start, shard_b, B.start, A.wait, shard_c, C.start, hidden_x, tables,
        norm_one, normed_core, B.wait, A.wait, A.wait, C.wait, A.wait, grads_x, A_keep, qkv,
        attention, out_part, grads_join, B.wait, part_core, part_x, B.wait, B.wait, C.wait,
        B_keep, norm_two, normed_two_core, mlp_mine, C.wait, grads_core, mlp_other, grad_down,
        C.wait, C_keep, back_other, scaled_core, D.start, back_mine, D.wait, scaled_x,
        grad_gate_up, G.start, U.start, D.wait, G.wait, down_mine, U.wait, down_other,
        down_core, G.wait, norm_two_back, U.wait, branch_core, heads_back, attention_back,
        D.wait, grad_qkv, G.wait, grad_out, finish_down, Q.start, down_x, O.start, grad_hidden,
        U.wait, Q.wait, O.wait, u_core, u_x, Q.wait, O.wait, finish_gate_up, finish_output,
        Q.wait, wait_u, finish_qkv, O.wait, wait_g, finish_hidden, finish_out,
    )
    for run in schedule:
        run()
    gains = lax.psum(jnp.concatenate([v.gain_one, v.gain_two], axis=0), "tensor")
    return (
        v.output,
        v.hidden_grad,
        gains[0],
        v.query_w,
        v.key_w,
        v.value_w,
        v.out_w.T,
        gains[1],
        v.gate_w,
        v.up_w,
        v.down_w.T,
    )


def solution(mesh):
    tokens, split = P(("dp", "tensor"), None), P("dp", "tensor")
    in_specs = (
        tokens, P("dp"), P("dp"), split, split, split, P("tensor", "dp"),
        P("dp"), split, split, P("tensor", "dp"), tokens,
    )
    out_specs = (
        tokens, tokens, P("dp"), split, split, split, P("tensor", "dp"),
        P("dp"), split, split, P("tensor", "dp"),
    )
    body = functools.partial(per_device, mesh.shape["dp"])
    return jax.shard_map(body, mesh=mesh, in_specs=in_specs, out_specs=out_specs, check_vma=False)
```
